32 devices in a mesh: members: 2 (over y), gx: 16 (over z, x, core).
Axes of the slice: x: 2, y: 2, z: 4, core: 2. Of those that a mesh axis runs over, the one named last changes fastest.
Arguments:
- pressure: float32 [64, 32, 128], P(('members', 'gx')), parts along dimension 0, may hold values from -6 to 6
- saturation: float32 [64, 32, 128], P(('members', 'gx')), parts along dimension 0, may hold values from 0.1 to 0.9
- lam_water: float32 [64, 32, 128], P(('members', 'gx')), parts along dimension 0, may hold values from -6 to 6
- lam_oil: float32 [64, 32, 128], P(('members', 'gx')), parts along dimension 0, may hold values from -6 to 6
- perm_x: float32 [64, 32, 128], P(('members', 'gx')), parts along dimension 0, may hold values from 0.1 to 10
- perm_y: float32 [64, 32, 128], P(('members', 'gx')), parts along dimension 0, may hold values from 0.1 to 10
- perm_z: float32 [64, 32, 128], P(('members', 'gx')), parts along dimension 0, may hold values from 0.05 to 2
- pore_volume: float32 [64, 32, 128], P(('members', 'gx')), parts along dimension 0, may hold values from 0.3 to 3
- perf_cell: int32 [8192], P(('members', 'gx')), parts along dimension 0, may hold values from 0 to 8191
- perf_well: int32 [8192], P(('members', 'gx')), parts along dimension 0, may hold values from 0 to 255
- well_index: float32 [8192], P(('members', 'gx')), parts along dimension 0, may hold values from 0.5 to 5
- well_pressure: float32 [512], P(('members', 'gx')), parts along dimension 0, may hold values from -6 to 6
Outputs:
- grad_sat: float32 [64, 32, 128], P(('members', 'gx')), parts along dimension 0
- grad_bhp: float32 [512], P(('members', 'gx')), parts along dimension 0
- pressure_adj: float32 [64, 128, 32], P(('members', 'gx')), parts along dimension 0
The draws below stay inside these ranges and needn't reach their ends.
There are 2 independent parts, one for each index of `members`. The reference program is written for one: setup_inputs(seed, part) draws one part's arguments, and reference() takes and returns one part's arrays. A program takes and returns all parts, laid end to end along the dimension named above; each array names one. Nothing has to cross between parts.
Inputs may be any that keep to these rules, and one draw needn't show every extreme that they name: `perf_cell`: perforation r lies in the box of device r // 256; the number counts cells of that box with x slowest and z fastest.
All inputs are finite; a program needn't handle non-finite values.
Results may differ from the reference program's by a relative error of at most 0.0001.
Values sent between devices are 32-bit elements; how exact they have to be, the bound alone decides.
No kernel may reach another device: no remote copies, remote signals or barrier semaphores. Data moves between devices by JAX's collectives and lax.ppermute only.
A program may use at most 64 MiB of HBM per device.

```python
import math
import jax
import jax.numpy as jnp
import numpy as np
from jax import lax

CX = 2
NZ = 128
PERF_DEV = 256
SWEEPS = 4
NX = 32
NY = 32
PERFS = 4096
WELLS = 256


def touch_ends(result, own_key, smallest, top_value):
    index_at = [jax.random.randint(jax.random.fold_in(own_key, axis), (), 0, length) for axis, length in enumerate(result.shape)]
    main_axis = result.shape.index(max(result.shape))
    next_to = index_at[:main_axis] + [(index_at[main_axis] + 1) % result.shape[main_axis]] + index_at[main_axis + 1:]
    return result.at[tuple(index_at)].set(smallest).at[tuple(next_to)].set(top_value)


def shard_levels(rng, dims, cuts, low, high):
    level = 1.0
    for position, blocks in cuts:
        heights = jax.random.uniform(jax.random.fold_in(jax.random.fold_in(rng, 6), position), (blocks,), jnp.float32, low / len(cuts), high / len(cuts))
        level = level * jnp.repeat(jnp.exp(heights), dims[position] // blocks).reshape((-1,) + (1,) * (len(dims) - 1 - position))
    return level


def rank_table(amount, lean):
    loads = [(1 << 20) // math.isqrt(grade ** lean) + 1 for grade in range(1, amount + 1)]
    spread = 1 + sum(loads) // (1 << 30)
    return np.cumsum(np.array([max(1, weight // spread) for weight in loads]))


def ranked_ids(rng, dims, amount, slope):
    listing = rank_table(amount, slope)
    pick = jax.random.randint(jax.random.fold_in(rng, 1), dims, 0, int(listing[amount - 1]))
    grade = jnp.searchsorted(jnp.asarray(listing, jnp.int32), pick, side="right")
    return jax.random.permutation(jax.random.fold_in(rng, 2), amount)[grade].astype(jnp.int32)


def gaussian(key, shape, scale, most, shards=(), held_as=jnp.bfloat16):
    entries = jax.random.normal(key, shape, jnp.float32) * scale
    if len(shards) > 0:
        entries = shard_levels(key, shape, shards, -0.22, 0.18) * entries
    return jnp.clip(entries, min=-most, max=most).astype(held_as)


def setup_inputs(seed: int = 0, part: int = 0) -> dict:
    key_list = jax.random.split(jax.random.key(seed), 13)
    part_keys = jax.random.split(jax.random.fold_in(key_list[12], part), 13)
    return {
        "pressure": gaussian(part_keys[0], (NX, NY, NZ), 1.0, 6.0, ((0, 16),), jnp.float32),
        "saturation": jnp.clip(0.1 + 0.79999997 * jax.random.uniform(part_keys[1], (NX, NY, NZ), jnp.float32) ** shard_levels(part_keys[1], (NX, NY, NZ), ((0, 16),), -0.2, 0.2), 0.1, 0.9),
        "lam_water": gaussian(part_keys[2], (NX, NY, NZ), 1.0, 6.0, ((0, 16),), jnp.float32),
        "lam_oil": gaussian(part_keys[3], (NX, NY, NZ), 1.0, 6.0, ((0, 16),), jnp.float32),
        "perm_x": jnp.clip(jnp.exp(math.log(10.0) - 4.6051702 * jax.random.uniform(part_keys[4], (NX, NY, NZ), jnp.float32) ** shard_levels(part_keys[4], (NX, NY, NZ), ((0, 16),), -0.2, 0.2)), 0.1, 10.0),
        "perm_y": jnp.clip(jnp.exp(math.log(10.0) - 4.6051702 * jax.random.uniform(part_keys[5], (NX, NY, NZ), jnp.float32) ** shard_levels(part_keys[5], (NX, NY, NZ), ((0, 16),), -0.2, 0.2)), 0.1, 10.0),
        "perm_z": jnp.clip(jnp.exp(math.log(2.0) - 3.6888794 * jax.random.uniform(part_keys[6], (NX, NY, NZ), jnp.float32) ** shard_levels(part_keys[6], (NX, NY, NZ), ((0, 16),), -0.2, 0.2)), 0.05, 2.0),
        "pore_volume": jnp.clip(jnp.exp(math.log(3.0) - 2.3025851 * jax.random.uniform(part_keys[7], (NX, NY, NZ), jnp.float32) ** shard_levels(part_keys[7], (NX, NY, NZ), ((0, 16),), -0.2, 0.2)), 0.3, 3.0),
        "perf_cell": touch_ends(jax.random.randint(part_keys[8], (PERFS,), 0, CX * NY * NZ), jax.random.fold_in(part_keys[8], 1), 0, (CX * NY * NZ) - 1).astype(jnp.int32),
        "perf_well": touch_ends(ranked_ids(part_keys[9], (PERFS,), WELLS, 2), jax.random.fold_in(part_keys[9], 3), 0, WELLS - 1).astype(jnp.int32),
        "well_index": jnp.clip(jnp.exp(math.log(5.0) - 2.3025851 * jax.random.uniform(part_keys[10], (PERFS,), jnp.float32) ** shard_levels(part_keys[10], (PERFS,), ((0, 16),), -0.2, 0.2)), 0.5, 5.0),
        "well_pressure": gaussian(part_keys[11], (WELLS,), 1.0, 6.0, ((0, 16),), jnp.float32),
    }


water_viscosity = 0.5
oil_viscosity = 2.0
compressibility = 0.2

def mobilities(saturation):
    water_mob = saturation * saturation / water_viscosity
    oil_mob = (1.0 - saturation) * (1.0 - saturation) / oil_viscosity
    water_slope = 2.0 * saturation / water_viscosity
    oil_slope = -2.0 * (1.0 - saturation) / oil_viscosity
    return (water_mob, oil_mob, water_slope, oil_slope)

def face_terms(center, across):
    press_here, sat_here, lamw_here, lamo_here, permeab_here = center
    press_there, sat_there, lamw_there, lamo_there, permeab_there = across
    trans = 2.0 * permeab_here * permeab_there / (permeab_here + permeab_there)
    mob_here = mobilities(sat_here)
    mob_there = mobilities(sat_there)
    water_face = 0.5 * (mob_here[0] + mob_there[0])
    oil_face = 0.5 * (mob_here[1] + mob_there[1])
    lamw_diff = lamw_here - lamw_there
    lamo_diff = lamo_here - lamo_there
    grad_press = trans * (water_face * lamw_diff + oil_face * lamo_diff)
    grad_satur = trans * 0.5 * (press_here - press_there) * (mob_here[2] * lamw_diff + mob_here[3] * lamo_diff)
    coupling = trans * (water_face + oil_face)
    return (grad_press, grad_satur, coupling)

def from_upper(field, dimension):
    widths = [(0, 1) if other == dimension else (0, 0) for other in range(field.ndim)]
    padded = jnp.pad(field, widths)
    return lax.slice_in_dim(padded, 1, field.shape[dimension] + 1, axis=dimension)

def from_lower(field, dimension):
    widths = [(1, 0) if other == dimension else (0, 0) for other in range(field.ndim)]
    padded = jnp.pad(field, widths)
    return lax.slice_in_dim(padded, 0, field.shape[dimension], axis=dimension)

def reference(pressure, saturation, lam_water, lam_oil, perm_x, perm_y, perm_z, pore_volume, perf_cell, perf_well, well_index, well_pressure):
    center_fields = (pressure, saturation, lam_water, lam_oil)
    perms = (perm_x, perm_y, perm_z)
    grad_press = jnp.zeros_like(pressure)
    grad_satur = pore_volume * (lam_water - lam_oil)
    diagonal = compressibility * pore_volume
    couplings = []
    for dimension in range(3):
        center = center_fields + (perms[dimension],)
        uppers = tuple((from_upper(field, dimension) for field in center))
        lowers = tuple((from_lower(field, dimension) for field in center))
        upper_terms = face_terms(center, uppers)
        lower_terms = face_terms(center, lowers)
        grad_press = grad_press + upper_terms[0] + lower_terms[0]
        grad_satur = grad_satur + upper_terms[1] + lower_terms[1]
        diagonal = diagonal + upper_terms[2] + lower_terms[2]
        couplings.append(upper_terms[2])
    owner_block = jnp.arange(PERFS, dtype=jnp.int32) // PERF_DEV
    cells = (owner_block * (CX * NY * NZ) + perf_cell).astype(jnp.int32)
    press_perf = pressure.ravel()[cells]
    sat_perf = saturation.ravel()[cells]
    lamw_perf = lam_water.ravel()[cells]
    lamo_perf = lam_oil.ravel()[cells]
    bhp_perf = well_pressure[perf_well]
    water_mob, oil_mob, water_slope, oil_slope = mobilities(sat_perf)
    inflow = well_index * (water_mob * lamw_perf + oil_mob * lamo_perf)
    sat_well = well_index * (water_slope * lamw_perf + oil_slope * lamo_perf) * (press_perf - bhp_perf)
    shape = pressure.shape
    grad_press = grad_press.ravel().at[cells].add(inflow).reshape(shape)
    grad_satur = grad_satur.ravel().at[cells].add(sat_well).reshape(shape)
    diagonal = diagonal.ravel().at[cells].add(well_index * (water_mob + oil_mob)).reshape(shape)
    grad_bhp = -jax.ops.segment_sum(inflow, perf_well, num_segments=WELLS)

    def to_columns(field):
        return jnp.transpose(field, (1, 2, 0))
    rhs = to_columns(grad_press)
    diag_col = to_columns(diagonal)
    cx_up = to_columns(couplings[0])
    cy_up = to_columns(couplings[1])
    cz_up = to_columns(couplings[2])
    cx_low = from_lower(cx_up, 2)
    cy_low = from_lower(cy_up, 0)
    cz_low = from_lower(cz_up, 1)
    solution = jnp.zeros_like(rhs)
    for sweep_index in range(SWEEPS):
        offline = cy_up * from_upper(solution, 0) + cy_low * from_lower(solution, 0)
        offline = offline + cz_up * from_upper(solution, 1) + cz_low * from_lower(solution, 1)
        target = rhs + offline
        solution = lax.linalg.tridiagonal_solve(-cx_low, diag_col, -cx_up, target[..., None])[..., 0]
    return (grad_satur, grad_bhp, solution)
```

```python
import functools

import jax
import jax.numpy as jnp
from jax import lax
from jax.experimental import pallas as pl
from jax.experimental.pallas import tpu as pltpu
from jax.sharding import PartitionSpec as P

water_viscosity = 0.5
oil_viscosity = 2.0
compressibility = 0.2

LANES = 128
TILE = 8
FIELDS = 8
RHS, DIAG, CY, CZ, SAT, LAMW, LAMO, PERMX = range(FIELDS)
EXTRA = FIELDS * TILE
WELL_ROW = EXTRA + 2
CHUNK = EXTRA + TILE
OUTSIDE = (0.0, 1.0, 0.0, 0.0, 0.0, 0.0, 0.0, 1.0)


def mobilities(s):
    return s * s * (1.0 / water_viscosity), (1.0 - s) * (1.0 - s) * (1.0 / oil_viscosity)


def slopes(s):
    return s * (2.0 / water_viscosity), (s - 1.0) * (2.0 / oil_viscosity)


def split(x):
    first = x.astype(jnp.bfloat16)
    rest = x - first.astype(jnp.float32)
    second = rest.astype(jnp.bfloat16)
    third = (rest - second.astype(jnp.float32)).astype(jnp.bfloat16)
    return first, second, third


def dot(a, b, over):
    return lax.dot_general(a, b, (over, ((), ())), preferred_element_type=jnp.float32)


def add_thirds(x):
    n = x.shape[0] // 3
    return x[:n] + x[n : 2 * n] + x[2 * n :]


def marks(index, count):
    return (lax.broadcasted_iota(jnp.int32, (count, index.shape[1]), 0) == index).astype(jnp.float32)


def scatter_cells(values, row_marks, lane_marks):
    left = jnp.concatenate([(row_marks * part.astype(jnp.float32)).astype(jnp.bfloat16) for part in split(values)])
    return add_thirds(dot(left, lane_marks.astype(jnp.bfloat16), ((1,), (1,))))


def upper(x, axis):
    return pltpu.roll(x, x.shape[axis] - 1, axis)


def lower(x, axis):
    return pltpu.roll(x, 1, axis)


def transmissibility(k, axis):
    kn = upper(k, axis)
    at = lax.broadcasted_iota(jnp.int32, k.shape, axis)
    return jnp.where(at < k.shape[axis] - 1, 2.0 * k * kn / (k + kn), 0.0)


def pack_kernel(
    groups, wells, press, sat, lamw, lamo, permx, permy, permz, pore, cell, well, index, bhp,
    packed, weight, above, below, padded, well_rows,
):
    ny = sat.shape[1]
    cells = cell[...]
    row_marks = marks(cells // LANES, 2 * ny)
    lane_marks = marks(cells % LANES, LANES)
    perf_weight = scatter_cells(index[...], row_marks, lane_marks)
    weight[...] = perf_weight
    flows = []
    for x in range(2):
        s, lw, lo = sat[x], lamw[x], lamo[x]
        mw, mo = mobilities(s)
        flow = mw * lw + mo * lo
        flows.append(flow)
        w = perf_weight[x * ny : (x + 1) * ny]
        rhs = flow * w
        diag = compressibility * pore[x] + (mw + mo) * w
        couplings = []
        for k, axis in ((permy[x], 0), (permz[x], 1)):
            trans = 0.5 * transmissibility(k, axis)
            fw = mw + upper(mw, axis)
            fo = mo + upper(mo, axis)
            g = trans * (fw * (lw - upper(lw, axis)) + fo * (lo - upper(lo, axis)))
            c = trans * (fw + fo)
            rhs = rhs + g - lower(g, axis)
            diag = diag + c + lower(c, axis)
            couplings.append(c)
        for field, value in enumerate((rhs, diag, couplings[0], couplings[1], s, lw, lo, permx[x])):
            edge = jnp.full((TILE, LANES), OUTSIDE[field], jnp.float32)
            padded[field, x, :TILE] = edge
            padded[field, x, TILE : TILE + ny] = value
            padded[field, x, TILE + ny :] = edge
    for member, field in enumerate((press, sat, lamw, lamo, permx)):
        above[member] = field[1]
        below[member] = field[0]

    flow_parts = jnp.concatenate([part for part in split(jnp.concatenate(flows))])
    row_parts = jnp.concatenate([row_marks.astype(jnp.bfloat16)] * 3)
    by_lane = dot(flow_parts, row_parts, ((0,), (0,)))
    inflow = index[...] * jnp.sum(by_lane * lane_marks, axis=0, keepdims=True)
    wells_each = bhp.shape[1]
    owners = marks(well[...] // wells_each, groups)
    places = marks(well[...] % wells_each + wells_each, LANES)
    partial = scatter_cells(inflow, owners, places)
    well_rows[...] = partial
    well_rows[:, :wells_each] = jnp.broadcast_to(bhp[...], (groups, wells_each))

    def chunk(d, _):
        start = TILE + 2 * d - 1
        for field in range(FIELDS):
            for x in range(2):
                packed[d, field * TILE + 4 * x : field * TILE + 4 * x + 4] = padded[field, x, pl.ds(start, 4)]
        for x in range(2):
            packed[d, EXTRA + x : EXTRA + x + 1] = padded[CY, x, pl.ds(start - 1, 1)]
        packed[d, WELL_ROW : WELL_ROW + 1] = well_rows[pl.ds(d, 1)]
        return 0

    if groups <= 16:
        for d in range(groups):
            chunk(d, 0)
    else:
        lax.fori_loop(0, groups, chunk, 0)


def sat_kernel(press, sat, lamw, lamo, permx, permy, permz, pore, weight, from_below, from_above, out):
    ny = sat.shape[1]

    def parts(here, there, trans):
        p, _, lw, lo = here
        pn, _, lwn, lon = there
        t = trans * (p - pn)
        return t * (lw - lwn), t * (lo - lon)

    layers = [tuple(r[x] for r in (press, sat, lamw, lamo)) for x in range(2)]
    ends = (tuple(from_below[m] for m in range(4)), tuple(from_above[m] for m in range(4)))
    perms = (from_below[4], permx[0], permx[1], from_above[4])
    chain = (ends[0], layers[0], layers[1], ends[1])
    x_faces = []
    for i in range(3):
        k, kn = perms[i], perms[i + 1]
        x_faces.append(parts(chain[i], chain[i + 1], k * kn / (k + kn)))
    for x in range(2):
        p, s, lw, lo = layers[x]
        water = x_faces[x][0] + x_faces[x + 1][0]
        oil = x_faces[x][1] + x_faces[x + 1][1]
        for k, axis in ((permy[x], 0), (permz[x], 1)):
            there = tuple(upper(f, axis) for f in layers[x])
            a, b = parts(layers[x], there, 0.5 * transmissibility(k, axis))
            water = water + a + lower(a, axis)
            oil = oil + b + lower(b, axis)
        dw, do = slopes(s)
        well = weight[x * ny : (x + 1) * ny] * p
        out[x] = pore[x] * (lw - lo) + dw * (water + well * lw) + do * (oil + well * lo)


def well_kernel(partial, sat, lamw, lamo, cell, well, index, well_rows, out, grad_bhp):
    ny = sat.shape[1]
    groups = well_rows.shape[0]
    wells_each = grad_bhp.shape[1]
    rows = well_rows[...]
    place = well[...] % wells_each
    owners = marks(well[...] // wells_each, groups)
    by_owner = add_thirds(
        dot(jnp.concatenate(split(rows)), marks(place, LANES).astype(jnp.bfloat16), ((1,), (0,)))
    )
    pressure = jnp.sum(by_owner * owners, axis=0, keepdims=True)
    cells = cell[...]
    drop = scatter_cells(index[...] * pressure, marks(cells // LANES, 2 * ny), marks(cells % LANES, LANES))
    for x in range(2):
        dw, do = slopes(sat[x])
        out[x] = partial[x] - (dw * lamw[x] + do * lamo[x]) * drop[x * ny : (x + 1) * ny]
    total = -jnp.sum(rows, axis=0, keepdims=True)
    grad_bhp[...] = total[:, wells_each : 2 * wells_each]


def swap(x):
    return pltpu.roll(x, 4, 0)


def sublane():
    return lax.broadcasted_iota(jnp.int32, (TILE, LANES), 0)


def sweep(targets, weights, inverses, middle):
    steps = len(targets)
    b = [targets[0]]
    for j in range(1, steps):
        b.append(targets[j] + weights[j - 1] * b[j - 1])
    diag_swapped, coupling, inverse = middle
    u = (b[-1] * diag_swapped + coupling * swap(b[-1])) * inverse
    found = [u]
    for j in range(steps - 2, -1, -1):
        u = inverses[j] * b[j] + weights[j] * u
        found.append(u)
    return found[::-1]


def first_kernel(received, rhs_out, cy_out, cyl_out, cz_out, weight_out, inverse_out, middle_out, u_out, send, well_rows):
    groups = received.shape[0]
    steps = groups
    low = sublane() < 4

    def field(s, f):
        return received[s, f * TILE : (f + 1) * TILE]

    def face(lw, lo, mw, mo, k):
        kn = swap(k)
        trans = k * kn / (k + kn)
        fw = mw + swap(mw)
        fo = mo + swap(mo)
        g = trans * (fw * (lw - swap(lw)) + fo * (lo - swap(lo)))
        return g, trans * (fw + fo)

    cells = []
    for s in range(groups):
        mw, mo = mobilities(field(s, SAT))
        cells.append((field(s, LAMW), field(s, LAMO), mw, mo, field(s, PERMX)))
    inner = [face(*cells[s]) for s in range(groups)]
    between = [
        face(*(jnp.where(low, after, here) for here, after in zip(cells[s], cells[s + 1])))
        for s in range(groups - 1)
    ]
    none = jnp.zeros((TILE, LANES), jnp.float32)

    def at_edges(s, part):
        before = between[s - 1][part] if s > 0 else none
        after = between[s][part] if s < groups - 1 else none
        return jnp.where(low, before, after)

    rhs = [field(s, RHS) + inner[s][0] + at_edges(s, 0) for s in range(groups)]
    diag = [field(s, DIAG) + inner[s][1] + at_edges(s, 1) for s in range(groups)]
    cy = [field(s, CY) for s in range(groups)]
    cz = [field(s, CZ) for s in range(groups)]
    row = sublane() % 4
    cyl = []
    for s in range(groups):
        first = received[s, EXTRA : EXTRA + 1]
        second = received[s, EXTRA + 1 : EXTRA + 2]
        edge = jnp.where(low, first, second)
        cyl.append(jnp.where(row == 0, edge, lower(cy[s], 0)))

    def paired(tiles):
        out = []
        for s in range(groups // 2):
            here, mirror = tiles[s], tiles[groups - 1 - s]
            out.append(jnp.where(low, here, mirror))
            out.append(swap(jnp.where(low, mirror, here)))
        return out

    rhs, diag, cy, cyl, cz = (paired(tiles) for tiles in (rhs, diag, cy, cyl, cz))
    link = []
    for s in range(groups // 2):
        link.append(jnp.where(low, inner[s][1], inner[groups - 1 - s][1]))
        link.append(jnp.where(low, between[s][1], between[groups - 2 - s][1]))
    weights, inverses = [], []
    d = diag[0]
    for j in range(steps - 1):
        inverse = 1.0 / d
        inverses.append(inverse)
        weights.append(link[j] * inverse)
        d = diag[j + 1] - link[j] * weights[j]
    d_swapped = swap(d)
    middle = (d_swapped, link[-1], 1.0 / (d * d_swapped - link[-1] * link[-1]))

    u = sweep(rhs, weights, inverses, middle)
    targets = []
    for j in range(steps):
        t = rhs[j] + cy[j] * upper(u[j], 0) + cyl[j] * lower(u[j], 0)
        targets.append(t + cz[j] * upper(u[j], 1) + lower(cz[j], 1) * lower(u[j], 1))
    u = sweep(targets, weights, inverses, middle)

    own = (row == 1) | (row == 2)
    for j in range(0, steps, 2):
        send[j * 4 : j * 4 + TILE] = jnp.where(own, u[j], pltpu.roll(u[j + 1], 2, 0))
    for j in range(steps):
        at = slice(j * TILE, (j + 1) * TILE)
        rhs_out[at] = rhs[j]
        cy_out[at] = cy[j]
        cyl_out[at] = cyl[j]
        cz_out[at] = cz[j]
        u_out[at] = u[j]
        if j < steps - 1:
            weight_out[at] = weights[j]
            inverse_out[at] = inverses[j]
    for i in range(3):
        middle_out[i * TILE : (i + 1) * TILE] = middle[i]
    for s in range(groups):
        well_rows[s : s + 1] = received[s, WELL_ROW : WELL_ROW + 1]


def second_kernel(rhs_in, cy_in, cyl_in, cz_in, weight_in, inverse_in, middle_in, u_in, from_below, from_above, out):
    steps = rhs_in.shape[0] // TILE
    row = sublane() % 4

    def tiles(ref, count):
        return [ref[j * TILE : (j + 1) * TILE] for j in range(count)]

    rhs, cy, cyl, cz, own = (tiles(ref, steps) for ref in (rhs_in, cy_in, cyl_in, cz_in, u_in))
    weights = tiles(weight_in, steps - 1)
    inverses = tiles(inverse_in, steps - 1)
    middle = tiles(middle_in, 3)
    below = tiles(from_below, steps // 2)
    above = tiles(from_above, steps // 2)

    def turned(x, by):
        return pltpu.roll(x, by % TILE, 0) if by % TILE else x

    targets = []
    for j in range(steps):
        b, a = below[j // 2], above[j // 2]
        shift = 2 * (j % 2)
        u = jnp.where(row == 0, turned(b, -2 - shift), jnp.where(row == 3, turned(a, 2 - shift), own[j]))
        up = jnp.where(row == 3, turned(a, 1 - shift), upper(u, 0))
        down = jnp.where(row == 0, turned(b, -1 - shift), lower(u, 0))
        t = rhs[j] + cy[j] * up + cyl[j] * down
        targets.append(t + cz[j] * upper(u, 1) + lower(cz[j], 1) * lower(u, 1))
    u = sweep(targets, weights, inverses, middle)
    targets = []
    for j in range(steps):
        t = rhs[j] + cy[j] * upper(u[j], 0) + cyl[j] * lower(u[j], 0)
        targets.append(t + cz[j] * upper(u[j], 1) + lower(cz[j], 1) * lower(u[j], 1))
    u = sweep(targets, weights, inverses, middle)
    for j in range(steps):
        mirror = 2 * steps - 1 - j
        for y in range(2):
            out[y, j : j + 1] = u[j][1 + y : 2 + y]
            out[y, mirror : mirror + 1] = u[j][5 + y : 6 + y]


def call(kernel, outs, *args, scratch=()):
    return pl.pallas_call(
        kernel,
        out_shape=tuple(jax.ShapeDtypeStruct(shape, jnp.float32) for shape in outs),
        in_specs=[pl.BlockSpec(memory_space=pltpu.VMEM)] * len(args),
        out_specs=tuple(pl.BlockSpec(memory_space=pltpu.VMEM) for _ in outs),
        scratch_shapes=[pltpu.VMEM(shape, jnp.float32) for shape in scratch],
        compiler_params=pltpu.CompilerParams(vmem_limit_bytes=40 << 20),
    )(*args)


def on_device(
    pressure, saturation, lam_water, lam_oil, perm_x, perm_y, perm_z, pore_volume,
    perf_cell, perf_well, well_index, well_pressure,
):
    groups = lax.axis_size("gx")
    ny = pressure.shape[1]
    wells_each = well_pressure.shape[0]
    wells = groups * wells_each
    cell, well, index, bhp = (v.reshape(1, -1) for v in (perf_cell, perf_well, well_index, well_pressure))
    fields = (pressure, saturation, lam_water, lam_oil, perm_x, perm_y, perm_z, pore_volume)
    up = [(i, i + 1) for i in range(groups - 1)]
    down = [(i + 1, i) for i in range(groups - 1)]

    packed, weight, top, bottom = call(
        functools.partial(pack_kernel, groups, wells),
        [(groups, CHUNK, LANES), (2 * ny, LANES), (5, ny, LANES), (5, ny, LANES)],
        *fields, cell, well, index, bhp,
        scratch=[(FIELDS, 2, ny + 2 * TILE, LANES), (groups, LANES)],
    )
    received = lax.all_to_all(packed, "gx", split_axis=0, concat_axis=0, tiled=True)
    from_below = lax.ppermute(top, "gx", up)
    from_above = lax.ppermute(bottom, "gx", down)
    (partial,) = call(sat_kernel, [(2, ny, LANES)], *fields, weight, from_below, from_above)

    steps = groups
    column = (steps * TILE, LANES)
    *state, send, well_rows = call(
        first_kernel,
        [column] * 6 + [(3 * TILE, LANES), column, (steps * 4, LANES), (groups, LANES)],
        received,
    )
    u_below = lax.ppermute(send, "gx", up)
    u_above = lax.ppermute(send, "gx", down)
    grad_sat, grad_bhp = call(
        well_kernel, [(2, ny, LANES), (1, wells_each)],
        partial, saturation, lam_water, lam_oil, cell, well, index, well_rows,
    )
    (columns,) = call(second_kernel, [(2, 2 * steps, LANES)], *state, u_below, u_above)
    return grad_sat, grad_bhp.reshape(wells_each), jnp.transpose(columns, (0, 2, 1))


def solution(mesh):
    cells = P(("members", "gx"), None, None)
    line = P(("members", "gx"))
    return jax.shard_map(
        on_device,
        mesh=mesh,
        in_specs=(cells,) * 8 + (line,) * 4,
        out_specs=(cells, line, cells),
        check_vma=False,
    )
```

```python
import functools

import jax
import jax.numpy as jnp
from jax import lax
from jax.experimental import pallas as pl
from jax.experimental.pallas import tpu as pltpu
from jax.sharding import PartitionSpec as P

water_viscosity = 0.5
oil_viscosity = 2.0
compressibility = 0.2

LANES = 128
TILE = 8
RHS, DIAG, CY, CZ = (TILE * i for i in range(4))
LINKS = 4 * TILE
FACE = 5 * TILE
CY_BELOW = FACE + 4
WELL_ROW = FACE + 6
CHUNK = 6 * TILE


def mobilities(s):
    return s * s * (1.0 / water_viscosity), (1.0 - s) * (1.0 - s) * (1.0 / oil_viscosity)


def slopes(s):
    return s * (2.0 / water_viscosity), (s - 1.0) * (2.0 / oil_viscosity)


def split(x):
    first = x.astype(jnp.bfloat16)
    rest = x - first.astype(jnp.float32)
    second = rest.astype(jnp.bfloat16)
    third = (rest - second.astype(jnp.float32)).astype(jnp.bfloat16)
    return first, second, third


def dot(a, b, over):
    return lax.dot_general(a, b, (over, ((), ())), preferred_element_type=jnp.float32)


def add_thirds(x):
    n = x.shape[0] // 3
    return x[:n] + x[n : 2 * n] + x[2 * n :]


def marks(index, count):
    return (lax.broadcasted_iota(jnp.int32, (count, index.shape[1]), 0) == index).astype(jnp.float32)


def scatter_cells(values, row_marks, lane_marks):
    left = jnp.concatenate([(row_marks * part.astype(jnp.float32)).astype(jnp.bfloat16) for part in split(values)])
    return add_thirds(dot(left, lane_marks.astype(jnp.bfloat16), ((1,), (1,))))


def upper(x, axis):
    return pltpu.roll(x, x.shape[axis] - 1, axis)


def lower(x, axis):
    return pltpu.roll(x, 1, axis)


def transmissibility(k, axis):
    kn = upper(k, axis)
    at = lax.broadcasted_iota(jnp.int32, k.shape, axis)
    return jnp.where(at < k.shape[axis] - 1, 2.0 * k * kn / (k + kn), 0.0)


def load_kernel(*refs):
    count = (len(refs) - 2) // 2
    fields, loaded, edge, sems = refs[:count], refs[count : 2 * count], refs[-2], refs[-1]
    pairs = [(fields[f].at[1], edge.at[m]) for m, f in enumerate(range(5))] + list(zip(fields, loaded))
    copies = [pltpu.make_async_copy(src, dst, sems.at[i]) for i, (src, dst) in enumerate(pairs)]
    for copy in copies:
        copy.start()
    for copy in copies:
        copy.wait()


def face(here, there, trans):
    lw, lo, mw, mo = here
    lwn, lon, mwn, mon = there
    fw = mw + mwn
    fo = mo + mon
    return trans * (fw * (lw - lwn) + fo * (lo - lon)), trans * (fw + fo)


def cell_kernel(
    groups, sat, lamw, lamo, permx, permy, permz, pore, cell, well, index, bhp,
    rhs_out, diag_out, cy_out, cz_out, inner_out, weight, well_rows,
):
    ny = sat.shape[1]
    cells = cell[...]
    row_marks = marks(cells // LANES, 2 * ny)
    lane_marks = marks(cells % LANES, LANES)
    perf_weight = scatter_cells(index[...], row_marks, lane_marks)
    weight[...] = perf_weight
    flows, layers, rhs, diag = [], [], [], []
    for x in range(2):
        s, lw, lo = sat[x], lamw[x], lamo[x]
        mw, mo = mobilities(s)
        layers.append((lw, lo, mw, mo))
        flow = mw * lw + mo * lo
        flows.append(flow)
        w = perf_weight[x * ny : (x + 1) * ny]
        rhs.append(flow * w)
        diag.append(compressibility * pore[x] + (mw + mo) * w)
        for k, axis, out in ((permy[x], 0, cy_out), (permz[x], 1, cz_out)):
            there = tuple(upper(f, axis) for f in layers[x])
            g, c = face(layers[x], there, 0.5 * transmissibility(k, axis))
            rhs[x] += g - lower(g, axis)
            diag[x] += c + lower(c, axis)
            out[x] = c
    k, kn = permx[0], permx[1]
    g, c = face(layers[0], layers[1], k * kn / (k + kn))
    inner_out[...] = c
    for x in range(2):
        rhs_out[x] = rhs[x] + (1 - 2 * x) * g
        diag_out[x] = diag[x] + c

    flow_parts = jnp.concatenate(split(jnp.concatenate(flows)))
    row_parts = jnp.concatenate([row_marks.astype(jnp.bfloat16)] * 3)
    by_lane = dot(flow_parts, row_parts, ((0,), (0,)))
    inflow = index[...] * jnp.sum(by_lane * lane_marks, axis=0, keepdims=True)
    wells_each = bhp.shape[1]
    owners = marks(well[...] // wells_each, groups)
    places = marks(well[...] % wells_each + wells_each, LANES)
    well_rows[...] = scatter_cells(inflow, owners, places)
    well_rows[:, :wells_each] = jnp.broadcast_to(bhp[...], (groups, wells_each))


def pack_kernel(
    groups, press, sat, lamw, lamo, permx, from_below, rhs, diag, cy, cz, inner, well_rows,
    packed, sat_face, padded, padded_links,
):
    ny = sat.shape[1]
    k, kn = permx[0], from_below[4]
    trans = k * kn / (k + kn)
    lw, lo, lwn, lon = lamw[0], lamo[0], from_below[2], from_below[3]
    g, c = face((lw, lo, *mobilities(sat[0])), (lwn, lon, *mobilities(from_below[1])), trans)
    t = trans * (press[0] - from_below[0])
    sat_face[0] = t * (lw - lwn)
    sat_face[1] = t * (lo - lon)

    def pad(ref, at, value, outside):
        edge = jnp.full((TILE, LANES), outside, jnp.float32)
        ref[(*at, slice(0, TILE))] = edge
        ref[(*at, slice(TILE, TILE + ny))] = value
        ref[(*at, slice(TILE + ny, 2 * TILE + ny))] = edge

    for x in range(2):
        pad(padded, (0, x), rhs[x] + g if x == 0 else rhs[x], 0.0)
        pad(padded, (1, x), diag[x] + c if x == 0 else diag[x], 1.0)
        pad(padded, (2, x), cy[x], 0.0)
        pad(padded, (3, x), cz[x], 0.0)
    for i, value in enumerate((inner[...], c, g)):
        pad(padded_links, (i,), value, 0.0)

    def chunk(d, _):
        start = TILE + 2 * d - 1
        for f, at in enumerate((RHS, DIAG, CY, CZ)):
            for x in range(2):
                packed[d, at + 4 * x : at + 4 * x + 4] = padded[f, x, pl.ds(start, 4)]
        for i, at in enumerate((LINKS, LINKS + 4, FACE)):
            packed[d, at : at + 4] = padded_links[i, pl.ds(start, 4)]
        for x in range(2):
            packed[d, CY_BELOW + x : CY_BELOW + x + 1] = padded[2, x, pl.ds(start - 1, 1)]
        packed[d, WELL_ROW : WELL_ROW + 1] = well_rows[pl.ds(d, 1)]
        packed[d, WELL_ROW + 1 : WELL_ROW + 2] = jnp.zeros((1, LANES), jnp.float32)
        return 0

    if groups <= 16:
        for d in range(groups):
            chunk(d, 0)
    else:
        lax.fori_loop(0, groups, chunk, 0)


def sat_kernel(press, sat, lamw, lamo, permx, permy, permz, pore, weight, sat_face, from_below, out, back):
    ny = sat.shape[1]

    def parts(here, there, trans):
        p, lw, lo = here
        pn, lwn, lon = there
        t = trans * (p - pn)
        return t * (lw - lwn), t * (lo - lon)

    layers = [tuple(r[x] for r in (press, lamw, lamo)) for x in range(2)]
    k, kn = permx[0], permx[1]
    inner = parts(layers[0], layers[1], k * kn / (k + kn))
    outer = (sat_face[0], sat_face[1])
    dw, do = slopes(from_below[1])
    back[...] = dw * outer[0] + do * outer[1]
    for x in range(2):
        p, lw, lo = layers[x]
        water, oil = (i + o for i, o in zip(inner, outer)) if x == 0 else inner
        for k, axis in ((permy[x], 0), (permz[x], 1)):
            there = tuple(upper(f, axis) for f in layers[x])
            a, b = parts(layers[x], there, 0.5 * transmissibility(k, axis))
            water = water + a + lower(a, axis)
            oil = oil + b + lower(b, axis)
        dw, do = slopes(sat[x])
        well = weight[x * ny : (x + 1) * ny] * p
        out[x] = pore[x] * (lw - lo) + dw * (water + well * lw) + do * (oil + well * lo)


def well_kernel(partial, from_above, sat, lamw, lamo, cell, well, index, well_rows, out, grad_bhp):
    ny = sat.shape[1]
    groups = well_rows.shape[0]
    wells_each = grad_bhp.shape[1]
    rows = well_rows[...]
    place = well[...] % wells_each
    owners = marks(well[...] // wells_each, groups)
    by_owner = add_thirds(
        dot(jnp.concatenate(split(rows)), marks(place, LANES).astype(jnp.bfloat16), ((1,), (0,)))
    )
    pressure = jnp.sum(by_owner * owners, axis=0, keepdims=True)
    cells = cell[...]
    drop = scatter_cells(index[...] * pressure, marks(cells // LANES, 2 * ny), marks(cells % LANES, LANES))
    for x in range(2):
        dw, do = slopes(sat[x])
        before = partial[x] if x == 0 else partial[x] + from_above[...]
        out[x] = before - (dw * lamw[x] + do * lamo[x]) * drop[x * ny : (x + 1) * ny]
    total = -jnp.sum(rows, axis=0, keepdims=True)
    grad_bhp[...] = total[:, wells_each : 2 * wells_each]


def swap(x):
    return pltpu.roll(x, 4, 0)


def sublane():
    return lax.broadcasted_iota(jnp.int32, (TILE, LANES), 0)


def sweep(targets, weights, inverses, middle):
    steps = len(targets)
    b = [targets[0]]
    for j in range(1, steps):
        b.append(targets[j] + weights[j - 1] * b[j - 1])
    diag_swapped, coupling, inverse = middle
    u = (b[-1] * diag_swapped + coupling * swap(b[-1])) * inverse
    found = [u]
    for j in range(steps - 2, -1, -1):
        u = inverses[j] * b[j] + weights[j] * u
        found.append(u)
    return found[::-1]


def first_kernel(received, rhs_out, cy_out, cyl_out, cz_out, weight_out, inverse_out, middle_out, u_out, send, well_rows):
    groups = received.shape[0]
    steps = groups
    low = sublane() < 4

    def tile(s, at):
        return received[s, at : at + TILE]

    none = jnp.zeros((TILE, LANES), jnp.float32)
    row = sublane() % 4
    links = [tile(s, LINKS) for s in range(groups)]
    swapped = [swap(t) for t in links]
    rhs, diag, cyl = [], [], []
    for s in range(groups):
        g = swap(tile(s + 1, FACE)) if s < groups - 1 else none
        c = links[s + 1] if s < groups - 1 else none
        rhs.append(tile(s, RHS) - jnp.where(low, 0.0, g))
        diag.append(tile(s, DIAG) + jnp.where(low, 0.0, c))
    cy = [tile(s, CY) for s in range(groups)]
    cz = [tile(s, CZ) for s in range(groups)]
    for s in range(groups):
        first = received[s, CY_BELOW : CY_BELOW + 1]
        second = received[s, CY_BELOW + 1 : CY_BELOW + 2]
        cyl.append(jnp.where(row == 0, jnp.where(low, first, second), lower(cy[s], 0)))

    def paired(tiles):
        out = []
        for s in range(groups // 2):
            here, mirror = tiles[s], tiles[groups - 1 - s]
            out.append(jnp.where(low, here, mirror))
            out.append(swap(jnp.where(low, mirror, here)))
        return out

    rhs, diag, cy, cyl, cz = (paired(tiles) for tiles in (rhs, diag, cy, cyl, cz))
    link = []
    for s in range(groups // 2):
        link.append(jnp.where(low, links[s], swapped[groups - 1 - s]))
        link.append(jnp.where(low, swapped[s + 1], links[groups - 1 - s]))
    weights, inverses = [], []
    d = diag[0]
    for j in range(steps - 1):
        inverse = 1.0 / d
        inverses.append(inverse)
        weights.append(link[j] * inverse)
        d = diag[j + 1] - link[j] * weights[j]
    d_swapped = swap(d)
    middle = (d_swapped, link[-1], 1.0 / (d * d_swapped - link[-1] * link[-1]))

    u = sweep(rhs, weights, inverses, middle)
    targets = []
    for j in range(steps):
        t = rhs[j] + cy[j] * upper(u[j], 0) + cyl[j] * lower(u[j], 0)
        targets.append(t + cz[j] * upper(u[j], 1) + lower(cz[j], 1) * lower(u[j], 1))
    u = sweep(targets, weights, inverses, middle)

    own = (row == 1) | (row == 2)
    for j in range(0, steps, 2):
        send[j * 4 : j * 4 + TILE] = jnp.where(own, u[j], pltpu.roll(u[j + 1], 2, 0))
    for j in range(steps):
        at = slice(j * TILE, (j + 1) * TILE)
        rhs_out[at] = rhs[j]
        cy_out[at] = cy[j]
        cyl_out[at] = cyl[j]
        cz_out[at] = cz[j]
        u_out[at] = u[j]
        if j < steps - 1:
            weight_out[at] = weights[j]
            inverse_out[at] = inverses[j]
    for i in range(3):
        middle_out[i * TILE : (i + 1) * TILE] = middle[i]
    for s in range(groups):
        well_rows[s : s + 1] = received[s, WELL_ROW : WELL_ROW + 1]


def second_kernel(rhs_in, cy_in, cyl_in, cz_in, weight_in, inverse_in, middle_in, u_in, from_below, from_above, out):
    steps = rhs_in.shape[0] // TILE
    row = sublane() % 4

    def tiles(ref, count):
        return [ref[j * TILE : (j + 1) * TILE] for j in range(count)]

    rhs, cy, cyl, cz, own = (tiles(ref, steps) for ref in (rhs_in, cy_in, cyl_in, cz_in, u_in))
    weights = tiles(weight_in, steps - 1)
    inverses = tiles(inverse_in, steps - 1)
    middle = tiles(middle_in, 3)
    below = tiles(from_below, steps // 2)
    above = tiles(from_above, steps // 2)

    def turned(x, by):
        return pltpu.roll(x, by % TILE, 0) if by % TILE else x

    targets = []
    for j in range(steps):
        b, a = below[j // 2], above[j // 2]
        shift = 2 * (j % 2)
        u = jnp.where(row == 0, turned(b, -2 - shift), jnp.where(row == 3, turned(a, 2 - shift), own[j]))
        up = jnp.where(row == 3, turned(a, 1 - shift), upper(u, 0))
        down = jnp.where(row == 0, turned(b, -1 - shift), lower(u, 0))
        t = rhs[j] + cy[j] * up + cyl[j] * down
        targets.append(t + cz[j] * upper(u, 1) + lower(cz[j], 1) * lower(u, 1))
    u = sweep(targets, weights, inverses, middle)
    targets = []
    for j in range(steps):
        t = rhs[j] + cy[j] * upper(u[j], 0) + cyl[j] * lower(u[j], 0)
        targets.append(t + cz[j] * upper(u[j], 1) + lower(cz[j], 1) * lower(u[j], 1))
    u = sweep(targets, weights, inverses, middle)
    for j in range(steps):
        mirror = 2 * steps - 1 - j
        for y in range(2):
            out[y, j : j + 1] = u[j][1 + y : 2 + y]
            out[y, mirror : mirror + 1] = u[j][5 + y : 6 + y]


def call(kernel, outs, *args, scratch=(), source=pltpu.VMEM):
    return pl.pallas_call(
        kernel,
        out_shape=tuple(o if isinstance(o, jax.ShapeDtypeStruct) else jax.ShapeDtypeStruct(o, jnp.float32) for o in outs),
        in_specs=[pl.BlockSpec(memory_space=source)] * len(args),
        out_specs=tuple(pl.BlockSpec(memory_space=pltpu.VMEM) for _ in outs),
        scratch_shapes=[pltpu.VMEM(o, jnp.float32) if isinstance(o, tuple) else o for o in scratch],
        compiler_params=pltpu.CompilerParams(vmem_limit_bytes=40 << 20),
    )(*args)


def on_device(
    pressure, saturation, lam_water, lam_oil, perm_x, perm_y, perm_z, pore_volume,
    perf_cell, perf_well, well_index, well_pressure,
):
    groups = lax.axis_size("gx")
    ny = pressure.shape[1]
    wells_each = well_pressure.shape[0]
    fields = (pressure, saturation, lam_water, lam_oil, perm_x, perm_y, perm_z, pore_volume)
    given = fields + tuple(v.reshape(1, -1) for v in (perf_cell, perf_well, well_index, well_pressure))
    up = [(i, i + 1) for i in range(groups - 1)]
    down = [(i + 1, i) for i in range(groups - 1)]

    *loaded, edge = call(
        load_kernel,
        [jax.ShapeDtypeStruct(v.shape, v.dtype) for v in given] + [(5, ny, LANES)],
        *given,
        scratch=[pltpu.SemaphoreType.DMA((len(given) + 5,))],
        source=pltpu.HBM,
    )
    press, sat, lamw, lamo, permx, permy, permz, pore, cell, well, index, bhp = loaded
    from_below = lax.ppermute(edge, "gx", up)
    box = (2, ny, LANES)
    rhs, diag, cy, cz, inner, weight, well_rows = call(
        functools.partial(cell_kernel, groups),
        [box] * 4 + [(ny, LANES), (2 * ny, LANES), (groups, LANES)],
        sat, lamw, lamo, permx, permy, permz, pore, cell, well, index, bhp,
    )
    packed, sat_face = call(
        functools.partial(pack_kernel, groups),
        [(groups, CHUNK, LANES), box],
        press, sat, lamw, lamo, permx, from_below, rhs, diag, cy, cz, inner, well_rows,
        scratch=[(4, 2, ny + 2 * TILE, LANES), (3, ny + 2 * TILE, LANES)],
    )
    received = lax.all_to_all(packed, "gx", split_axis=0, concat_axis=0, tiled=True)
    partial, back = call(
        sat_kernel, [box, (ny, LANES)],
        press, sat, lamw, lamo, permx, permy, permz, pore, weight, sat_face, from_below,
    )
    from_above = lax.ppermute(back, "gx", down)

    steps = groups
    column = (steps * TILE, LANES)
    *state, send, well_rows = call(
        first_kernel,
        [column] * 6 + [(3 * TILE, LANES), column, (steps * 4, LANES), (groups, LANES)],
        received,
    )
    u_below = lax.ppermute(send, "gx", up)
    u_above = lax.ppermute(send, "gx", down)
    grad_sat, grad_bhp = call(
        well_kernel, [box, (1, wells_each)],
        partial, from_above, sat, lamw, lamo, cell, well, index, well_rows,
    )
    (columns,) = call(second_kernel, [(2, 2 * steps, LANES)], *state, u_below, u_above)
    return grad_sat, grad_bhp.reshape(wells_each), jnp.transpose(columns, (0, 2, 1))


def solution(mesh):
    cells = P(("members", "gx"), None, None)
    line = P(("members", "gx"))
    return jax.shard_map(
        on_device,
        mesh=mesh,
        in_specs=(cells,) * 8 + (line,) * 4,
        out_specs=(cells, line, cells),
        check_vma=False,
    )
```

```python
import functools

import jax
import jax.numpy as jnp
from jax import lax
from jax.experimental import pallas as pl
from jax.experimental.pallas import tpu as pltpu
from jax.sharding import PartitionSpec as P

water_viscosity = 0.5
oil_viscosity = 2.0
compressibility = 0.2

LANES = 128
TILE = 8
RHS, DIAG, CY, CZ = (TILE * i for i in range(4))
LINKS = 4 * TILE
FACE = 5 * TILE
CY_BELOW = FACE + 4
WELL_ROW = FACE + 6
CHUNK = 6 * TILE


def mobilities(s):
    return s * s * (1.0 / water_viscosity), (1.0 - s) * (1.0 - s) * (1.0 / oil_viscosity)


def slopes(s):
    return s * (2.0 / water_viscosity), (s - 1.0) * (2.0 / oil_viscosity)


def split(x):
    first = x.astype(jnp.bfloat16)
    rest = x - first.astype(jnp.float32)
    second = rest.astype(jnp.bfloat16)
    third = (rest - second.astype(jnp.float32)).astype(jnp.bfloat16)
    return first, second, third


def dot(a, b, over):
    return lax.dot_general(a, b, (over, ((), ())), preferred_element_type=jnp.float32)


def add_thirds(x):
    n = x.shape[0] // 3
    return x[:n] + x[n : 2 * n] + x[2 * n :]


def marks(index, count):
    return (lax.broadcasted_iota(jnp.int32, (count, index.shape[1]), 0) == index).astype(jnp.float32)


def scatter_cells(values, row_marks, lane_marks):
    left = jnp.concatenate([(row_marks * part.astype(jnp.float32)).astype(jnp.bfloat16) for part in split(values)])
    return add_thirds(dot(left, lane_marks.astype(jnp.bfloat16), ((1,), (1,))))


def upper(x, axis):
    return pltpu.roll(x, x.shape[axis] - 1, axis)


def lower(x, axis):
    return pltpu.roll(x, 1, axis)


def transmissibility(k, axis):
    kn = upper(k, axis)
    at = lax.broadcasted_iota(jnp.int32, k.shape, axis)
    return jnp.where(at < k.shape[axis] - 1, 2.0 * k * kn / (k + kn), 0.0)


def load_kernel(*refs):
    count = (len(refs) - 2) // 2
    fields, loaded, edge, sems = refs[:count], refs[count : 2 * count], refs[-2], refs[-1]
    pairs = [(fields[f].at[1], edge.at[m]) for m, f in enumerate(range(5))] + list(zip(fields, loaded))
    copies = [pltpu.make_async_copy(src, dst, sems.at[i]) for i, (src, dst) in enumerate(pairs)]
    for copy in copies:
        copy.start()
    for copy in copies:
        copy.wait()


def face(here, there, trans):
    lw, lo, mw, mo = here
    lwn, lon, mwn, mon = there
    fw = mw + mwn
    fo = mo + mon
    return trans * (fw * (lw - lwn) + fo * (lo - lon)), trans * (fw + fo)


def cell_kernel(
    groups, sat, lamw, lamo, permx, permy, permz, pore, cell, well, index, bhp,
    rhs_out, diag_out, cy_out, cz_out, inner_out, weight, well_rows,
):
    ny = sat.shape[1]
    cells = cell[...]
    row_marks = marks(cells // LANES, 2 * ny)
    lane_marks = marks(cells % LANES, LANES)
    perf_weight = scatter_cells(index[...], row_marks, lane_marks)
    weight[...] = perf_weight
    flows, layers, rhs, diag = [], [], [], []
    for x in range(2):
        s, lw, lo = sat[x], lamw[x], lamo[x]
        mw, mo = mobilities(s)
        layers.append((lw, lo, mw, mo))
        flow = mw * lw + mo * lo
        flows.append(flow)
        w = perf_weight[x * ny : (x + 1) * ny]
        rhs.append(flow * w)
        diag.append(compressibility * pore[x] + (mw + mo) * w)
        for k, axis, out in ((permy[x], 0, cy_out), (permz[x], 1, cz_out)):
            there = tuple(upper(f, axis) for f in layers[x])
            g, c = face(layers[x], there, 0.5 * transmissibility(k, axis))
            rhs[x] += g - lower(g, axis)
            diag[x] += c + lower(c, axis)
            out[x] = c
    k, kn = permx[0], permx[1]
    g, c = face(layers[0], layers[1], k * kn / (k + kn))
    inner_out[...] = c
    for x in range(2):
        rhs_out[x] = rhs[x] + (1 - 2 * x) * g
        diag_out[x] = diag[x] + c

    flow_parts = jnp.concatenate(split(jnp.concatenate(flows)))
    row_parts = jnp.concatenate([row_marks.astype(jnp.bfloat16)] * 3)
    by_lane = dot(flow_parts, row_parts, ((0,), (0,)))
    inflow = index[...] * jnp.sum(by_lane * lane_marks, axis=0, keepdims=True)
    wells_each = bhp.shape[1]
    owners = marks(well[...] // wells_each, groups)
    places = marks(well[...] % wells_each + wells_each, LANES)
    well_rows[...] = scatter_cells(inflow, owners, places)
    well_rows[:, :wells_each] = jnp.broadcast_to(bhp[...], (groups, wells_each))


def pack_kernel(
    groups, press, sat, lamw, lamo, permx, from_below, rhs, diag, cy, cz, inner, well_rows,
    packed, sat_face, padded, padded_links,
):
    ny = sat.shape[1]
    k, kn = permx[0], from_below[4]
    trans = k * kn / (k + kn)
    lw, lo, lwn, lon = lamw[0], lamo[0], from_below[2], from_below[3]
    g, c = face((lw, lo, *mobilities(sat[0])), (lwn, lon, *mobilities(from_below[1])), trans)
    t = trans * (press[0] - from_below[0])
    sat_face[0] = t * (lw - lwn)
    sat_face[1] = t * (lo - lon)

    def pad(ref, at, value, outside):
        edge = jnp.full((TILE, LANES), outside, jnp.float32)
        ref[(*at, slice(0, TILE))] = edge
        ref[(*at, slice(TILE, TILE + ny))] = value
        ref[(*at, slice(TILE + ny, 2 * TILE + ny))] = edge

    for x in range(2):
        pad(padded, (0, x), rhs[x] + g if x == 0 else rhs[x], 0.0)
        pad(padded, (1, x), diag[x] + c if x == 0 else diag[x], 1.0)
        pad(padded, (2, x), cy[x], 0.0)
        pad(padded, (3, x), cz[x], 0.0)
    for i, value in enumerate((inner[...], c, g)):
        pad(padded_links, (i,), value, 0.0)

    def chunk(d, _):
        start = TILE + 2 * d - 1
        for f, at in enumerate((RHS, DIAG, CY, CZ)):
            for x in range(2):
                packed[d, at + 4 * x : at + 4 * x + 4] = padded[f, x, pl.ds(start, 4)]
        for i, at in enumerate((LINKS, LINKS + 4, FACE)):
            packed[d, at : at + 4] = padded_links[i, pl.ds(start, 4)]
        for x in range(2):
            packed[d, CY_BELOW + x : CY_BELOW + x + 1] = padded[2, x, pl.ds(start - 1, 1)]
        packed[d, WELL_ROW : WELL_ROW + 1] = well_rows[pl.ds(d, 1)]
        packed[d, WELL_ROW + 1 : WELL_ROW + 2] = jnp.zeros((1, LANES), jnp.float32)
        return 0

    if groups <= 16:
        for d in range(groups):
            chunk(d, 0)
    else:
        lax.fori_loop(0, groups, chunk, 0)


def sat_kernel(press, sat, lamw, lamo, permx, permy, permz, pore, weight, sat_face, from_below, out, back):
    ny = sat.shape[1]

    def parts(here, there, trans):
        p, lw, lo = here
        pn, lwn, lon = there
        t = trans * (p - pn)
        return t * (lw - lwn), t * (lo - lon)

    layers = [tuple(r[x] for r in (press, lamw, lamo)) for x in range(2)]
    k, kn = permx[0], permx[1]
    inner = parts(layers[0], layers[1], k * kn / (k + kn))
    outer = (sat_face[0], sat_face[1])
    dw, do = slopes(from_below[1])
    back[...] = dw * outer[0] + do * outer[1]
    for x in range(2):
        p, lw, lo = layers[x]
        water, oil = (i + o for i, o in zip(inner, outer)) if x == 0 else inner
        for k, axis in ((permy[x], 0), (permz[x], 1)):
            there = tuple(upper(f, axis) for f in layers[x])
            a, b = parts(layers[x], there, 0.5 * transmissibility(k, axis))
            water = water + a + lower(a, axis)
            oil = oil + b + lower(b, axis)
        dw, do = slopes(sat[x])
        well = weight[x * ny : (x + 1) * ny] * p
        out[x] = pore[x] * (lw - lo) + dw * (water + well * lw) + do * (oil + well * lo)


def well_kernel(partial, from_above, sat, lamw, lamo, cell, well, index, well_rows, out, grad_bhp):
    ny = sat.shape[1]
    groups = well_rows.shape[0]
    wells_each = grad_bhp.shape[1]
    rows = well_rows[...]
    place = well[...] % wells_each
    owners = marks(well[...] // wells_each, groups)
    by_owner = add_thirds(
        dot(jnp.concatenate(split(rows)), marks(place, LANES).astype(jnp.bfloat16), ((1,), (0,)))
    )
    pressure = jnp.sum(by_owner * owners, axis=0, keepdims=True)
    cells = cell[...]
    drop = scatter_cells(index[...] * pressure, marks(cells // LANES, 2 * ny), marks(cells % LANES, LANES))
    for x in range(2):
        dw, do = slopes(sat[x])
        before = partial[x] if x == 0 else partial[x] + from_above[...]
        out[x] = before - (dw * lamw[x] + do * lamo[x]) * drop[x * ny : (x + 1) * ny]
    total = -jnp.sum(rows, axis=0, keepdims=True)
    grad_bhp[...] = total[:, wells_each : 2 * wells_each]


def swap(x):
    return pltpu.roll(x, 4, 0)


def sublane():
    return lax.broadcasted_iota(jnp.int32, (TILE, LANES), 0)


def sweep(targets, weights, inverses, middle):
    steps = len(targets)
    b = [targets[0]]
    for j in range(1, steps):
        b.append(targets[j] + weights[j - 1] * b[j - 1])
    diag_swapped, coupling, inverse = middle
    u = (b[-1] * diag_swapped + coupling * swap(b[-1])) * inverse
    found = [u]
    for j in range(steps - 2, -1, -1):
        u = inverses[j] * b[j] + weights[j] * u
        found.append(u)
    return found[::-1]


def first_kernel(received, _, rhs_out, cy_out, cyl_out, cz_out, weight_out, inverse_out, middle_out, u_out, send, well_rows):
    groups = received.shape[0]
    steps = groups
    low = sublane() < 4

    def tile(s, at):
        return received[s, at : at + TILE]

    none = jnp.zeros((TILE, LANES), jnp.float32)
    row = sublane() % 4
    links = [tile(s, LINKS) for s in range(groups)]
    swapped = [swap(t) for t in links]
    rhs, diag, cyl = [], [], []
    for s in range(groups):
        g = swap(tile(s + 1, FACE)) if s < groups - 1 else none
        c = links[s + 1] if s < groups - 1 else none
        rhs.append(tile(s, RHS) - jnp.where(low, 0.0, g))
        diag.append(tile(s, DIAG) + jnp.where(low, 0.0, c))
    cy = [tile(s, CY) for s in range(groups)]
    cz = [tile(s, CZ) for s in range(groups)]
    for s in range(groups):
        first = received[s, CY_BELOW : CY_BELOW + 1]
        second = received[s, CY_BELOW + 1 : CY_BELOW + 2]
        cyl.append(jnp.where(row == 0, jnp.where(low, first, second), lower(cy[s], 0)))

    def paired(tiles):
        out = []
        for s in range(groups // 2):
            here, mirror = tiles[s], tiles[groups - 1 - s]
            out.append(jnp.where(low, here, mirror))
            out.append(swap(jnp.where(low, mirror, here)))
        return out

    rhs, diag, cy, cyl, cz = (paired(tiles) for tiles in (rhs, diag, cy, cyl, cz))
    link = []
    for s in range(groups // 2):
        link.append(jnp.where(low, links[s], swapped[groups - 1 - s]))
        link.append(jnp.where(low, swapped[s + 1], links[groups - 1 - s]))
    weights, inverses = [], []
    d = diag[0]
    for j in range(steps - 1):
        inverse = 1.0 / d
        inverses.append(inverse)
        weights.append(link[j] * inverse)
        d = diag[j + 1] - link[j] * weights[j]
    d_swapped = swap(d)
    middle = (d_swapped, link[-1], 1.0 / (d * d_swapped - link[-1] * link[-1]))

    u = sweep(rhs, weights, inverses, middle)
    targets = []
    for j in range(steps):
        t = rhs[j] + cy[j] * upper(u[j], 0) + cyl[j] * lower(u[j], 0)
        targets.append(t + cz[j] * upper(u[j], 1) + lower(cz[j], 1) * lower(u[j], 1))
    u = sweep(targets, weights, inverses, middle)

    own = (row == 1) | (row == 2)
    for j in range(0, steps, 2):
        send[j * 4 : j * 4 + TILE] = jnp.where(own, u[j], pltpu.roll(u[j + 1], 2, 0))
    for j in range(steps):
        at = slice(j * TILE, (j + 1) * TILE)
        rhs_out[at] = rhs[j]
        cy_out[at] = cy[j]
        cyl_out[at] = cyl[j]
        cz_out[at] = cz[j]
        u_out[at] = u[j]
        if j < steps - 1:
            weight_out[at] = weights[j]
            inverse_out[at] = inverses[j]
    for i in range(3):
        middle_out[i * TILE : (i + 1) * TILE] = middle[i]
    for s in range(groups):
        well_rows[s : s + 1] = received[s, WELL_ROW : WELL_ROW + 1]


def second_kernel(rhs_in, cy_in, cyl_in, cz_in, weight_in, inverse_in, middle_in, u_in, from_below, from_above, out):
    steps = rhs_in.shape[0] // TILE
    row = sublane() % 4

    def tiles(ref, count):
        return [ref[j * TILE : (j + 1) * TILE] for j in range(count)]

    rhs, cy, cyl, cz, own = (tiles(ref, steps) for ref in (rhs_in, cy_in, cyl_in, cz_in, u_in))
    weights = tiles(weight_in, steps - 1)
    inverses = tiles(inverse_in, steps - 1)
    middle = tiles(middle_in, 3)
    below = tiles(from_below, steps // 2)
    above = tiles(from_above, steps // 2)

    def turned(x, by):
        return pltpu.roll(x, by % TILE, 0) if by % TILE else x

    targets = []
    for j in range(steps):
        b, a = below[j // 2], above[j // 2]
        shift = 2 * (j % 2)
        u = jnp.where(row == 0, turned(b, -2 - shift), jnp.where(row == 3, turned(a, 2 - shift), own[j]))
        up = jnp.where(row == 3, turned(a, 1 - shift), upper(u, 0))
        down = jnp.where(row == 0, turned(b, -1 - shift), lower(u, 0))
        t = rhs[j] + cy[j] * up + cyl[j] * down
        targets.append(t + cz[j] * upper(u, 1) + lower(cz[j], 1) * lower(u, 1))
    u = sweep(targets, weights, inverses, middle)
    targets = []
    for j in range(steps):
        t = rhs[j] + cy[j] * upper(u[j], 0) + cyl[j] * lower(u[j], 0)
        targets.append(t + cz[j] * upper(u[j], 1) + lower(cz[j], 1) * lower(u[j], 1))
    u = sweep(targets, weights, inverses, middle)
    for j in range(steps):
        mirror = 2 * steps - 1 - j
        for y in range(2):
            out[y, j : j + 1] = u[j][1 + y : 2 + y]
            out[y, mirror : mirror + 1] = u[j][5 + y : 6 + y]


def call(kernel, outs, *args, scratch=(), source=pltpu.VMEM, limit=40 << 20):
    return pl.pallas_call(
        kernel,
        out_shape=tuple(o if isinstance(o, jax.ShapeDtypeStruct) else jax.ShapeDtypeStruct(o, jnp.float32) for o in outs),
        in_specs=[pl.BlockSpec(memory_space=source)] * len(args),
        out_specs=tuple(pl.BlockSpec(memory_space=pltpu.VMEM) for _ in outs),
        scratch_shapes=[pltpu.VMEM(o, jnp.float32) if isinstance(o, tuple) else o for o in scratch],
        compiler_params=pltpu.CompilerParams(vmem_limit_bytes=limit),
    )(*args)


def on_device(
    pressure, saturation, lam_water, lam_oil, perm_x, perm_y, perm_z, pore_volume,
    perf_cell, perf_well, well_index, well_pressure,
):
    groups = lax.axis_size("gx")
    ny = pressure.shape[1]
    wells_each = well_pressure.shape[0]
    fields = (pressure, saturation, lam_water, lam_oil, perm_x, perm_y, perm_z, pore_volume)
    given = fields + tuple(v.reshape(1, -1) for v in (perf_cell, perf_well, well_index, well_pressure))
    up = [(i, i + 1) for i in range(groups - 1)]
    down = [(i + 1, i) for i in range(groups - 1)]

    *loaded, edge = call(
        load_kernel,
        [jax.ShapeDtypeStruct(v.shape, v.dtype) for v in given] + [(5, ny, LANES)],
        *(pltpu.with_memory_space_constraint(v, pltpu.HBM) for v in given),
        scratch=[pltpu.SemaphoreType.DMA((len(given) + 5,))],
        source=pltpu.HBM,
        limit=40 << 20,
    )
    press, sat, lamw, lamo, permx, permy, permz, pore, cell, well, index, bhp = loaded
    from_below = lax.ppermute(edge, "gx", up)
    box = (2, ny, LANES)
    rhs, diag, cy, cz, inner, weight, well_rows = call(
        functools.partial(cell_kernel, groups),
        [box] * 4 + [(ny, LANES), (2 * ny, LANES), (groups, LANES)],
        sat, lamw, lamo, permx, permy, permz, pore, cell, well, index, bhp,
    )
    packed, sat_face = call(
        functools.partial(pack_kernel, groups),
        [(groups, CHUNK, LANES), box],
        press, sat, lamw, lamo, permx, from_below, rhs, diag, cy, cz, inner, well_rows,
        scratch=[(4, 2, ny + 2 * TILE, LANES), (3, ny + 2 * TILE, LANES)],
    )
    received = lax.all_to_all(packed, "gx", split_axis=0, concat_axis=0, tiled=True)
    partial, back = call(
        sat_kernel, [box, (ny, LANES)],
        press, sat, lamw, lamo, permx, permy, permz, pore, weight, sat_face, from_below,
    )
    from_above = lax.ppermute(back, "gx", down)

    steps = groups
    column = (steps * TILE, LANES)
    *state, send, well_rows = call(
        first_kernel,
        [column] * 6 + [(3 * TILE, LANES), column, (steps * 4, LANES), (groups, LANES)],
        received,
        from_above,
    )
    u_below = lax.ppermute(send, "gx", up)
    u_above = lax.ppermute(send, "gx", down)
    grad_sat, grad_bhp = call(
        well_kernel, [box, (1, wells_each)],
        partial, from_above, sat, lamw, lamo, cell, well, index, well_rows,
    )
    (columns,) = call(second_kernel, [(2, 2 * steps, LANES)], *state, u_below, u_above)
    return grad_sat, grad_bhp.reshape(wells_each), jnp.transpose(columns, (0, 2, 1))


def solution(mesh):
    cells = P(("members", "gx"), None, None)
    line = P(("members", "gx"))
    return jax.shard_map(
        on_device,
        mesh=mesh,
        in_specs=(cells,) * 8 + (line,) * 4,
        out_specs=(cells, line, cells),
        check_vma=False,
    )
```

```python
import functools

import jax
import jax.numpy as jnp
from jax import lax
from jax.experimental import pallas as pl
from jax.experimental.pallas import tpu as pltpu
from jax.sharding import PartitionSpec as P

water_viscosity = 0.5
oil_viscosity = 2.0
compressibility = 0.2
SWEEPS = 4

LANES = 128
TILE = 8
HALO = 3
ROWS = 5
RHS, DIAG, SAT, LAMW, LAMO, PERMX, CY, CZ = range(8)
OUTSIDE = (0.0, 1.0, 0.0, 0.0, 0.0, 1.0, 0.0, 0.0)
FIELDS = 8
WELL_ROW = CZ * 2 * ROWS
CHUNK = FIELDS * 2 * ROWS


def mobilities(s):
    return s * s * (1.0 / water_viscosity), (1.0 - s) * (1.0 - s) * (1.0 / oil_viscosity)


def slopes(s):
    return s * (2.0 / water_viscosity), (s - 1.0) * (2.0 / oil_viscosity)


def split(x):
    first = x.astype(jnp.bfloat16)
    rest = x - first.astype(jnp.float32)
    second = rest.astype(jnp.bfloat16)
    third = (rest - second.astype(jnp.float32)).astype(jnp.bfloat16)
    return first, second, third


def dot(a, b, over):
    return lax.dot_general(a, b, (over, ((), ())), preferred_element_type=jnp.float32)


def add_thirds(x):
    n = x.shape[0] // 3
    return x[:n] + x[n : 2 * n] + x[2 * n :]


def marks(index, count):
    return (lax.broadcasted_iota(jnp.int32, (count, index.shape[1]), 0) == index).astype(jnp.float32)


def scatter_cells(values, row_marks, lane_marks):
    left = jnp.concatenate([(row_marks * part.astype(jnp.float32)).astype(jnp.bfloat16) for part in split(values)])
    return add_thirds(dot(left, lane_marks.astype(jnp.bfloat16), ((1,), (1,))))


def upper(x, axis):
    return pltpu.roll(x, x.shape[axis] - 1, axis)


def lower(x, axis):
    return pltpu.roll(x, 1, axis)


def transmissibility(k, axis):
    kn = upper(k, axis)
    at = lax.broadcasted_iota(jnp.int32, k.shape, axis)
    return jnp.where(at < k.shape[axis] - 1, 2.0 * k * kn / (k + kn), 0.0)


def face(here, there, trans):
    lw, lo, mw, mo = here
    lwn, lon, mwn, mon = there
    fw = mw + mwn
    fo = mo + mon
    return trans * (fw * (lw - lwn) + fo * (lo - lon)), trans * (fw + fo)


def pack_kernel(groups, *refs):
    sources, (packed, weight, above, below) = refs[:12], refs[12:16]
    loaded, padded, well_rows, sems = refs[16:28], refs[28], refs[29], refs[30]
    copies = [pltpu.make_async_copy(src, dst, sems.at[i]) for i, (src, dst) in enumerate(zip(sources, loaded))]
    for i in (8, 10, 9, 11, 1, 2, 3, 5, 6, 7, 4, 0):
        copies[i].start()
    press, sat, lamw, lamo, permx, permy, permz, pore, cell, well, index, bhp = loaded
    ny = sat.shape[1]
    for i in (8, 10):
        copies[i].wait()
    cells = cell[...]
    row_marks = marks(cells // LANES, 2 * ny)
    lane_marks = marks(cells % LANES, LANES)
    perf_weight = scatter_cells(index[...], row_marks, lane_marks)
    weight[...] = perf_weight
    for i in (0, 1, 2, 3, 4, 5, 6, 7, 9, 11):
        copies[i].wait()

    flows = []
    for x in range(2):
        s, lw, lo = sat[x], lamw[x], lamo[x]
        mw, mo = mobilities(s)
        here = (lw, lo, mw, mo)
        flow = mw * lw + mo * lo
        flows.append(flow)
        w = perf_weight[x * ny : (x + 1) * ny]
        rhs = flow * w
        diag = compressibility * pore[x] + (mw + mo) * w
        couplings = []
        for k, axis in ((permy[x], 0), (permz[x], 1)):
            there = tuple(upper(f, axis) for f in here)
            g, c = face(here, there, 0.5 * transmissibility(k, axis))
            rhs = rhs + g - lower(g, axis)
            diag = diag + c + lower(c, axis)
            couplings.append(c)
        for field, value in enumerate((rhs, diag, s, lw, lo, permx[x], *couplings)):
            edge = jnp.full((TILE, LANES), OUTSIDE[field], jnp.float32)
            padded[field, x, :TILE] = edge
            padded[field, x, TILE : TILE + ny] = value
            padded[field, x, TILE + ny :] = edge
    for member, field in enumerate((press, sat, lamw, lamo, permx)):
        above[member] = field[1]
        below[member] = field[0]

    flow_parts = jnp.concatenate(split(jnp.concatenate(flows)))
    row_parts = jnp.concatenate([row_marks.astype(jnp.bfloat16)] * 3)
    by_lane = dot(flow_parts, row_parts, ((0,), (0,)))
    inflow = index[...] * jnp.sum(by_lane * lane_marks, axis=0, keepdims=True)
    wells_each = bhp.shape[1]
    owners = marks(well[...] // wells_each, groups)
    places = marks(well[...] % wells_each + wells_each, LANES)
    well_rows[...] = scatter_cells(inflow, owners, places)
    well_rows[:, :wells_each] = jnp.broadcast_to(bhp[...], (groups, wells_each))

    def chip(c, _):
        for parity in range(2):
            d = 2 * c + parity
            start = TILE + 4 * c - HALO + ROWS * parity
            for field in range(FIELDS):
                for x in range(2):
                    at = (2 * field + x) * ROWS
                    if at == WELL_ROW:
                        packed[d, at + 1 : at + ROWS] = padded[field, x, pl.ds(start + 1 - parity, ROWS - 1)]
                    else:
                        packed[d, at : at + ROWS] = padded[field, x, pl.ds(start, ROWS)]
            packed[d, WELL_ROW : WELL_ROW + 1] = well_rows[pl.ds(d, 1)]
        return 0

    if groups <= 16:
        for c in range(groups // 2):
            chip(c, 0)
    else:
        lax.fori_loop(0, groups // 2, chip, 0)


def sat_kernel(press, sat, lamw, lamo, permx, permy, permz, pore, weight, from_below, from_above, out):
    ny = sat.shape[1]

    def parts(here, there, trans):
        p, lw, lo = here
        pn, lwn, lon = there
        t = trans * (p - pn)
        return t * (lw - lwn), t * (lo - lon)

    layers = [tuple(r[x] for r in (press, lamw, lamo)) for x in range(2)]
    ends = [tuple(r[m] for m in (0, 2, 3)) for r in (from_below, from_above)]
    chain = (ends[0], *layers, ends[1])
    perms = (from_below[4], permx[0], permx[1], from_above[4])
    across = []
    for i in range(3):
        k, kn = perms[i], perms[i + 1]
        across.append(parts(chain[i], chain[i + 1], k * kn / (k + kn)))
    for x in range(2):
        p, lw, lo = layers[x]
        water, oil = (a + b for a, b in zip(across[x], across[x + 1]))
        for k, axis in ((permy[x], 0), (permz[x], 1)):
            there = tuple(upper(f, axis) for f in layers[x])
            a, b = parts(layers[x], there, 0.5 * transmissibility(k, axis))
            water = water + a + lower(a, axis)
            oil = oil + b + lower(b, axis)
        dw, do = slopes(sat[x])
        well = weight[x * ny : (x + 1) * ny] * p
        out[x] = pore[x] * (lw - lo) + dw * (water + well * lw) + do * (oil + well * lo)


def well_kernel(partial, sat, lamw, lamo, cell, well, index, well_rows, out, grad_bhp):
    ny = sat.shape[1]
    groups = well_rows.shape[0]
    wells_each = grad_bhp.shape[1]
    rows = well_rows[...]
    place = well[...] % wells_each
    owners = marks(well[...] // wells_each, groups)
    by_owner = add_thirds(
        dot(jnp.concatenate(split(rows)), marks(place, LANES).astype(jnp.bfloat16), ((1,), (0,)))
    )
    pressure = jnp.sum(by_owner * owners, axis=0, keepdims=True)
    cells = cell[...]
    drop = scatter_cells(index[...] * pressure, marks(cells // LANES, 2 * ny), marks(cells % LANES, LANES))
    for x in range(2):
        dw, do = slopes(sat[x])
        out[x] = partial[x] - (dw * lamw[x] + do * lamo[x]) * drop[x * ny : (x + 1) * ny]
    total = -jnp.sum(rows, axis=0, keepdims=True)
    grad_bhp[...] = total[:, wells_each : 2 * wells_each]


def swap(x):
    return pltpu.roll(x, 4, 0)


def sublane():
    return lax.broadcasted_iota(jnp.int32, (TILE, LANES), 0)


def core():
    return lax.axis_index("gx") % 2


def face_kernel(received, _, own, send, well_rows):
    total = received.shape[0]
    groups = total // CHUNK
    low = sublane() < 4

    def body(parity):
        def tile(x, field):
            at = (x // 2) * CHUNK + (2 * field + x % 2) * ROWS
            start = at - HALO * parity
            if field == CZ and x % 2 == 0:
                start += parity
            inside = min(max(start, 0), total - TILE)
            rows = received[inside : inside + TILE]
            return rows if inside == start else pltpu.roll(rows, (inside - start) % TILE, 0)

        count = 2 * groups
        cells = []
        for x in range(count):
            cells.append((tile(x, LAMW), tile(x, LAMO), *mobilities(tile(x, SAT)), tile(x, PERMX)))
        before = None
        waiting = []
        for x in range(count):
            rhs, diag = tile(x, RHS), tile(x, DIAG)
            if before is not None:
                rhs, diag = rhs - before[0], diag + before[1]
            if x < count - 1:
                k, kn = cells[x][4], cells[x + 1][4]
                before = face(cells[x][:4], cells[x + 1][:4], k * kn / (k + kn))
                rhs, diag, link = rhs + before[0], diag + before[1], before[1]
            else:
                link = jnp.zeros_like(rhs)
            fields = (rhs, diag, link, tile(x, CY), tile(x, CZ))
            for f, value in enumerate(fields):
                own[f, x * TILE : (x + 1) * TILE] = value
            waiting += fields
            while len(waiting) >= 2:
                a, b = waiting[:2]
                waiting = waiting[2:]
                at = ((5 * x + 5 - len(waiting)) // 2 - 1) * TILE
                send[at : at + TILE] = jnp.where(low, pltpu.roll(a, TILE - 2, 0), pltpu.roll(b, 2, 0))

    for parity in range(2):
        pl.when(core() == parity)(functools.partial(body, parity))
    for s in range(groups):
        well_rows[s : s + 1] = received[s * CHUNK + WELL_ROW : s * CHUNK + WELL_ROW + 1]


def sweep(targets, weights, inverses, middle):
    count = len(targets)
    half = count // 2
    b = list(targets)
    for j in range(1, half):
        b[j] = b[j] + weights[j - 1] * b[j - 1]
        m = count - 1 - j
        b[m] = b[m] + weights[m + 1] * b[m + 1]
    da, db, c, inverse = middle
    u = [None] * count
    u[half - 1] = (b[half - 1] * db + c * b[half]) * inverse
    u[half] = (b[half] * da + c * b[half - 1]) * inverse
    for j in range(half - 2, -1, -1):
        u[j] = inverses[j] * b[j] + weights[j] * u[j + 1]
        m = count - 1 - j
        u[m] = inverses[m] * b[m] + weights[m] * u[m - 1]
    return u


def sweep_kernel(sweeps, own, other, out):
    count = own.shape[1] // TILE
    half = count // 2
    row = sublane()
    first = core() == 0
    kept = jnp.logical_and(row >= jnp.where(first, 0, HALO), row < jnp.where(first, ROWS, TILE))
    fields = [[], [], [], [], []]
    for i in range(5 * count // 2):
        packed = other[i * TILE : (i + 1) * TILE]
        turned = swap(packed)
        for n, value in ((2 * i, jnp.where(first, turned, packed)), (2 * i + 1, jnp.where(first, packed, turned))):
            x, f = n // 5, n % 5
            fields[f].append(jnp.where(kept, own[f, x * TILE : (x + 1) * TILE], value))
    rhs, diag, link, cy, cz = fields
    weights, inverses = [None] * count, [None] * count
    da, db = diag[0], diag[count - 1]
    for j in range(half - 1):
        m = count - 1 - j
        inverses[j], inverses[m] = 1.0 / da, 1.0 / db
        weights[j], weights[m] = link[j] * inverses[j], link[m - 1] * inverses[m]
        da = diag[j + 1] - link[j] * weights[j]
        db = diag[m - 1] - link[m - 1] * weights[m]
    c = link[half - 1]
    middle = (da, db, c, 1.0 / (da * db - c * c))

    u = sweep(rhs, weights, inverses, middle)
    for _ in range(1, sweeps):
        targets = []
        for x in range(count):
            t = rhs[x] + cy[x] * upper(u[x], 0) + lower(cy[x] * u[x], 0)
            targets.append(t + cz[x] * upper(u[x], 1) + lower(cz[x] * u[x], 1))
        u = sweep(targets, weights, inverses, middle)
    for x in range(count):
        for y in range(2):
            out[y, x : x + 1] = u[x][HALO + y : HALO + y + 1]


def call(kernel, outs, *args, scratch=(), source=pltpu.VMEM, limit=40 << 20):
    return pl.pallas_call(
        kernel,
        out_shape=tuple(o if isinstance(o, jax.ShapeDtypeStruct) else jax.ShapeDtypeStruct(o, jnp.float32) for o in outs),
        in_specs=[pl.BlockSpec(memory_space=source)] * len(args),
        out_specs=tuple(pl.BlockSpec(memory_space=pltpu.VMEM) for _ in outs),
        scratch_shapes=[pltpu.VMEM(o, jnp.float32) if isinstance(o, tuple) else o for o in scratch],
        compiler_params=pltpu.CompilerParams(vmem_limit_bytes=limit),
    )(*args)


def on_device(
    pressure, saturation, lam_water, lam_oil, perm_x, perm_y, perm_z, pore_volume,
    perf_cell, perf_well, well_index, well_pressure,
):
    groups = lax.axis_size("gx")
    ny = pressure.shape[1]
    wells_each = well_pressure.shape[0]
    fields = (pressure, saturation, lam_water, lam_oil, perm_x, perm_y, perm_z, pore_volume)
    cell, well, index, bhp = (v.reshape(1, -1) for v in (perf_cell, perf_well, well_index, well_pressure))
    given = fields + (cell, well, index, bhp)
    up = [(i, i + 1) for i in range(groups - 1)]
    down = [(i + 1, i) for i in range(groups - 1)]
    pairs = [(i, i + 1 - 2 * (i % 2)) for i in range(groups)]
    box = (2, ny, LANES)

    packed, weight, top, bottom = call(
        functools.partial(pack_kernel, groups),
        [(groups, CHUNK, LANES), (2 * ny, LANES), (5, ny, LANES), (5, ny, LANES)],
        *(pltpu.with_memory_space_constraint(v, pltpu.HBM) for v in given),
        scratch=[pltpu.VMEM(v.shape, v.dtype) for v in given]
        + [(FIELDS, 2, ny + 2 * TILE, LANES), (groups, LANES), pltpu.SemaphoreType.DMA((len(given),))],
        source=pltpu.HBM,
    )
    received = lax.all_to_all(packed, "gx", split_axis=0, concat_axis=0, tiled=True)
    from_below = lax.ppermute(top, "gx", up)
    from_above = lax.ppermute(bottom, "gx", down)
    (partial,) = call(sat_kernel, [box], *fields, weight, from_below, from_above)

    count = 2 * groups
    own, send, well_rows = call(
        face_kernel,
        [(5, count * TILE, LANES), (5 * count // 2 * TILE, LANES), (groups, LANES)],
        received.reshape(groups * CHUNK, LANES),
        partial,
    )
    other = lax.ppermute(send, "gx", pairs)
    grad_sat, grad_bhp = call(
        well_kernel, [box, (1, wells_each)],
        partial, saturation, lam_water, lam_oil, cell, well, index, well_rows,
    )
    (columns,) = call(functools.partial(sweep_kernel, SWEEPS), [(2, count, LANES)], own, other)
    return grad_sat, grad_bhp.reshape(wells_each), jnp.transpose(columns, (0, 2, 1))


def solution(mesh):
    cells = P(("members", "gx"), None, None)
    line = P(("members", "gx"))
    return jax.shard_map(
        on_device,
        mesh=mesh,
        in_specs=(cells,) * 8 + (line,) * 4,
        out_specs=(cells, line, cells),
        check_vma=False,
    )
```

```python
import functools

import jax
import jax.numpy as jnp
from jax import lax
from jax.experimental import pallas as pl
from jax.experimental.pallas import tpu as pltpu
from jax.sharding import PartitionSpec as P

water_viscosity = 0.5
oil_viscosity = 2.0
compressibility = 0.2
SWEEPS = 4

LANES = 128
TILE = 8
HALO = 3
ROWS = 5
RHS, DIAG, SAT, LAMW, LAMO, PERMX, CY, CZ = range(8)
OUTSIDE = (0.0, 1.0, 0.0, 0.0, 0.0, 1.0, 0.0, 0.0)
FIELDS = 8
WELL_ROW = CZ * 2 * ROWS
CHUNK = FIELDS * 2 * ROWS


def mobilities(s):
    return s * s * (1.0 / water_viscosity), (1.0 - s) * (1.0 - s) * (1.0 / oil_viscosity)


def slopes(s):
    return s * (2.0 / water_viscosity), (s - 1.0) * (2.0 / oil_viscosity)


def split(x):
    first = x.astype(jnp.bfloat16)
    rest = x - first.astype(jnp.float32)
    second = rest.astype(jnp.bfloat16)
    third = (rest - second.astype(jnp.float32)).astype(jnp.bfloat16)
    return first, second, third


def dot(a, b, over):
    return lax.dot_general(a, b, (over, ((), ())), preferred_element_type=jnp.float32)


def add_thirds(x):
    n = x.shape[0] // 3
    return x[:n] + x[n : 2 * n] + x[2 * n :]


def marks(index, count):
    return (lax.broadcasted_iota(jnp.int32, (count, index.shape[1]), 0) == index).astype(jnp.float32)


def scatter_cells(values, row_marks, lane_marks):
    left = jnp.concatenate([(row_marks * part.astype(jnp.float32)).astype(jnp.bfloat16) for part in split(values)])
    return add_thirds(dot(left, lane_marks.astype(jnp.bfloat16), ((1,), (1,))))


def upper(x, axis):
    return pltpu.roll(x, x.shape[axis] - 1, axis)


def lower(x, axis):
    return pltpu.roll(x, 1, axis)


def transmissibility(k, axis):
    kn = upper(k, axis)
    at = lax.broadcasted_iota(jnp.int32, k.shape, axis)
    return jnp.where(at < k.shape[axis] - 1, 2.0 * k * kn / (k + kn), 0.0)


def face(here, there, trans):
    lw, lo, mw, mo = here
    lwn, lon, mwn, mon = there
    fw = mw + mwn
    fo = mo + mon
    return trans * (fw * (lw - lwn) + fo * (lo - lon)), trans * (fw + fo)


def pack_kernel(groups, *refs):
    sources, loaded, (packed, weight, above, below) = refs[:12], refs[12:24], refs[24:28]
    padded, well_rows, sems = refs[28:]
    copies = [pltpu.make_async_copy(src, dst, sems.at[i]) for i, (src, dst) in enumerate(zip(sources, loaded))]
    for i in (8, 10, 9, 11, 1, 2, 3, 5, 6, 7, 4, 0):
        copies[i].start()
    press, sat, lamw, lamo, permx, permy, permz, pore, cell, well, index, bhp = loaded
    ny = sat.shape[1]
    for i in (8, 10):
        copies[i].wait()
    cells = cell[...]
    row_marks = marks(cells // LANES, 2 * ny)
    lane_marks = marks(cells % LANES, LANES)
    perf_weight = scatter_cells(index[...], row_marks, lane_marks)
    weight[...] = perf_weight
    for i in (0, 1, 2, 3, 4, 5, 6, 7, 9, 11):
        copies[i].wait()

    flows = []
    for x in range(2):
        s, lw, lo = sat[x], lamw[x], lamo[x]
        mw, mo = mobilities(s)
        here = (lw, lo, mw, mo)
        flow = mw * lw + mo * lo
        flows.append(flow)
        w = perf_weight[x * ny : (x + 1) * ny]
        rhs = flow * w
        diag = compressibility * pore[x] + (mw + mo) * w
        couplings = []
        for k, axis in ((permy[x], 0), (permz[x], 1)):
            there = tuple(upper(f, axis) for f in here)
            g, c = face(here, there, 0.5 * transmissibility(k, axis))
            rhs = rhs + g - lower(g, axis)
            diag = diag + c + lower(c, axis)
            couplings.append(c)
        for field, value in enumerate((rhs, diag, s, lw, lo, permx[x], *couplings)):
            edge = jnp.full((TILE, LANES), OUTSIDE[field], jnp.float32)
            padded[field, x, :TILE] = edge
            padded[field, x, TILE : TILE + ny] = value
            padded[field, x, TILE + ny :] = edge
    for member, field in enumerate((press, lamw, lamo, permx)):
        above[member] = field[1]
        below[member] = field[0]

    flow_parts = jnp.concatenate(split(jnp.concatenate(flows)))
    row_parts = jnp.concatenate([row_marks.astype(jnp.bfloat16)] * 3)
    by_lane = dot(flow_parts, row_parts, ((0,), (0,)))
    inflow = index[...] * jnp.sum(by_lane * lane_marks, axis=0, keepdims=True)
    wells_each = bhp.shape[1]
    owners = marks(well[...] // wells_each, groups)
    places = marks(well[...] % wells_each + wells_each, LANES)
    well_rows[...] = scatter_cells(inflow, owners, places)
    well_rows[:, :wells_each] = jnp.broadcast_to(bhp[...], (groups, wells_each))

    def chip(c, _):
        for parity in range(2):
            d = 2 * c + parity
            start = TILE + 4 * c - HALO + ROWS * parity
            for field in range(FIELDS):
                for x in range(2):
                    at = (2 * field + x) * ROWS
                    if at == WELL_ROW:
                        packed[d, at + 1 : at + ROWS] = padded[field, x, pl.ds(start + 1 - parity, ROWS - 1)]
                    else:
                        packed[d, at : at + ROWS] = padded[field, x, pl.ds(start, ROWS)]
            packed[d, WELL_ROW : WELL_ROW + 1] = well_rows[pl.ds(d, 1)]
        return 0

    if groups <= 16:
        for c in range(groups // 2):
            chip(c, 0)
    else:
        lax.fori_loop(0, groups // 2, chip, 0)


def sat_parts(here, there, trans):
    p, lw, lo = here
    pn, lwn, lon = there
    t = trans * (p - pn)
    return t * (lw - lwn), t * (lo - lon)


def sat_kernel(press, sat, lamw, lamo, permx, permy, permz, pore, weight, out):
    ny = sat.shape[1]
    layers = [tuple(r[x] for r in (press, lamw, lamo)) for x in range(2)]
    k, kn = permx[0], permx[1]
    inner = sat_parts(layers[0], layers[1], k * kn / (k + kn))
    for x in range(2):
        p, lw, lo = layers[x]
        water, oil = inner
        for k, axis in ((permy[x], 0), (permz[x], 1)):
            there = tuple(upper(f, axis) for f in layers[x])
            a, b = sat_parts(layers[x], there, 0.5 * transmissibility(k, axis))
            water = water + a + lower(a, axis)
            oil = oil + b + lower(b, axis)
        dw, do = slopes(sat[x])
        well = weight[x * ny : (x + 1) * ny] * p
        out[x] = pore[x] * (lw - lo) + dw * (water + well * lw) + do * (oil + well * lo)


def well_kernel(partial, sat, lamw, lamo, cell, well, index, well_rows, out, grad_bhp):
    ny = sat.shape[1]
    groups = well_rows.shape[0]
    wells_each = grad_bhp.shape[1]
    rows = well_rows[...]
    place = well[...] % wells_each
    owners = marks(well[...] // wells_each, groups)
    by_owner = add_thirds(
        dot(jnp.concatenate(split(rows)), marks(place, LANES).astype(jnp.bfloat16), ((1,), (0,)))
    )
    pressure = jnp.sum(by_owner * owners, axis=0, keepdims=True)
    cells = cell[...]
    drop = scatter_cells(index[...] * pressure, marks(cells // LANES, 2 * ny), marks(cells % LANES, LANES))
    for x in range(2):
        dw, do = slopes(sat[x])
        out[x] = partial[x] - (dw * lamw[x] + do * lamo[x]) * drop[x * ny : (x + 1) * ny]
    total = -jnp.sum(rows, axis=0, keepdims=True)
    grad_bhp[...] = total[:, wells_each : 2 * wells_each]


def outer_kernel(partial, press, sat, lamw, lamo, permx, from_below, from_above, _, out):
    for x, end in enumerate((from_below, from_above)):
        k, kn = permx[x], end[3]
        there = tuple(end[m] for m in range(3))
        water, oil = sat_parts((press[x], lamw[x], lamo[x]), there, k * kn / (k + kn))
        dw, do = slopes(sat[x])
        out[x] = partial[x] + dw * water + do * oil


def swap(x):
    return pltpu.roll(x, 4, 0)


def sublane():
    return lax.broadcasted_iota(jnp.int32, (TILE, LANES), 0)


def core():
    return lax.axis_index("gx") % 2


def face_kernel(received, _, own, send, well_rows):
    total = received.shape[0]
    groups = total // CHUNK
    low = sublane() < 4

    def body(parity):
        def tile(x, field):
            at = (x // 2) * CHUNK + (2 * field + x % 2) * ROWS
            start = at - HALO * parity
            if field == CZ and x % 2 == 0:
                start += parity
            inside = min(max(start, 0), total - TILE)
            rows = received[inside : inside + TILE]
            return rows if inside == start else pltpu.roll(rows, (inside - start) % TILE, 0)

        count = 2 * groups
        cells = []
        for x in range(count):
            cells.append((tile(x, LAMW), tile(x, LAMO), *mobilities(tile(x, SAT)), tile(x, PERMX)))
        before = None
        waiting = []
        for x in range(count):
            rhs, diag = tile(x, RHS), tile(x, DIAG)
            if before is not None:
                rhs, diag = rhs - before[0], diag + before[1]
            if x < count - 1:
                k, kn = cells[x][4], cells[x + 1][4]
                before = face(cells[x][:4], cells[x + 1][:4], k * kn / (k + kn))
                rhs, diag, link = rhs + before[0], diag + before[1], before[1]
            else:
                link = jnp.zeros_like(rhs)
            fields = (rhs, diag, link, tile(x, CY), tile(x, CZ))
            for f, value in enumerate(fields):
                own[f, x * TILE : (x + 1) * TILE] = value
            waiting += fields
            while len(waiting) >= 2:
                a, b = waiting[:2]
                waiting = waiting[2:]
                at = ((5 * x + 5 - len(waiting)) // 2 - 1) * TILE
                send[at : at + TILE] = jnp.where(low, pltpu.roll(a, TILE - 2, 0), pltpu.roll(b, 2, 0))

    for parity in range(2):
        pl.when(core() == parity)(functools.partial(body, parity))
    for s in range(groups):
        well_rows[s : s + 1] = received[s * CHUNK + WELL_ROW : s * CHUNK + WELL_ROW + 1]


def sweep(targets, weights, inverses, middle):
    count = len(targets)
    half = count // 2
    b = list(targets)
    for j in range(1, half):
        b[j] = b[j] + weights[j - 1] * b[j - 1]
        m = count - 1 - j
        b[m] = b[m] + weights[m + 1] * b[m + 1]
    da, db, c, inverse = middle
    u = [None] * count
    u[half - 1] = (b[half - 1] * db + c * b[half]) * inverse
    u[half] = (b[half] * da + c * b[half - 1]) * inverse
    for j in range(half - 2, -1, -1):
        u[j] = inverses[j] * b[j] + weights[j] * u[j + 1]
        m = count - 1 - j
        u[m] = inverses[m] * b[m] + weights[m] * u[m - 1]
    return u


def sweep_kernel(sweeps, own, other, out):
    count = own.shape[1] // TILE
    half = count // 2
    row = sublane()
    first = core() == 0
    kept = jnp.logical_and(row >= jnp.where(first, 0, HALO), row < jnp.where(first, ROWS, TILE))
    fields = [[], [], [], [], []]
    for i in range(5 * count // 2):
        packed = other[i * TILE : (i + 1) * TILE]
        turned = swap(packed)
        for n, value in ((2 * i, jnp.where(first, turned, packed)), (2 * i + 1, jnp.where(first, packed, turned))):
            x, f = n // 5, n % 5
            fields[f].append(jnp.where(kept, own[f, x * TILE : (x + 1) * TILE], value))
    rhs, diag, link, cy, cz = fields
    weights, inverses = [None] * count, [None] * count
    da, db = diag[0], diag[count - 1]
    for j in range(half - 1):
        m = count - 1 - j
        inverses[j], inverses[m] = 1.0 / da, 1.0 / db
        weights[j], weights[m] = link[j] * inverses[j], link[m - 1] * inverses[m]
        da = diag[j + 1] - link[j] * weights[j]
        db = diag[m - 1] - link[m - 1] * weights[m]
    c = link[half - 1]
    middle = (da, db, c, 1.0 / (da * db - c * c))

    u = sweep(rhs, weights, inverses, middle)
    for _ in range(1, sweeps):
        targets = []
        for x in range(count):
            t = rhs[x] + cy[x] * upper(u[x], 0) + lower(cy[x] * u[x], 0)
            targets.append(t + cz[x] * upper(u[x], 1) + lower(cz[x] * u[x], 1))
        u = sweep(targets, weights, inverses, middle)
    for x in range(count):
        for y in range(2):
            out[y, x : x + 1] = u[x][HALO + y : HALO + y + 1]


def call(kernel, outs, *args, scratch=(), in_hbm=0, limit=40 << 20):
    places = [pltpu.VMEM] * (len(args) - in_hbm) + [pltpu.HBM] * in_hbm
    args = [pltpu.with_memory_space_constraint(v, place) if place == pltpu.HBM else v for v, place in zip(args, places)]
    return pl.pallas_call(
        kernel,
        out_shape=tuple(o if isinstance(o, jax.ShapeDtypeStruct) else jax.ShapeDtypeStruct(o, jnp.float32) for o in outs),
        in_specs=[pl.BlockSpec(memory_space=place) for place in places],
        out_specs=tuple(pl.BlockSpec(memory_space=pltpu.VMEM) for _ in outs),
        scratch_shapes=[pltpu.VMEM(o, jnp.float32) if isinstance(o, tuple) else o for o in scratch],
        compiler_params=pltpu.CompilerParams(vmem_limit_bytes=limit),
    )(*args)


def on_device(
    pressure, saturation, lam_water, lam_oil, perm_x, perm_y, perm_z, pore_volume,
    perf_cell, perf_well, well_index, well_pressure,
):
    groups = lax.axis_size("gx")
    ny = pressure.shape[1]
    wells_each = well_pressure.shape[0]
    fields = (pressure, saturation, lam_water, lam_oil, perm_x, perm_y, perm_z, pore_volume)
    cell, well, index, bhp = (v.reshape(1, -1) for v in (perf_cell, perf_well, well_index, well_pressure))
    given = fields + (cell, well, index, bhp)
    up = [(i, i + 1) for i in range(groups - 1)]
    down = [(i + 1, i) for i in range(groups - 1)]
    pairs = [(i, i + 1 - 2 * (i % 2)) for i in range(groups)]
    box = (2, ny, LANES)

    *loaded, packed, weight, top, bottom = call(
        functools.partial(pack_kernel, groups),
        [jax.ShapeDtypeStruct(v.shape, v.dtype) for v in given]
        + [(groups, CHUNK, LANES), (2 * ny, LANES), (4, ny, LANES), (4, ny, LANES)],
        *given,
        scratch=[(FIELDS, 2, ny + 2 * TILE, LANES), (groups, LANES), pltpu.SemaphoreType.DMA((len(given),))],
        in_hbm=len(given),
    )
    press, sat, lamw, lamo, permx, permy, permz, pore, cell, well, index, _ = loaded
    received = lax.all_to_all(packed, "gx", split_axis=0, concat_axis=0, tiled=True)
    from_below = lax.ppermute(top, "gx", up)
    from_above = lax.ppermute(bottom, "gx", down)
    (partial,) = call(sat_kernel, [box], press, sat, lamw, lamo, permx, permy, permz, pore, weight)

    count = 2 * groups
    own, send, well_rows = call(
        face_kernel,
        [(5, count * TILE, LANES), (5 * count // 2 * TILE, LANES), (groups, LANES)],
        received.reshape(groups * CHUNK, LANES),
        partial,
    )
    other = lax.ppermute(send, "gx", pairs)
    partial, grad_bhp = call(
        well_kernel, [box, (1, wells_each)], partial, sat, lamw, lamo, cell, well, index, well_rows
    )
    (columns,) = call(functools.partial(sweep_kernel, SWEEPS), [(2, count, LANES)], own, other)
    (grad_sat,) = call(
        outer_kernel, [box], partial, press, sat, lamw, lamo, permx, from_below, from_above, columns, in_hbm=1
    )
    return grad_sat, grad_bhp.reshape(wells_each), jnp.transpose(columns, (0, 2, 1))


def solution(mesh):
    cells = P(("members", "gx"), None, None)
    line = P(("members", "gx"))
    return jax.shard_map(
        on_device,
        mesh=mesh,
        in_specs=(cells,) * 8 + (line,) * 4,
        out_specs=(cells, line, cells),
        check_vma=False,
    )
```

```python
import functools

import jax
import jax.numpy as jnp
from jax import lax
from jax.experimental import pallas as pl
from jax.experimental.pallas import tpu as pltpu
from jax.sharding import PartitionSpec as P

water_viscosity = 0.5
oil_viscosity = 2.0
compressibility = 0.2
SWEEPS = 4

LANES = 128
TILE = 8
HALO = 3
ROWS = 5
RHS, DIAG, SAT, LAMW, LAMO, PERMX, CY, CZ = range(8)
OUTSIDE = (0.0, 1.0, 0.0, 0.0, 0.0, 1.0, 0.0, 0.0)
FIELDS = 8
WELL_ROW = CZ * 2 * ROWS
CHUNK = FIELDS * 2 * ROWS


def mobilities(s):
    return s * s * (1.0 / water_viscosity), (1.0 - s) * (1.0 - s) * (1.0 / oil_viscosity)


def slopes(s):
    return s * (2.0 / water_viscosity), (s - 1.0) * (2.0 / oil_viscosity)


def split(x):
    first = x.astype(jnp.bfloat16)
    rest = x - first.astype(jnp.float32)
    second = rest.astype(jnp.bfloat16)
    third = (rest - second.astype(jnp.float32)).astype(jnp.bfloat16)
    return first, second, third


def dot(a, b, over):
    return lax.dot_general(a, b, (over, ((), ())), preferred_element_type=jnp.float32)


def add_thirds(x):
    n = x.shape[0] // 3
    return x[:n] + x[n : 2 * n] + x[2 * n :]


def marks(index, count):
    return (lax.broadcasted_iota(jnp.int32, (count, index.shape[1]), 0) == index).astype(jnp.float32)


def scatter_cells(values, row_marks, lane_marks):
    left = jnp.concatenate([(row_marks * part.astype(jnp.float32)).astype(jnp.bfloat16) for part in split(values)])
    return add_thirds(dot(left, lane_marks.astype(jnp.bfloat16), ((1,), (1,))))


def upper(x, axis):
    return pltpu.roll(x, x.shape[axis] - 1, axis)


def lower(x, axis):
    return pltpu.roll(x, 1, axis)


def transmissibility(k, axis):
    kn = upper(k, axis)
    at = lax.broadcasted_iota(jnp.int32, k.shape, axis)
    return jnp.where(at < k.shape[axis] - 1, 2.0 * k * kn / (k + kn), 0.0)


def face(here, there, trans):
    lw, lo, mw, mo = here
    lwn, lon, mwn, mon = there
    fw = mw + mwn
    fo = mo + mon
    return trans * (fw * (lw - lwn) + fo * (lo - lon)), trans * (fw + fo)


def pack_kernel(groups, *refs):
    sources, loaded, (packed, weight, above, below) = refs[:12], refs[12:24], refs[24:28]
    padded, well_rows, sems = refs[28:]
    copies = [pltpu.make_async_copy(src, dst, sems.at[i]) for i, (src, dst) in enumerate(zip(sources, loaded))]
    for i in (8, 10, 9, 11, 1, 2, 3, 5, 6, 7, 4, 0):
        copies[i].start()
    press, sat, lamw, lamo, permx, permy, permz, pore, cell, well, index, bhp = loaded
    ny = sat.shape[1]
    for i in (8, 10):
        copies[i].wait()
    cells = cell[...]
    row_marks = marks(cells // LANES, 2 * ny)
    lane_marks = marks(cells % LANES, LANES)
    perf_weight = scatter_cells(index[...], row_marks, lane_marks)
    weight[...] = perf_weight
    for i in (0, 1, 2, 3, 4, 5, 6, 7, 9, 11):
        copies[i].wait()

    flows = []
    for x in range(2):
        s, lw, lo = sat[x], lamw[x], lamo[x]
        mw, mo = mobilities(s)
        here = (lw, lo, mw, mo)
        flow = mw * lw + mo * lo
        flows.append(flow)
        w = perf_weight[x * ny : (x + 1) * ny]
        rhs = flow * w
        diag = compressibility * pore[x] + (mw + mo) * w
        couplings = []
        for k, axis in ((permy[x], 0), (permz[x], 1)):
            there = tuple(upper(f, axis) for f in here)
            g, c = face(here, there, 0.5 * transmissibility(k, axis))
            rhs = rhs + g - lower(g, axis)
            diag = diag + c + lower(c, axis)
            couplings.append(c)
        for field, value in enumerate((rhs, diag, s, lw, lo, permx[x], *couplings)):
            edge = jnp.full((TILE, LANES), OUTSIDE[field], jnp.float32)
            padded[field, x, :TILE] = edge
            padded[field, x, TILE : TILE + ny] = value
            padded[field, x, TILE + ny :] = edge
    for member, field in enumerate((press, lamw, lamo, permx)):
        above[member] = field[1]
        below[member] = field[0]

    flow_parts = jnp.concatenate(split(jnp.concatenate(flows)))
    row_parts = jnp.concatenate([row_marks.astype(jnp.bfloat16)] * 3)
    by_lane = dot(flow_parts, row_parts, ((0,), (0,)))
    inflow = index[...] * jnp.sum(by_lane * lane_marks, axis=0, keepdims=True)
    wells_each = bhp.shape[1]
    owners = marks(well[...] // wells_each, groups)
    places = marks(well[...] % wells_each + wells_each, LANES)
    well_rows[...] = scatter_cells(inflow, owners, places)
    well_rows[:, :wells_each] = jnp.broadcast_to(bhp[...], (groups, wells_each))

    def chip(c, _):
        for parity in range(2):
            d = 2 * c + parity
            start = TILE + 4 * c - HALO + ROWS * parity
            for field in range(FIELDS):
                for x in range(2):
                    at = (2 * field + x) * ROWS
                    if at == WELL_ROW:
                        packed[d, at + 1 : at + ROWS] = padded[field, x, pl.ds(start + 1 - parity, ROWS - 1)]
                    else:
                        packed[d, at : at + ROWS] = padded[field, x, pl.ds(start, ROWS)]
            packed[d, WELL_ROW : WELL_ROW + 1] = well_rows[pl.ds(d, 1)]
        return 0

    if groups <= 16:
        for c in range(groups // 2):
            chip(c, 0)
    else:
        lax.fori_loop(0, groups // 2, chip, 0)


def sat_parts(here, there, trans):
    p, lw, lo = here
    pn, lwn, lon = there
    t = trans * (p - pn)
    return t * (lw - lwn), t * (lo - lon)


def sat_kernel(press, sat, lamw, lamo, permx, permy, permz, pore, weight, out):
    ny = sat.shape[1]
    layers = [tuple(r[x] for r in (press, lamw, lamo)) for x in range(2)]
    k, kn = permx[0], permx[1]
    inner = sat_parts(layers[0], layers[1], k * kn / (k + kn))
    for x in range(2):
        p, lw, lo = layers[x]
        water, oil = inner
        for k, axis in ((permy[x], 0), (permz[x], 1)):
            there = tuple(upper(f, axis) for f in layers[x])
            a, b = sat_parts(layers[x], there, 0.5 * transmissibility(k, axis))
            water = water + a + lower(a, axis)
            oil = oil + b + lower(b, axis)
        dw, do = slopes(sat[x])
        well = weight[x * ny : (x + 1) * ny] * p
        out[x] = pore[x] * (lw - lo) + dw * (water + well * lw) + do * (oil + well * lo)


def well_kernel(
    partial, press, sat, lamw, lamo, permx, cell, well, index, well_rows, from_below, from_above, out, grad_bhp
):
    ny = sat.shape[1]
    groups = well_rows.shape[0]
    wells_each = grad_bhp.shape[1]
    rows = well_rows[...]
    place = well[...] % wells_each
    owners = marks(well[...] // wells_each, groups)
    by_owner = add_thirds(
        dot(jnp.concatenate(split(rows)), marks(place, LANES).astype(jnp.bfloat16), ((1,), (0,)))
    )
    pressure = jnp.sum(by_owner * owners, axis=0, keepdims=True)
    cells = cell[...]
    drop = scatter_cells(index[...] * pressure, marks(cells // LANES, 2 * ny), marks(cells % LANES, LANES))
    for x, end in enumerate((from_below, from_above)):
        k, kn = permx[x], end[3]
        lw, lo = lamw[x], lamo[x]
        water, oil = sat_parts((press[x], lw, lo), tuple(end[m] for m in range(3)), k * kn / (k + kn))
        dw, do = slopes(sat[x])
        well = drop[x * ny : (x + 1) * ny]
        out[x] = partial[x] + dw * (water - well * lw) + do * (oil - well * lo)
    total = -jnp.sum(rows, axis=0, keepdims=True)
    grad_bhp[...] = total[:, wells_each : 2 * wells_each]


def swap(x):
    return pltpu.roll(x, 4, 0)


def sublane():
    return lax.broadcasted_iota(jnp.int32, (TILE, LANES), 0)


def core():
    return lax.axis_index("gx") % 2


def face_kernel(received, _, own, send, well_rows):
    total = received.shape[0]
    groups = total // CHUNK
    low = sublane() < 4

    def body(parity):
        def tile(x, field):
            at = (x // 2) * CHUNK + (2 * field + x % 2) * ROWS
            start = at - HALO * parity
            if field == CZ and x % 2 == 0:
                start += parity
            inside = min(max(start, 0), total - TILE)
            rows = received[inside : inside + TILE]
            return rows if inside == start else pltpu.roll(rows, (inside - start) % TILE, 0)

        count = 2 * groups
        cells = []
        for x in range(count):
            cells.append((tile(x, LAMW), tile(x, LAMO), *mobilities(tile(x, SAT)), tile(x, PERMX)))
        before = None
        waiting = []
        for x in range(count):
            rhs, diag = tile(x, RHS), tile(x, DIAG)
            if before is not None:
                rhs, diag = rhs - before[0], diag + before[1]
            if x < count - 1:
                k, kn = cells[x][4], cells[x + 1][4]
                before = face(cells[x][:4], cells[x + 1][:4], k * kn / (k + kn))
                rhs, diag, link = rhs + before[0], diag + before[1], before[1]
            else:
                link = jnp.zeros_like(rhs)
            fields = (rhs, diag, link, tile(x, CY), tile(x, CZ))
            for f, value in enumerate(fields):
                own[f, x * TILE : (x + 1) * TILE] = value
            waiting += fields
            while len(waiting) >= 2:
                a, b = waiting[:2]
                waiting = waiting[2:]
                at = ((5 * x + 5 - len(waiting)) // 2 - 1) * TILE
                send[at : at + TILE] = jnp.where(low, pltpu.roll(a, TILE - 2, 0), pltpu.roll(b, 2, 0))

    for parity in range(2):
        pl.when(core() == parity)(functools.partial(body, parity))
    for s in range(groups):
        well_rows[s : s + 1] = received[s * CHUNK + WELL_ROW : s * CHUNK + WELL_ROW + 1]


def sweep(targets, weights, inverses, middle):
    count = len(targets)
    half = count // 2
    b = list(targets)
    for j in range(1, half):
        b[j] = b[j] + weights[j - 1] * b[j - 1]
        m = count - 1 - j
        b[m] = b[m] + weights[m + 1] * b[m + 1]
    da, db, c, inverse = middle
    u = [None] * count
    u[half - 1] = (b[half - 1] * db + c * b[half]) * inverse
    u[half] = (b[half] * da + c * b[half - 1]) * inverse
    for j in range(half - 2, -1, -1):
        u[j] = inverses[j] * b[j] + weights[j] * u[j + 1]
        m = count - 1 - j
        u[m] = inverses[m] * b[m] + weights[m] * u[m - 1]
    return u


def sweep_kernel(sweeps, own, other, out):
    count = own.shape[1] // TILE
    half = count // 2
    row = sublane()
    first = core() == 0
    kept = jnp.logical_and(row >= jnp.where(first, 0, HALO), row < jnp.where(first, ROWS, TILE))
    fields = [[], [], [], [], []]
    for i in range(5 * count // 2):
        packed = other[i * TILE : (i + 1) * TILE]
        turned = swap(packed)
        for n, value in ((2 * i, jnp.where(first, turned, packed)), (2 * i + 1, jnp.where(first, packed, turned))):
            x, f = n // 5, n % 5
            fields[f].append(jnp.where(kept, own[f, x * TILE : (x + 1) * TILE], value))
    rhs, diag, link, cy, cz = fields
    weights, inverses = [None] * count, [None] * count
    da, db = diag[0], diag[count - 1]
    for j in range(half - 1):
        m = count - 1 - j
        inverses[j], inverses[m] = 1.0 / da, 1.0 / db
        weights[j], weights[m] = link[j] * inverses[j], link[m - 1] * inverses[m]
        da = diag[j + 1] - link[j] * weights[j]
        db = diag[m - 1] - link[m - 1] * weights[m]
    c = link[half - 1]
    middle = (da, db, c, 1.0 / (da * db - c * c))

    u = sweep(rhs, weights, inverses, middle)
    for _ in range(1, sweeps):
        targets = []
        for x in range(count):
            t = rhs[x] + cy[x] * upper(u[x], 0) + lower(cy[x] * u[x], 0)
            targets.append(t + cz[x] * upper(u[x], 1) + lower(cz[x] * u[x], 1))
        u = sweep(targets, weights, inverses, middle)
    for x in range(count):
        for y in range(2):
            out[y, x : x + 1] = u[x][HALO + y : HALO + y + 1]


def call(kernel, outs, *args, scratch=(), in_hbm=0):
    places = [pltpu.VMEM] * (len(args) - in_hbm) + [pltpu.HBM] * in_hbm
    args = [pltpu.with_memory_space_constraint(v, place) if place == pltpu.HBM else v for v, place in zip(args, places)]
    return pl.pallas_call(
        kernel,
        out_shape=tuple(o if isinstance(o, jax.ShapeDtypeStruct) else jax.ShapeDtypeStruct(o, jnp.float32) for o in outs),
        in_specs=[pl.BlockSpec(memory_space=place) for place in places],
        out_specs=tuple(pl.BlockSpec(memory_space=pltpu.VMEM) for _ in outs),
        scratch_shapes=[pltpu.VMEM(o, jnp.float32) if isinstance(o, tuple) else o for o in scratch],
        compiler_params=pltpu.CompilerParams(vmem_limit_bytes=40 << 20),
    )(*args)


def on_device(
    pressure, saturation, lam_water, lam_oil, perm_x, perm_y, perm_z, pore_volume,
    perf_cell, perf_well, well_index, well_pressure,
):
    groups = lax.axis_size("gx")
    ny = pressure.shape[1]
    wells_each = well_pressure.shape[0]
    fields = (pressure, saturation, lam_water, lam_oil, perm_x, perm_y, perm_z, pore_volume)
    cell, well, index, bhp = (v.reshape(1, -1) for v in (perf_cell, perf_well, well_index, well_pressure))
    given = fields + (cell, well, index, bhp)
    up = [(i, i + 1) for i in range(groups - 1)]
    down = [(i + 1, i) for i in range(groups - 1)]
    pairs = [(i, i + 1 - 2 * (i % 2)) for i in range(groups)]
    box = (2, ny, LANES)

    *loaded, packed, weight, top, bottom = call(
        functools.partial(pack_kernel, groups),
        [jax.ShapeDtypeStruct(v.shape, v.dtype) for v in given]
        + [(groups, CHUNK, LANES), (2 * ny, LANES), (4, ny, LANES), (4, ny, LANES)],
        *given,
        scratch=[(FIELDS, 2, ny + 2 * TILE, LANES), (groups, LANES), pltpu.SemaphoreType.DMA((len(given),))],
        in_hbm=len(given),
    )
    press, sat, lamw, lamo, permx, permy, permz, pore, cell, well, index, _ = loaded
    received = lax.all_to_all(packed, "gx", split_axis=0, concat_axis=0, tiled=True)
    from_below = lax.ppermute(top, "gx", up)
    from_above = lax.ppermute(bottom, "gx", down)
    (partial,) = call(sat_kernel, [box], press, sat, lamw, lamo, permx, permy, permz, pore, weight)

    count = 2 * groups
    own, send, well_rows = call(
        face_kernel,
        [(5, count * TILE, LANES), (5 * count // 2 * TILE, LANES), (groups, LANES)],
        received.reshape(groups * CHUNK, LANES),
        partial,
    )
    other = lax.ppermute(send, "gx", pairs)
    grad_sat, grad_bhp = call(
        well_kernel, [box, (1, wells_each)],
        partial, press, sat, lamw, lamo, permx, cell, well, index, well_rows, from_below, from_above,
    )
    (columns,) = call(functools.partial(sweep_kernel, SWEEPS), [(2, count, LANES)], own, other)
    return grad_sat, grad_bhp.reshape(wells_each), jnp.transpose(columns, (0, 2, 1))


def solution(mesh):
    cells = P(("members", "gx"), None, None)
    line = P(("members", "gx"))
    return jax.shard_map(
        on_device,
        mesh=mesh,
        in_specs=(cells,) * 8 + (line,) * 4,
        out_specs=(cells, line, cells),
        check_vma=False,
    )
```

```python
import functools

import jax
import jax.numpy as jnp
from jax import lax
from jax.experimental import pallas as pl
from jax.experimental.pallas import tpu as pltpu
from jax.sharding import PartitionSpec as P

water_viscosity = 0.5
oil_viscosity = 2.0
compressibility = 0.2
SWEEPS = 4

LANES = 128
TILE = 8
HALO = 3
ROWS = 5
RHS, DIAG, SAT, LAMW, LAMO, PERMX, CY, CZ = range(8)
OUTSIDE = (0.0, 1.0, 0.0, 0.0, 0.0, 1.0, 0.0, 0.0)
FIELDS = 8
WELL_ROW = CZ * 2 * ROWS
CHUNK = FIELDS * 2 * ROWS


def mobilities(s):
    return s * s * (1.0 / water_viscosity), (1.0 - s) * (1.0 - s) * (1.0 / oil_viscosity)


def slopes(s):
    return s * (2.0 / water_viscosity), (s - 1.0) * (2.0 / oil_viscosity)


def split(x):
    first = x.astype(jnp.bfloat16)
    rest = x - first.astype(jnp.float32)
    second = rest.astype(jnp.bfloat16)
    third = (rest - second.astype(jnp.float32)).astype(jnp.bfloat16)
    return first, second, third


def dot(a, b, over):
    return lax.dot_general(a, b, (over, ((), ())), preferred_element_type=jnp.float32)


def add_thirds(x):
    n = x.shape[0] // 3
    return x[:n] + x[n : 2 * n] + x[2 * n :]


def marks(index, count):
    return (lax.broadcasted_iota(jnp.int32, (count, index.shape[1]), 0) == index).astype(jnp.float32)


def scatter_cells(values, row_marks, lane_marks):
    left = jnp.concatenate([(row_marks * part.astype(jnp.float32)).astype(jnp.bfloat16) for part in split(values)])
    return add_thirds(dot(left, lane_marks.astype(jnp.bfloat16), ((1,), (1,))))


def core():
    return lax.axis_index("gx") % 2


def upper(x, axis):
    return pltpu.roll(x, x.shape[axis] - 1, axis)


def lower(x, axis):
    return pltpu.roll(x, 1, axis)


def transmissibility(k, axis):
    kn = upper(k, axis)
    at = lax.broadcasted_iota(jnp.int32, k.shape, axis)
    return jnp.where(at < k.shape[axis] - 1, 2.0 * k * kn / (k + kn), 0.0)


def face(here, there, trans):
    lw, lo, mw, mo = here
    lwn, lon, mwn, mon = there
    fw = mw + mwn
    fo = mo + mon
    return trans * (fw * (lw - lwn) + fo * (lo - lon)), trans * (fw + fo)


def pack_kernel(groups, *refs):
    sources, loaded, (packed, weight, chip_edge, outer_edge) = refs[:12], refs[12:24], refs[24:28]
    padded, well_rows, sems = refs[28:]
    copies = [pltpu.make_async_copy(src, dst, sems.at[i]) for i, (src, dst) in enumerate(zip(sources, loaded))]
    for i in (8, 10, 9, 11, 1, 2, 3, 5, 6, 7, 4, 0):
        copies[i].start()
    press, sat, lamw, lamo, permx, permy, permz, pore, cell, well, index, bhp = loaded
    ny = sat.shape[1]
    for i in (8, 10):
        copies[i].wait()
    cells = cell[...]
    row_marks = marks(cells // LANES, 2 * ny)
    lane_marks = marks(cells % LANES, LANES)
    perf_weight = scatter_cells(index[...], row_marks, lane_marks)
    weight[...] = perf_weight
    for i in (0, 1, 2, 3, 4, 5, 6, 7, 9, 11):
        copies[i].wait()

    flows = []
    for x in range(2):
        s, lw, lo = sat[x], lamw[x], lamo[x]
        mw, mo = mobilities(s)
        here = (lw, lo, mw, mo)
        flow = mw * lw + mo * lo
        flows.append(flow)
        w = perf_weight[x * ny : (x + 1) * ny]
        rhs = flow * w
        diag = compressibility * pore[x] + (mw + mo) * w
        couplings = []
        for k, axis in ((permy[x], 0), (permz[x], 1)):
            there = tuple(upper(f, axis) for f in here)
            g, c = face(here, there, 0.5 * transmissibility(k, axis))
            rhs = rhs + g - lower(g, axis)
            diag = diag + c + lower(c, axis)
            couplings.append(c)
        for field, value in enumerate((rhs, diag, s, lw, lo, permx[x], *couplings)):
            edge = jnp.full((TILE, LANES), OUTSIDE[field], jnp.float32)
            padded[field, x, :TILE] = edge
            padded[field, x, TILE : TILE + ny] = value
            padded[field, x, TILE + ny :] = edge
    for member, field in enumerate((press, lamw, lamo, permx)):
        chip_edge[member] = field[1 - core()]
        outer_edge[member] = field[core()]

    flow_parts = jnp.concatenate(split(jnp.concatenate(flows)))
    row_parts = jnp.concatenate([row_marks.astype(jnp.bfloat16)] * 3)
    by_lane = dot(flow_parts, row_parts, ((0,), (0,)))
    inflow = index[...] * jnp.sum(by_lane * lane_marks, axis=0, keepdims=True)
    wells_each = bhp.shape[1]
    owners = marks(well[...] // wells_each, groups)
    places = marks(well[...] % wells_each + wells_each, LANES)
    well_rows[...] = scatter_cells(inflow, owners, places)
    well_rows[:, :wells_each] = jnp.broadcast_to(bhp[...], (groups, wells_each))

    def chip(c, _):
        for parity in range(2):
            d = 2 * c + parity
            start = TILE + 4 * c - HALO + ROWS * parity
            for field in range(FIELDS):
                for x in range(2):
                    at = (2 * field + x) * ROWS
                    if at == WELL_ROW:
                        packed[d, at + 1 : at + ROWS] = padded[field, x, pl.ds(start + 1 - parity, ROWS - 1)]
                    else:
                        packed[d, at : at + ROWS] = padded[field, x, pl.ds(start, ROWS)]
            packed[d, WELL_ROW : WELL_ROW + 1] = well_rows[pl.ds(d, 1)]
        return 0

    if groups <= 16:
        for c in range(groups // 2):
            chip(c, 0)
    else:
        lax.fori_loop(0, groups // 2, chip, 0)


def sat_parts(here, there, trans):
    p, lw, lo = here
    pn, lwn, lon = there
    t = trans * (p - pn)
    return t * (lw - lwn), t * (lo - lon)


def sat_kernel(press, sat, lamw, lamo, permx, permy, permz, pore, weight, from_chip, from_outside, out):
    ny = sat.shape[1]
    first = core() == 0
    layers = [tuple(r[x] for r in (press, lamw, lamo, permx)) for x in range(2)]
    ends = [tuple(r[m] for m in range(4)) for r in (from_outside, from_chip)]
    below = tuple(jnp.where(first, a, b) for a, b in zip(*ends))
    above = tuple(jnp.where(first, b, a) for a, b in zip(*ends))
    chain = (below, *layers, above)
    across = []
    for here, there in zip(chain, chain[1:]):
        k, kn = here[3], there[3]
        across.append(sat_parts(here[:3], there[:3], k * kn / (k + kn)))
    for x in range(2):
        p, lw, lo, _ = layers[x]
        water, oil = (a + b for a, b in zip(across[x], across[x + 1]))
        for k, axis in ((permy[x], 0), (permz[x], 1)):
            there = tuple(upper(f, axis) for f in (p, lw, lo))
            a, b = sat_parts((p, lw, lo), there, 0.5 * transmissibility(k, axis))
            water = water + a + lower(a, axis)
            oil = oil + b + lower(b, axis)
        dw, do = slopes(sat[x])
        well = weight[x * ny : (x + 1) * ny] * p
        out[x] = pore[x] * (lw - lo) + dw * (water + well * lw) + do * (oil + well * lo)


def well_kernel(partial, sat, lamw, lamo, cell, well, index, well_rows, out, grad_bhp):
    ny = sat.shape[1]
    groups = well_rows.shape[0]
    wells_each = grad_bhp.shape[1]
    rows = well_rows[...]
    place = well[...] % wells_each
    owners = marks(well[...] // wells_each, groups)
    by_owner = add_thirds(
        dot(jnp.concatenate(split(rows)), marks(place, LANES).astype(jnp.bfloat16), ((1,), (0,)))
    )
    pressure = jnp.sum(by_owner * owners, axis=0, keepdims=True)
    cells = cell[...]
    drop = scatter_cells(index[...] * pressure, marks(cells // LANES, 2 * ny), marks(cells % LANES, LANES))
    for x in range(2):
        dw, do = slopes(sat[x])
        out[x] = partial[x] - (dw * lamw[x] + do * lamo[x]) * drop[x * ny : (x + 1) * ny]
    total = -jnp.sum(rows, axis=0, keepdims=True)
    grad_bhp[...] = total[:, wells_each : 2 * wells_each]


def swap(x):
    return pltpu.roll(x, 4, 0)


def sublane():
    return lax.broadcasted_iota(jnp.int32, (TILE, LANES), 0)


def face_kernel(received, _, own, send, well_rows):
    total = received.shape[0]
    groups = total // CHUNK
    low = sublane() < 4

    def body(parity):
        def tile(x, field):
            at = (x // 2) * CHUNK + (2 * field + x % 2) * ROWS
            start = at - HALO * parity
            if field == CZ and x % 2 == 0:
                start += parity
            inside = min(max(start, 0), total - TILE)
            rows = received[inside : inside + TILE]
            return rows if inside == start else pltpu.roll(rows, (inside - start) % TILE, 0)

        count = 2 * groups
        cells = []
        for x in range(count):
            cells.append((tile(x, LAMW), tile(x, LAMO), *mobilities(tile(x, SAT)), tile(x, PERMX)))
        before = None
        waiting = []
        for x in range(count):
            rhs, diag = tile(x, RHS), tile(x, DIAG)
            if before is not None:
                rhs, diag = rhs - before[0], diag + before[1]
            if x < count - 1:
                k, kn = cells[x][4], cells[x + 1][4]
                before = face(cells[x][:4], cells[x + 1][:4], k * kn / (k + kn))
                rhs, diag, link = rhs + before[0], diag + before[1], before[1]
            else:
                link = jnp.zeros_like(rhs)
            fields = (rhs, diag, link, tile(x, CY), tile(x, CZ))
            for f, value in enumerate(fields):
                own[f, x * TILE : (x + 1) * TILE] = value
            waiting += fields
            while len(waiting) >= 2:
                a, b = waiting[:2]
                waiting = waiting[2:]
                at = ((5 * x + 5 - len(waiting)) // 2 - 1) * TILE
                send[at : at + TILE] = jnp.where(low, pltpu.roll(a, TILE - 2, 0), pltpu.roll(b, 2, 0))

    for parity in range(2):
        pl.when(core() == parity)(functools.partial(body, parity))
    for s in range(groups):
        well_rows[s : s + 1] = received[s * CHUNK + WELL_ROW : s * CHUNK + WELL_ROW + 1]


def sweep(targets, weights, inverses, middle):
    count = len(targets)
    half = count // 2
    b = list(targets)
    for j in range(1, half):
        b[j] = b[j] + weights[j - 1] * b[j - 1]
        m = count - 1 - j
        b[m] = b[m] + weights[m + 1] * b[m + 1]
    da, db, c, inverse = middle
    u = [None] * count
    u[half - 1] = (b[half - 1] * db + c * b[half]) * inverse
    u[half] = (b[half] * da + c * b[half - 1]) * inverse
    for j in range(half - 2, -1, -1):
        u[j] = inverses[j] * b[j] + weights[j] * u[j + 1]
        m = count - 1 - j
        u[m] = inverses[m] * b[m] + weights[m] * u[m - 1]
    return u


def sweep_kernel(sweeps, own, other, out):
    count = own.shape[1] // TILE
    half = count // 2
    row = sublane()
    first = core() == 0
    kept = jnp.logical_and(row >= jnp.where(first, 0, HALO), row < jnp.where(first, ROWS, TILE))
    fields = [[], [], [], [], []]
    for i in range(5 * count // 2):
        packed = other[i * TILE : (i + 1) * TILE]
        turned = swap(packed)
        for n, value in ((2 * i, jnp.where(first, turned, packed)), (2 * i + 1, jnp.where(first, packed, turned))):
            x, f = n // 5, n % 5
            fields[f].append(jnp.where(kept, own[f, x * TILE : (x + 1) * TILE], value))
    rhs, diag, link, cy, cz = fields
    weights, inverses = [None] * count, [None] * count
    da, db = diag[0], diag[count - 1]
    for j in range(half - 1):
        m = count - 1 - j
        inverses[j], inverses[m] = 1.0 / da, 1.0 / db
        weights[j], weights[m] = link[j] * inverses[j], link[m - 1] * inverses[m]
        da = diag[j + 1] - link[j] * weights[j]
        db = diag[m - 1] - link[m - 1] * weights[m]
    c = link[half - 1]
    middle = (da, db, c, 1.0 / (da * db - c * c))

    u = sweep(rhs, weights, inverses, middle)
    for _ in range(1, sweeps):
        targets = []
        for x in range(count):
            t = rhs[x] + cy[x] * upper(u[x], 0) + lower(cy[x] * u[x], 0)
            targets.append(t + cz[x] * upper(u[x], 1) + lower(cz[x] * u[x], 1))
        u = sweep(targets, weights, inverses, middle)
    for x in range(count):
        for y in range(2):
            out[y, x : x + 1] = u[x][HALO + y : HALO + y + 1]


def call(kernel, outs, *args, scratch=(), in_hbm=0):
    places = [pltpu.VMEM] * (len(args) - in_hbm) + [pltpu.HBM] * in_hbm
    args = [pltpu.with_memory_space_constraint(v, place) if place == pltpu.HBM else v for v, place in zip(args, places)]
    return pl.pallas_call(
        kernel,
        out_shape=tuple(o if isinstance(o, jax.ShapeDtypeStruct) else jax.ShapeDtypeStruct(o, jnp.float32) for o in outs),
        in_specs=[pl.BlockSpec(memory_space=place) for place in places],
        out_specs=tuple(pl.BlockSpec(memory_space=pltpu.VMEM) for _ in outs),
        scratch_shapes=[pltpu.VMEM(o, jnp.float32) if isinstance(o, tuple) else o for o in scratch],
        compiler_params=pltpu.CompilerParams(vmem_limit_bytes=40 << 20),
    )(*args)


def on_device(
    pressure, saturation, lam_water, lam_oil, perm_x, perm_y, perm_z, pore_volume,
    perf_cell, perf_well, well_index, well_pressure,
):
    groups = lax.axis_size("gx")
    ny = pressure.shape[1]
    wells_each = well_pressure.shape[0]
    fields = (pressure, saturation, lam_water, lam_oil, perm_x, perm_y, perm_z, pore_volume)
    cell, well, index, bhp = (v.reshape(1, -1) for v in (perf_cell, perf_well, well_index, well_pressure))
    given = fields + (cell, well, index, bhp)
    chip_pairs = [(i, i + 1 - 2 * (i % 2)) for i in range(groups)]
    outer_pairs = [(i, i - 1 + 2 * (i % 2)) for i in range(1, groups - 1)]
    box = (2, ny, LANES)

    *loaded, packed, weight, chip_edge, outer_edge = call(
        functools.partial(pack_kernel, groups),
        [jax.ShapeDtypeStruct(v.shape, v.dtype) for v in given]
        + [(groups, CHUNK, LANES), (2 * ny, LANES), (4, ny, LANES), (4, ny, LANES)],
        *given,
        scratch=[(FIELDS, 2, ny + 2 * TILE, LANES), (groups, LANES), pltpu.SemaphoreType.DMA((len(given),))],
        in_hbm=len(given),
    )
    press, sat, lamw, lamo, permx, permy, permz, pore, cell, well, index, _ = loaded
    received = lax.all_to_all(packed, "gx", split_axis=0, concat_axis=0, tiled=True)
    from_outside = lax.ppermute(outer_edge, "gx", outer_pairs)
    from_chip = lax.ppermute(chip_edge, "gx", chip_pairs)
    (partial,) = call(
        sat_kernel, [box], press, sat, lamw, lamo, permx, permy, permz, pore, weight, from_chip, from_outside
    )

    count = 2 * groups
    own, send, well_rows = call(
        face_kernel,
        [(5, count * TILE, LANES), (5 * count // 2 * TILE, LANES), (groups, LANES)],
        received.reshape(groups * CHUNK, LANES),
        partial,
    )
    other = lax.ppermute(send, "gx", chip_pairs)
    grad_sat, grad_bhp = call(
        well_kernel, [box, (1, wells_each)], partial, sat, lamw, lamo, cell, well, index, well_rows
    )
    (columns,) = call(functools.partial(sweep_kernel, SWEEPS), [(2, count, LANES)], own, other)
    return grad_sat, grad_bhp.reshape(wells_each), jnp.transpose(columns, (0, 2, 1))


def solution(mesh):
    cells = P(("members", "gx"), None, None)
    line = P(("members", "gx"))
    return jax.shard_map(
        on_device,
        mesh=mesh,
        in_specs=(cells,) * 8 + (line,) * 4,
        out_specs=(cells, line, cells),
        check_vma=False,
    )
```

```python
import functools

import jax
import jax.numpy as jnp
from jax import lax
from jax.experimental import pallas as pl
from jax.experimental.pallas import tpu as pltpu
from jax.sharding import PartitionSpec as P

water_viscosity = 0.5
oil_viscosity = 2.0
compressibility = 0.2
SWEEPS = 4

LANES = 128
TILE = 8
HALO = 3
ROWS = 5
RHS, DIAG, CY, CZ, INNER, SAT, LAMW, LAMO, PERMX, CHIP = 0, 2, 4, 6, 8, 9, 10, 11, 12, 13
FIELDS = 14
WELL_ROW = FIELDS * ROWS
CHUNK = WELL_ROW + 2


def mobilities(s):
    return s * s * (1.0 / water_viscosity), (1.0 - s) * (1.0 - s) * (1.0 / oil_viscosity)


def slopes(s):
    return s * (2.0 / water_viscosity), (s - 1.0) * (2.0 / oil_viscosity)


def split(x):
    first = x.astype(jnp.bfloat16)
    rest = x - first.astype(jnp.float32)
    second = rest.astype(jnp.bfloat16)
    third = (rest - second.astype(jnp.float32)).astype(jnp.bfloat16)
    return first, second, third


def dot(a, b, over):
    return lax.dot_general(a, b, (over, ((), ())), preferred_element_type=jnp.float32)


def add_thirds(x):
    n = x.shape[0] // 3
    return x[:n] + x[n : 2 * n] + x[2 * n :]


def marks(index, count):
    return (lax.broadcasted_iota(jnp.int32, (count, index.shape[1]), 0) == index).astype(jnp.float32)


def scatter_cells(values, row_marks, lane_marks):
    left = jnp.concatenate([(row_marks * part.astype(jnp.float32)).astype(jnp.bfloat16) for part in split(values)])
    return add_thirds(dot(left, lane_marks.astype(jnp.bfloat16), ((1,), (1,))))


def core():
    return lax.axis_index("gx") % 2


def upper(x, axis):
    return pltpu.roll(x, x.shape[axis] - 1, axis)


def lower(x, axis):
    return pltpu.roll(x, 1, axis)


def transmissibility(k, axis):
    kn = upper(k, axis)
    at = lax.broadcasted_iota(jnp.int32, k.shape, axis)
    return jnp.where(at < k.shape[axis] - 1, 2.0 * k * kn / (k + kn), 0.0)


def face(here, there, trans):
    lw, lo, mw, mo = here
    lwn, lon, mwn, mon = there
    fw = mw + mwn
    fo = mo + mon
    return trans * (fw * (lw - lwn) + fo * (lo - lon)), trans * (fw + fo)


def load_kernel(*refs):
    sources, loaded, edge, sems = refs[:12], refs[12:24], refs[24], refs[25]
    pairs = [(sources[i].at[1 - core()], edge.at[i]) for i in range(5)] + list(zip(sources, loaded))
    copies = [pltpu.make_async_copy(src, dst, sems.at[i]) for i, (src, dst) in enumerate(pairs)]
    for copy in copies:
        copy.start()
    for copy in copies:
        copy.wait()


def cell_kernel(
    groups, sat, lamw, lamo, permx, permy, permz, pore, cell, well, index, bhp,
    rhs_out, diag_out, cy_out, cz_out, inner_out, weight, well_rows,
):
    ny = sat.shape[1]
    cells = cell[...]
    row_marks = marks(cells // LANES, 2 * ny)
    lane_marks = marks(cells % LANES, LANES)
    perf_weight = scatter_cells(index[...], row_marks, lane_marks)
    weight[...] = perf_weight
    flows, layers, rhs, diag = [], [], [], []
    for x in range(2):
        s, lw, lo = sat[x], lamw[x], lamo[x]
        mw, mo = mobilities(s)
        layers.append((lw, lo, mw, mo))
        flow = mw * lw + mo * lo
        flows.append(flow)
        w = perf_weight[x * ny : (x + 1) * ny]
        rhs.append(flow * w)
        diag.append(compressibility * pore[x] + (mw + mo) * w)
        for k, axis, out in ((permy[x], 0, cy_out), (permz[x], 1, cz_out)):
            there = tuple(upper(f, axis) for f in layers[x])
            g, c = face(layers[x], there, 0.5 * transmissibility(k, axis))
            rhs[x] += g - lower(g, axis)
            diag[x] += c + lower(c, axis)
            out[x] = c
    k, kn = permx[0], permx[1]
    g, c = face(layers[0], layers[1], k * kn / (k + kn))
    inner_out[...] = c
    for x in range(2):
        rhs_out[x] = rhs[x] + (1 - 2 * x) * g
        diag_out[x] = diag[x] + c

    flow_parts = jnp.concatenate(split(jnp.concatenate(flows)))
    row_parts = jnp.concatenate([row_marks.astype(jnp.bfloat16)] * 3)
    by_lane = dot(flow_parts, row_parts, ((0,), (0,)))
    inflow = index[...] * jnp.sum(by_lane * lane_marks, axis=0, keepdims=True)
    wells_each = bhp.shape[1]
    owners = marks(well[...] // wells_each, groups)
    places = marks(well[...] % wells_each + wells_each, LANES)
    well_rows[...] = scatter_cells(inflow, owners, places)
    well_rows[:, :wells_each] = jnp.broadcast_to(bhp[...], (groups, wells_each))


def pack_kernel(
    groups, press, sat, lamw, lamo, permx, from_chip, rhs, diag, cy, cz, inner, well_rows,
    packed, outer_a, outer_b, padded,
):
    ny = sat.shape[1]
    near, far = 1 - core(), core()
    k, kn = permx[near], from_chip[4]
    here = (lamw[near], lamo[near], *mobilities(sat[near]))
    there = (from_chip[2], from_chip[3], *mobilities(from_chip[1]))
    g, c = face(here, there, k * kn / (k + kn))
    for i, ref in enumerate((press, lamw)):
        outer_a[i] = ref[far]
    for i, ref in enumerate((lamo, permx)):
        outer_b[i] = ref[far]

    values = [None] * FIELDS
    for x in range(2):
        touches = near == x
        values[RHS + x] = rhs[x] + jnp.where(touches, g, 0.0)
        values[DIAG + x] = diag[x] + jnp.where(touches, c, 0.0)
        values[CY + x] = cy[x]
        values[CZ + x] = cz[x]
    values[INNER] = inner[...]
    values[SAT], values[LAMW], values[LAMO], values[PERMX] = sat[far], lamw[far], lamo[far], permx[far]
    values[CHIP] = c
    for f, value in enumerate(values):
        edge = jnp.full((TILE, LANES), 1.0 if f in (DIAG, DIAG + 1, PERMX) else 0.0, jnp.float32)
        padded[f, :TILE] = edge
        padded[f, TILE : TILE + ny] = value
        padded[f, TILE + ny :] = edge

    def chip(c, _):
        for parity in range(2):
            d = 2 * c + parity
            start = TILE + 4 * c - HALO + ROWS * parity
            for f in range(FIELDS):
                packed[d, f * ROWS : (f + 1) * ROWS] = padded[f, pl.ds(start, ROWS)]
            packed[d, WELL_ROW : WELL_ROW + 1] = well_rows[pl.ds(d, 1)]
            packed[d, WELL_ROW + 1 :] = jnp.zeros((1, LANES), jnp.float32)
        return 0

    if groups <= 16:
        for c in range(groups // 2):
            chip(c, 0)
    else:
        lax.fori_loop(0, groups // 2, chip, 0)


def sat_parts(here, there, trans):
    p, lw, lo = here
    pn, lwn, lon = there
    t = trans * (p - pn)
    return t * (lw - lwn), t * (lo - lon)


def sat_kernel(press, sat, lamw, lamo, permx, permy, permz, pore, weight, from_chip, outside_a, outside_b, out):
    ny = sat.shape[1]
    first = core() == 0
    layers = [tuple(r[x] for r in (press, lamw, lamo, permx)) for x in range(2)]
    ends = (outside_a[0], outside_a[1], outside_b[0], outside_b[1]), tuple(from_chip[m] for m in (0, 2, 3, 4))
    below = tuple(jnp.where(first, a, b) for a, b in zip(*ends))
    above = tuple(jnp.where(first, b, a) for a, b in zip(*ends))
    chain = (below, *layers, above)
    across = []
    for here, there in zip(chain, chain[1:]):
        k, kn = here[3], there[3]
        across.append(sat_parts(here[:3], there[:3], k * kn / (k + kn)))
    for x in range(2):
        p, lw, lo, _ = layers[x]
        water, oil = (a + b for a, b in zip(across[x], across[x + 1]))
        for k, axis in ((permy[x], 0), (permz[x], 1)):
            there = tuple(upper(f, axis) for f in (p, lw, lo))
            a, b = sat_parts((p, lw, lo), there, 0.5 * transmissibility(k, axis))
            water = water + a + lower(a, axis)
            oil = oil + b + lower(b, axis)
        dw, do = slopes(sat[x])
        well = weight[x * ny : (x + 1) * ny] * p
        out[x] = pore[x] * (lw - lo) + dw * (water + well * lw) + do * (oil + well * lo)


def well_kernel(partial, sat, lamw, lamo, cell, well, index, well_rows, out, grad_bhp):
    ny = sat.shape[1]
    groups = well_rows.shape[0]
    wells_each = grad_bhp.shape[1]
    rows = well_rows[...]
    place = well[...] % wells_each
    owners = marks(well[...] // wells_each, groups)
    by_owner = add_thirds(
        dot(jnp.concatenate(split(rows)), marks(place, LANES).astype(jnp.bfloat16), ((1,), (0,)))
    )
    pressure = jnp.sum(by_owner * owners, axis=0, keepdims=True)
    cells = cell[...]
    drop = scatter_cells(index[...] * pressure, marks(cells // LANES, 2 * ny), marks(cells % LANES, LANES))
    for x in range(2):
        dw, do = slopes(sat[x])
        out[x] = partial[x] - (dw * lamw[x] + do * lamo[x]) * drop[x * ny : (x + 1) * ny]
    total = -jnp.sum(rows, axis=0, keepdims=True)
    grad_bhp[...] = total[:, wells_each : 2 * wells_each]


def swap(x):
    return pltpu.roll(x, 4, 0)


def sublane():
    return lax.broadcasted_iota(jnp.int32, (TILE, LANES), 0)


def face_kernel(received, _, own, send, well_rows):
    total = received.shape[0]
    groups = total // CHUNK
    low = sublane() < 4

    def body(parity):
        def tile(s, field):
            start = s * CHUNK + field * ROWS - HALO * parity
            inside = min(max(start, 0), total - TILE)
            rows = received[inside : inside + TILE]
            return rows if inside == start else pltpu.roll(rows, (inside - start) % TILE, 0)

        count = 2 * groups
        below = None
        waiting = []
        for x in range(count):
            s = x // 2
            rhs, diag = tile(s, RHS + x % 2), tile(s, DIAG + x % 2)
            if below is not None:
                rhs, diag = rhs - below[0], diag + below[1]
            below = None
            if x % 2 == 0:
                link = tile(s, INNER)
            elif x % 4 == 1:
                link = tile(s, CHIP)
            elif x < count - 1:
                near, far = (
                    (tile(t, LAMW), tile(t, LAMO), *mobilities(tile(t, SAT)), tile(t, PERMX)) for t in (s, s + 1)
                )
                k, kn = near[4], far[4]
                below = face(near[:4], far[:4], k * kn / (k + kn))
                rhs, diag, link = rhs + below[0], diag + below[1], below[1]
            else:
                link = jnp.zeros_like(rhs)
            fields = (rhs, diag, link, tile(s, CY + x % 2), tile(s, CZ + x % 2))
            for f, value in enumerate(fields):
                own[f, x * TILE : (x + 1) * TILE] = value
            waiting += fields
            while len(waiting) >= 2:
                a, b = waiting[:2]
                waiting = waiting[2:]
                at = ((5 * x + 5 - len(waiting)) // 2 - 1) * TILE
                send[at : at + TILE] = jnp.where(low, pltpu.roll(a, TILE - 2, 0), pltpu.roll(b, 2, 0))

    for parity in range(2):
        pl.when(core() == parity)(functools.partial(body, parity))
    for s in range(groups):
        well_rows[s : s + 1] = received[s * CHUNK + WELL_ROW : s * CHUNK + WELL_ROW + 1]


def sweep(targets, weights, inverses, middle):
    count = len(targets)
    half = count // 2
    b = list(targets)
    for j in range(1, half):
        b[j] = b[j] + weights[j - 1] * b[j - 1]
        m = count - 1 - j
        b[m] = b[m] + weights[m + 1] * b[m + 1]
    da, db, c, inverse = middle
    u = [None] * count
    u[half - 1] = (b[half - 1] * db + c * b[half]) * inverse
    u[half] = (b[half] * da + c * b[half - 1]) * inverse
    for j in range(half - 2, -1, -1):
        u[j] = inverses[j] * b[j] + weights[j] * u[j + 1]
        m = count - 1 - j
        u[m] = inverses[m] * b[m] + weights[m] * u[m - 1]
    return u


def sweep_kernel(sweeps, own, other, out):
    count = own.shape[1] // TILE
    half = count // 2
    row = sublane()
    first = core() == 0
    kept = jnp.logical_and(row >= jnp.where(first, 0, HALO), row < jnp.where(first, ROWS, TILE))
    fields = [[], [], [], [], []]
    for i in range(5 * count // 2):
        packed = other[i * TILE : (i + 1) * TILE]
        turned = swap(packed)
        for n, value in ((2 * i, jnp.where(first, turned, packed)), (2 * i + 1, jnp.where(first, packed, turned))):
            x, f = n // 5, n % 5
            fields[f].append(jnp.where(kept, own[f, x * TILE : (x + 1) * TILE], value))
    rhs, diag, link, cy, cz = fields
    weights, inverses = [None] * count, [None] * count
    da, db = diag[0], diag[count - 1]
    for j in range(half - 1):
        m = count - 1 - j
        inverses[j], inverses[m] = 1.0 / da, 1.0 / db
        weights[j], weights[m] = link[j] * inverses[j], link[m - 1] * inverses[m]
        da = diag[j + 1] - link[j] * weights[j]
        db = diag[m - 1] - link[m - 1] * weights[m]
    c = link[half - 1]
    middle = (da, db, c, 1.0 / (da * db - c * c))

    u = sweep(rhs, weights, inverses, middle)
    for _ in range(1, sweeps):
        targets = []
        for x in range(count):
            t = rhs[x] + cy[x] * upper(u[x], 0) + lower(cy[x] * u[x], 0)
            targets.append(t + cz[x] * upper(u[x], 1) + lower(cz[x] * u[x], 1))
        u = sweep(targets, weights, inverses, middle)
    for x in range(count):
        for y in range(2):
            out[y, x : x + 1] = u[x][HALO + y : HALO + y + 1]


def call(kernel, outs, *args, scratch=(), in_hbm=0):
    places = [pltpu.VMEM] * (len(args) - in_hbm) + [pltpu.HBM] * in_hbm
    args = [pltpu.with_memory_space_constraint(v, place) if place == pltpu.HBM else v for v, place in zip(args, places)]
    return pl.pallas_call(
        kernel,
        out_shape=tuple(o if isinstance(o, jax.ShapeDtypeStruct) else jax.ShapeDtypeStruct(o, jnp.float32) for o in outs),
        in_specs=[pl.BlockSpec(memory_space=place) for place in places],
        out_specs=tuple(pl.BlockSpec(memory_space=pltpu.VMEM) for _ in outs),
        scratch_shapes=[pltpu.VMEM(o, jnp.float32) if isinstance(o, tuple) else o for o in scratch],
        compiler_params=pltpu.CompilerParams(vmem_limit_bytes=40 << 20),
    )(*args)


def on_device(
    pressure, saturation, lam_water, lam_oil, perm_x, perm_y, perm_z, pore_volume,
    perf_cell, perf_well, well_index, well_pressure,
):
    groups = lax.axis_size("gx")
    ny = pressure.shape[1]
    wells_each = well_pressure.shape[0]
    fields = (pressure, saturation, lam_water, lam_oil, perm_x, perm_y, perm_z, pore_volume)
    cell, well, index, bhp = (v.reshape(1, -1) for v in (perf_cell, perf_well, well_index, well_pressure))
    given = fields + (cell, well, index, bhp)
    chip_pairs = [(i, i + 1 - 2 * (i % 2)) for i in range(groups)]
    outer_pairs = [(i, i - 1 + 2 * (i % 2)) for i in range(1, groups - 1)]
    box = (2, ny, LANES)

    *loaded, chip_edge = call(
        load_kernel,
        [jax.ShapeDtypeStruct(v.shape, v.dtype) for v in given] + [(5, ny, LANES)],
        *given,
        scratch=[pltpu.SemaphoreType.DMA((len(given) + 5,))],
        in_hbm=len(given),
    )
    press, sat, lamw, lamo, permx, permy, permz, pore, cell, well, index, bhp = loaded
    from_chip = lax.ppermute(chip_edge, "gx", chip_pairs)
    rhs, diag, cy, cz, inner, weight, well_rows = call(
        functools.partial(cell_kernel, groups),
        [box] * 4 + [(ny, LANES), (2 * ny, LANES), (groups, LANES)],
        sat, lamw, lamo, permx, permy, permz, pore, cell, well, index, bhp,
    )
    packed, outer_a, outer_b = call(
        functools.partial(pack_kernel, groups),
        [(groups, CHUNK, LANES), box, box],
        press, sat, lamw, lamo, permx, from_chip, rhs, diag, cy, cz, inner, well_rows,
        scratch=[(FIELDS, ny + 2 * TILE, LANES)],
    )
    received = lax.all_to_all(packed, "gx", split_axis=0, concat_axis=0, tiled=True)
    outside_a = lax.ppermute(outer_a, "gx", outer_pairs)
    outside_b = lax.ppermute(outer_b, "gx", outer_pairs)
    (partial,) = call(
        sat_kernel, [box],
        press, sat, lamw, lamo, permx, permy, permz, pore, weight, from_chip, outside_a, outside_b,
    )

    count = 2 * groups
    own, send, well_rows = call(
        face_kernel,
        [(5, count * TILE, LANES), (5 * count // 2 * TILE, LANES), (groups, LANES)],
        received.reshape(groups * CHUNK, LANES),
        partial,
    )
    other = lax.ppermute(send, "gx", chip_pairs)
    grad_sat, grad_bhp = call(
        well_kernel, [box, (1, wells_each)], partial, sat, lamw, lamo, cell, well, index, well_rows
    )
    (columns,) = call(functools.partial(sweep_kernel, SWEEPS), [(2, count, LANES)], own, other)
    return grad_sat, grad_bhp.reshape(wells_each), jnp.transpose(columns, (0, 2, 1))


def solution(mesh):
    cells = P(("members", "gx"), None, None)
    line = P(("members", "gx"))
    return jax.shard_map(
        on_device,
        mesh=mesh,
        in_specs=(cells,) * 8 + (line,) * 4,
        out_specs=(cells, line, cells),
        check_vma=False,
    )
```

```python
import functools

import jax
import jax.numpy as jnp
from jax import lax
from jax.experimental import pallas as pl
from jax.experimental.pallas import tpu as pltpu
from jax.sharding import PartitionSpec as P

water_viscosity = 0.5
oil_viscosity = 2.0
compressibility = 0.2
SWEEPS = 4

LANES = 128
TILE = 8
HALO = 3
ROWS = 5
RHS, DIAG, CY, CZ, INNER, SAT, LAMW, LAMO, PERMX, CHIP = 0, 2, 4, 6, 8, 9, 10, 11, 12, 13
FIELDS = 14
WELL_ROW = FIELDS * ROWS
CHUNK = WELL_ROW + 2


def mobilities(s):
    return s * s * (1.0 / water_viscosity), (1.0 - s) * (1.0 - s) * (1.0 / oil_viscosity)


def slopes(s):
    return s * (2.0 / water_viscosity), (s - 1.0) * (2.0 / oil_viscosity)


def split(x):
    first = x.astype(jnp.bfloat16)
    rest = x - first.astype(jnp.float32)
    second = rest.astype(jnp.bfloat16)
    third = (rest - second.astype(jnp.float32)).astype(jnp.bfloat16)
    return first, second, third


def dot(a, b, over):
    return lax.dot_general(a, b, (over, ((), ())), preferred_element_type=jnp.float32)


def add_thirds(x):
    n = x.shape[0] // 3
    return x[:n] + x[n : 2 * n] + x[2 * n :]


def marks(index, count):
    return (lax.broadcasted_iota(jnp.int32, (count, index.shape[1]), 0) == index).astype(jnp.float32)


def scatter_cells(values, row_marks, lane_marks):
    left = jnp.concatenate([(row_marks * part.astype(jnp.float32)).astype(jnp.bfloat16) for part in split(values)])
    return add_thirds(dot(left, lane_marks.astype(jnp.bfloat16), ((1,), (1,))))


def core():
    return lax.axis_index("gx") % 2


def upper(x, axis):
    return pltpu.roll(x, x.shape[axis] - 1, axis)


def lower(x, axis):
    return pltpu.roll(x, 1, axis)


def transmissibility(k, axis):
    kn = upper(k, axis)
    at = lax.broadcasted_iota(jnp.int32, k.shape, axis)
    return jnp.where(at < k.shape[axis] - 1, 2.0 * k * kn / (k + kn), 0.0)


def face(here, there, trans):
    lw, lo, mw, mo = here
    lwn, lon, mwn, mon = there
    fw = mw + mwn
    fo = mo + mon
    return trans * (fw * (lw - lwn) + fo * (lo - lon)), trans * (fw + fo)


def load_kernel(*refs):
    sources, loaded, edge, sems = refs[:12], refs[12:24], refs[24], refs[25]
    pairs = [(sources[i].at[1 - core()], edge.at[i]) for i in range(5)] + list(zip(sources, loaded))
    copies = [pltpu.make_async_copy(src, dst, sems.at[i]) for i, (src, dst) in enumerate(pairs)]
    for copy in copies:
        copy.start()
    for copy in copies:
        copy.wait()


def cell_kernel(
    groups, sat, lamw, lamo, permx, permy, permz, pore, cell, well, index, bhp,
    rhs_out, diag_out, cy_out, cz_out, inner_out, weight, well_rows,
):
    ny = sat.shape[1]
    cells = cell[...]
    row_marks = marks(cells // LANES, 2 * ny)
    lane_marks = marks(cells % LANES, LANES)
    perf_weight = scatter_cells(index[...], row_marks, lane_marks)
    weight[...] = perf_weight
    flows, layers, rhs, diag = [], [], [], []
    for x in range(2):
        s, lw, lo = sat[x], lamw[x], lamo[x]
        mw, mo = mobilities(s)
        layers.append((lw, lo, mw, mo))
        flow = mw * lw + mo * lo
        flows.append(flow)
        w = perf_weight[x * ny : (x + 1) * ny]
        rhs.append(flow * w)
        diag.append(compressibility * pore[x] + (mw + mo) * w)
        for k, axis, out in ((permy[x], 0, cy_out), (permz[x], 1, cz_out)):
            there = tuple(upper(f, axis) for f in layers[x])
            g, c = face(layers[x], there, 0.5 * transmissibility(k, axis))
            rhs[x] += g - lower(g, axis)
            diag[x] += c + lower(c, axis)
            out[x] = c
    k, kn = permx[0], permx[1]
    g, c = face(layers[0], layers[1], k * kn / (k + kn))
    inner_out[...] = c
    for x in range(2):
        rhs_out[x] = rhs[x] + (1 - 2 * x) * g
        diag_out[x] = diag[x] + c

    flow_parts = jnp.concatenate(split(jnp.concatenate(flows)))
    row_parts = jnp.concatenate([row_marks.astype(jnp.bfloat16)] * 3)
    by_lane = dot(flow_parts, row_parts, ((0,), (0,)))
    inflow = index[...] * jnp.sum(by_lane * lane_marks, axis=0, keepdims=True)
    wells_each = bhp.shape[1]
    owners = marks(well[...] // wells_each, groups)
    places = marks(well[...] % wells_each + wells_each, LANES)
    well_rows[...] = scatter_cells(inflow, owners, places)
    well_rows[:, :wells_each] = jnp.broadcast_to(bhp[...], (groups, wells_each))


def pack_kernel(
    groups, press, sat, lamw, lamo, permx, from_chip, rhs, diag, cy, cz, inner, well_rows,
    packed, outer_a, outer_b, padded,
):
    ny = sat.shape[1]
    near, far = 1 - core(), core()
    k, kn = permx[near], from_chip[4]
    here = (lamw[near], lamo[near], *mobilities(sat[near]))
    there = (from_chip[2], from_chip[3], *mobilities(from_chip[1]))
    g, c = face(here, there, k * kn / (k + kn))
    for i, ref in enumerate((press, lamw)):
        outer_a[i] = ref[far]
    for i, ref in enumerate((lamo, permx)):
        outer_b[i] = ref[far]

    values = [None] * FIELDS
    for x in range(2):
        touches = near == x
        values[RHS + x] = rhs[x] + jnp.where(touches, g, 0.0)
        values[DIAG + x] = diag[x] + jnp.where(touches, c, 0.0)
        values[CY + x] = cy[x]
        values[CZ + x] = cz[x]
    values[INNER] = inner[...]
    values[SAT], values[LAMW], values[LAMO], values[PERMX] = sat[far], lamw[far], lamo[far], permx[far]
    values[CHIP] = c
    for f, value in enumerate(values):
        edge = jnp.full((TILE, LANES), 1.0 if f in (DIAG, DIAG + 1, PERMX) else 0.0, jnp.float32)
        padded[f, :TILE] = edge
        padded[f, TILE : TILE + ny] = value
        padded[f, TILE + ny :] = edge

    def chip(c, _):
        for parity in range(2):
            d = 2 * c + parity
            start = TILE + 4 * c - HALO + ROWS * parity
            for f in range(FIELDS):
                packed[d, f * ROWS : (f + 1) * ROWS] = padded[f, pl.ds(start, ROWS)]
            packed[d, WELL_ROW : WELL_ROW + 1] = well_rows[pl.ds(d, 1)]
            packed[d, WELL_ROW + 1 :] = jnp.zeros((1, LANES), jnp.float32)
        return 0

    if groups <= 16:
        for c in range(groups // 2):
            chip(c, 0)
    else:
        lax.fori_loop(0, groups // 2, chip, 0)


def sat_parts(here, there, trans):
    p, lw, lo = here
    pn, lwn, lon = there
    t = trans * (p - pn)
    return t * (lw - lwn), t * (lo - lon)


def sat_kernel(press, sat, lamw, lamo, permx, permy, permz, pore, weight, from_chip, outside_a, outside_b, out):
    ny = sat.shape[1]
    first = core() == 0
    layers = [tuple(r[x] for r in (press, lamw, lamo, permx)) for x in range(2)]
    ends = (outside_a[0], outside_a[1], outside_b[0], outside_b[1]), tuple(from_chip[m] for m in (0, 2, 3, 4))
    below = tuple(jnp.where(first, a, b) for a, b in zip(*ends))
    above = tuple(jnp.where(first, b, a) for a, b in zip(*ends))
    chain = (below, *layers, above)
    across = []
    for here, there in zip(chain, chain[1:]):
        k, kn = here[3], there[3]
        across.append(sat_parts(here[:3], there[:3], k * kn / (k + kn)))
    for x in range(2):
        p, lw, lo, _ = layers[x]
        water, oil = (a + b for a, b in zip(across[x], across[x + 1]))
        for k, axis in ((permy[x], 0), (permz[x], 1)):
            there = tuple(upper(f, axis) for f in (p, lw, lo))
            a, b = sat_parts((p, lw, lo), there, 0.5 * transmissibility(k, axis))
            water = water + a + lower(a, axis)
            oil = oil + b + lower(b, axis)
        dw, do = slopes(sat[x])
        well = weight[x * ny : (x + 1) * ny] * p
        out[x] = pore[x] * (lw - lo) + dw * (water + well * lw) + do * (oil + well * lo)


def well_kernel(partial, sat, lamw, lamo, cell, well, index, well_rows, out, grad_bhp):
    ny = sat.shape[1]
    groups = well_rows.shape[0]
    wells_each = grad_bhp.shape[1]
    rows = well_rows[...]
    place = well[...] % wells_each
    owners = marks(well[...] // wells_each, groups)
    by_owner = add_thirds(
        dot(jnp.concatenate(split(rows)), marks(place, LANES).astype(jnp.bfloat16), ((1,), (0,)))
    )
    pressure = jnp.sum(by_owner * owners, axis=0, keepdims=True)
    cells = cell[...]
    drop = scatter_cells(index[...] * pressure, marks(cells // LANES, 2 * ny), marks(cells % LANES, LANES))
    for x in range(2):
        dw, do = slopes(sat[x])
        out[x] = partial[x] - (dw * lamw[x] + do * lamo[x]) * drop[x * ny : (x + 1) * ny]
    total = -jnp.sum(rows, axis=0, keepdims=True)
    grad_bhp[...] = total[:, wells_each : 2 * wells_each]


def swap(x):
    return pltpu.roll(x, 4, 0)


def sublane():
    return lax.broadcasted_iota(jnp.int32, (TILE, LANES), 0)


def face_kernel(received, _, own, send, well_rows):
    total = received.shape[0]
    groups = total // CHUNK
    low = sublane() < 4

    def body(parity):
        def tile(s, field):
            start = s * CHUNK + field * ROWS - HALO * parity
            inside = min(max(start, 0), total - TILE)
            rows = received[inside : inside + TILE]
            return rows if inside == start else pltpu.roll(rows, (inside - start) % TILE, 0)

        count = 2 * groups
        below = None
        waiting = []
        for x in range(count):
            s = x // 2
            rhs, diag = tile(s, RHS + x % 2), tile(s, DIAG + x % 2)
            if below is not None:
                rhs, diag = rhs - below[0], diag + below[1]
            below = None
            if x % 2 == 0:
                link = tile(s, INNER)
            elif x % 4 == 1:
                link = tile(s, CHIP)
            elif x < count - 1:
                near, far = (
                    (tile(t, LAMW), tile(t, LAMO), *mobilities(tile(t, SAT)), tile(t, PERMX)) for t in (s, s + 1)
                )
                k, kn = near[4], far[4]
                below = face(near[:4], far[:4], k * kn / (k + kn))
                rhs, diag, link = rhs + below[0], diag + below[1], below[1]
            else:
                link = jnp.zeros_like(rhs)
            fields = (rhs, diag, link, tile(s, CY + x % 2), tile(s, CZ + x % 2))
            for f, value in enumerate(fields):
                own[f, x * TILE : (x + 1) * TILE] = value
            waiting += fields
            while len(waiting) >= 2:
                a, b = waiting[:2]
                waiting = waiting[2:]
                at = ((5 * x + 5 - len(waiting)) // 2 - 1) * TILE
                send[at : at + TILE] = jnp.where(low, pltpu.roll(a, TILE - 2, 0), pltpu.roll(b, 2, 0))

    for parity in range(2):
        pl.when(core() == parity)(functools.partial(body, parity))
    for s in range(groups):
        well_rows[s : s + 1] = received[s * CHUNK + WELL_ROW : s * CHUNK + WELL_ROW + 1]


def sweep(targets, weights, inverses, middle):
    count = len(targets)
    half = count // 2
    b = list(targets)
    for j in range(1, half):
        b[j] = b[j] + weights[j - 1] * b[j - 1]
        m = count - 1 - j
        b[m] = b[m] + weights[m + 1] * b[m + 1]
    da, db, c, inverse = middle
    u = [None] * count
    u[half - 1] = (b[half - 1] * db + c * b[half]) * inverse
    u[half] = (b[half] * da + c * b[half - 1]) * inverse
    for j in range(half - 2, -1, -1):
        u[j] = inverses[j] * b[j] + weights[j] * u[j + 1]
        m = count - 1 - j
        u[m] = inverses[m] * b[m] + weights[m] * u[m - 1]
    return u


def sweep_kernel(sweeps, own, other, out):
    count = own.shape[1] // TILE
    half = count // 2
    row = sublane()
    first = core() == 0
    kept = jnp.logical_and(row >= jnp.where(first, 0, HALO), row < jnp.where(first, ROWS, TILE))
    fields = [[], [], [], [], []]
    for i in range(5 * count // 2):
        packed = other[i * TILE : (i + 1) * TILE]
        turned = swap(packed)
        for n, value in ((2 * i, jnp.where(first, turned, packed)), (2 * i + 1, jnp.where(first, packed, turned))):
            x, f = n // 5, n % 5
            fields[f].append(jnp.where(kept, own[f, x * TILE : (x + 1) * TILE], value))
    rhs, diag, link, cy, cz = fields
    weights, inverses = [None] * count, [None] * count
    da, db = diag[0], diag[count - 1]
    for j in range(half - 1):
        m = count - 1 - j
        inverses[j], inverses[m] = 1.0 / da, 1.0 / db
        weights[j], weights[m] = link[j] * inverses[j], link[m - 1] * inverses[m]
        da = diag[j + 1] - link[j] * weights[j]
        db = diag[m - 1] - link[m - 1] * weights[m]
    c = link[half - 1]
    middle = (da, db, c, 1.0 / (da * db - c * c))

    u = sweep(rhs, weights, inverses, middle)
    for _ in range(1, sweeps):
        targets = []
        for x in range(count):
            t = rhs[x] + cy[x] * upper(u[x], 0) + lower(cy[x] * u[x], 0)
            targets.append(t + cz[x] * upper(u[x], 1) + lower(cz[x] * u[x], 1))
        u = sweep(targets, weights, inverses, middle)
    for x in range(count):
        for y in range(2):
            out[y, x : x + 1] = u[x][HALO + y : HALO + y + 1]


def call(kernel, outs, *args, scratch=(), in_hbm=0):
    places = [pltpu.VMEM] * (len(args) - in_hbm) + [pltpu.HBM] * in_hbm
    args = [pltpu.with_memory_space_constraint(v, place) if place == pltpu.HBM else v for v, place in zip(args, places)]
    return pl.pallas_call(
        kernel,
        out_shape=tuple(jax.ShapeDtypeStruct(o, jnp.float32) if isinstance(o, tuple) else o for o in outs),
        in_specs=[pl.BlockSpec(memory_space=place) for place in places],
        out_specs=tuple(pl.BlockSpec(memory_space=pltpu.VMEM) for _ in outs),
        scratch_shapes=[pltpu.VMEM(o, jnp.float32) if isinstance(o, tuple) else o for o in scratch],
        compiler_params=pltpu.CompilerParams(vmem_limit_bytes=40 << 20),
    )(*args)


def on_device(
    pressure, saturation, lam_water, lam_oil, perm_x, perm_y, perm_z, pore_volume,
    perf_cell, perf_well, well_index, well_pressure,
):
    groups = lax.axis_size("gx")
    ny = pressure.shape[1]
    wells_each = well_pressure.shape[0]
    fields = (pressure, saturation, lam_water, lam_oil, perm_x, perm_y, perm_z, pore_volume)
    cell, well, index, bhp = (v.reshape(1, -1) for v in (perf_cell, perf_well, well_index, well_pressure))
    given = fields + (cell, well, index, bhp)
    chip_pairs = [(i, i + 1 - 2 * (i % 2)) for i in range(groups)]
    outer_pairs = [(i, i - 1 + 2 * (i % 2)) for i in range(1, groups - 1)]
    box = (2, ny, LANES)

    *loaded, chip_edge = call(
        load_kernel,
        [jax.ShapeDtypeStruct(v.shape, v.dtype) for v in given] + [(5, ny, LANES)],
        *given,
        scratch=[pltpu.SemaphoreType.DMA((len(given) + 5,))],
        in_hbm=len(given),
    )
    press, sat, lamw, lamo, permx, permy, permz, pore, cell, well, index, bhp = loaded
    from_chip = lax.ppermute(chip_edge, "gx", chip_pairs)
    rhs, diag, cy, cz, inner, weight, well_rows = call(
        functools.partial(cell_kernel, groups),
        [box] * 4 + [(ny, LANES), (2 * ny, LANES), (groups, LANES)],
        sat, lamw, lamo, permx, permy, permz, pore, cell, well, index, bhp,
    )
    packed, outer_a, outer_b = call(
        functools.partial(pack_kernel, groups),
        [pltpu.VMEM((groups, CHUNK, LANES), jnp.float32), box, box],
        press, sat, lamw, lamo, permx, from_chip, rhs, diag, cy, cz, inner, well_rows,
        scratch=[(FIELDS, ny + 2 * TILE, LANES)],
    )
    received = lax.all_to_all(packed, "gx", split_axis=0, concat_axis=0, tiled=True)
    outside_a = lax.ppermute(outer_a, "gx", outer_pairs)
    outside_b = lax.ppermute(outer_b, "gx", outer_pairs)
    (partial,) = call(
        sat_kernel, [box],
        press, sat, lamw, lamo, permx, permy, permz, pore, weight, from_chip, outside_a, outside_b,
    )

    count = 2 * groups
    own, send, well_rows = call(
        face_kernel,
        [(5, count * TILE, LANES), (5 * count // 2 * TILE, LANES), (groups, LANES)],
        received.reshape(groups * CHUNK, LANES),
        partial,
    )
    other = lax.ppermute(send, "gx", chip_pairs)
    grad_sat, grad_bhp = call(
        well_kernel, [box, (1, wells_each)], partial, sat, lamw, lamo, cell, well, index, well_rows
    )
    (columns,) = call(functools.partial(sweep_kernel, SWEEPS), [(2, count, LANES)], own, other)
    return grad_sat, grad_bhp.reshape(wells_each), jnp.transpose(columns, (0, 2, 1))


def solution(mesh):
    cells = P(("members", "gx"), None, None)
    line = P(("members", "gx"))
    return jax.shard_map(
        on_device,
        mesh=mesh,
        in_specs=(cells,) * 8 + (line,) * 4,
        out_specs=(cells, line, cells),
        check_vma=False,
    )
```

```python
import functools

import jax
import jax.numpy as jnp
from jax import lax
from jax.experimental import pallas as pl
from jax.experimental.pallas import tpu as pltpu
from jax.sharding import PartitionSpec as P

water_viscosity = 0.5
oil_viscosity = 2.0
compressibility = 0.2
SWEEPS = 4
REDUCTIONS = 2

LANES = 128
TILE = 8
HALO = 3
ROWS = 5
RHS, DIAG, CY, CZ, INNER, SAT, LAMW, LAMO, PERMX, CHIP = 0, 2, 4, 6, 8, 9, 10, 11, 12, 13
FIELDS = 14
WELL_ROW = FIELDS * ROWS
CHUNK = WELL_ROW + 2


def mobilities(s):
    return s * s * (1.0 / water_viscosity), (1.0 - s) * (1.0 - s) * (1.0 / oil_viscosity)


def slopes(s):
    return s * (2.0 / water_viscosity), (s - 1.0) * (2.0 / oil_viscosity)


def split(x):
    first = x.astype(jnp.bfloat16)
    rest = x - first.astype(jnp.float32)
    second = rest.astype(jnp.bfloat16)
    third = (rest - second.astype(jnp.float32)).astype(jnp.bfloat16)
    return first, second, third


def dot(a, b, over):
    return lax.dot_general(a, b, (over, ((), ())), preferred_element_type=jnp.float32)


def add_thirds(x):
    n = x.shape[0] // 3
    return x[:n] + x[n : 2 * n] + x[2 * n :]


def marks(index, count):
    return (lax.broadcasted_iota(jnp.int32, (count, index.shape[1]), 0) == index).astype(jnp.float32)


def scatter_cells(values, row_marks, lane_marks):
    left = jnp.concatenate([(row_marks * part.astype(jnp.float32)).astype(jnp.bfloat16) for part in split(values)])
    return add_thirds(dot(left, lane_marks.astype(jnp.bfloat16), ((1,), (1,))))


def core():
    return lax.axis_index("gx") % 2


def upper(x, axis):
    return pltpu.roll(x, x.shape[axis] - 1, axis)


def lower(x, axis):
    return pltpu.roll(x, 1, axis)


def transmissibility(k, axis):
    kn = upper(k, axis)
    at = lax.broadcasted_iota(jnp.int32, k.shape, axis)
    return jnp.where(at < k.shape[axis] - 1, 2.0 * k * kn / (k + kn), 0.0)


def face(here, there, trans):
    lw, lo, mw, mo = here
    lwn, lon, mwn, mon = there
    fw = mw + mwn
    fo = mo + mon
    return trans * (fw * (lw - lwn) + fo * (lo - lon)), trans * (fw + fo)


def load_kernel(*refs):
    sources, loaded, edge, sems = refs[:12], refs[12:24], refs[24], refs[25]
    pairs = [(sources[i].at[1 - core()], edge.at[i]) for i in range(5)] + list(zip(sources, loaded))
    copies = [pltpu.make_async_copy(src, dst, sems.at[i]) for i, (src, dst) in enumerate(pairs)]
    for copy in copies:
        copy.start()
    for copy in copies:
        copy.wait()


def cell_kernel(
    groups, sat, lamw, lamo, permx, permy, permz, pore, cell, well, index, bhp,
    rhs_out, diag_out, cy_out, cz_out, inner_out, weight, well_rows,
):
    ny = sat.shape[1]
    cells = cell[...]
    row_marks = marks(cells // LANES, 2 * ny)
    lane_marks = marks(cells % LANES, LANES)
    perf_weight = scatter_cells(index[...], row_marks, lane_marks)
    weight[...] = perf_weight
    flows, layers, rhs, diag = [], [], [], []
    for x in range(2):
        s, lw, lo = sat[x], lamw[x], lamo[x]
        mw, mo = mobilities(s)
        layers.append((lw, lo, mw, mo))
        flow = mw * lw + mo * lo
        flows.append(flow)
        w = perf_weight[x * ny : (x + 1) * ny]
        rhs.append(flow * w)
        diag.append(compressibility * pore[x] + (mw + mo) * w)
        for k, axis, out in ((permy[x], 0, cy_out), (permz[x], 1, cz_out)):
            there = tuple(upper(f, axis) for f in layers[x])
            g, c = face(layers[x], there, 0.5 * transmissibility(k, axis))
            rhs[x] += g - lower(g, axis)
            diag[x] += c + lower(c, axis)
            out[x] = c
    k, kn = permx[0], permx[1]
    g, c = face(layers[0], layers[1], k * kn / (k + kn))
    inner_out[...] = c
    for x in range(2):
        rhs_out[x] = rhs[x] + (1 - 2 * x) * g
        diag_out[x] = diag[x] + c

    flow_parts = jnp.concatenate(split(jnp.concatenate(flows)))
    row_parts = jnp.concatenate([row_marks.astype(jnp.bfloat16)] * 3)
    by_lane = dot(flow_parts, row_parts, ((0,), (0,)))
    inflow = index[...] * jnp.sum(by_lane * lane_marks, axis=0, keepdims=True)
    wells_each = bhp.shape[1]
    owners = marks(well[...] // wells_each, groups)
    places = marks(well[...] % wells_each + wells_each, LANES)
    well_rows[...] = scatter_cells(inflow, owners, places)
    well_rows[:, :wells_each] = jnp.broadcast_to(bhp[...], (groups, wells_each))


def pack_kernel(
    groups, press, sat, lamw, lamo, permx, from_chip, rhs, diag, cy, cz, inner, well_rows,
    packed, outer, padded,
):
    ny = sat.shape[1]
    near, far = 1 - core(), core()
    k, kn = permx[near], from_chip[4]
    here = (lamw[near], lamo[near], *mobilities(sat[near]))
    there = (from_chip[2], from_chip[3], *mobilities(from_chip[1]))
    g, c = face(here, there, k * kn / (k + kn))
    for i, ref in enumerate((press, lamw, lamo, permx)):
        outer[i] = ref[far]

    values = [None] * FIELDS
    for x in range(2):
        touches = near == x
        values[RHS + x] = rhs[x] + jnp.where(touches, g, 0.0)
        values[DIAG + x] = diag[x] + jnp.where(touches, c, 0.0)
        values[CY + x] = cy[x]
        values[CZ + x] = cz[x]
    values[INNER] = inner[...]
    values[SAT], values[LAMW], values[LAMO], values[PERMX] = sat[far], lamw[far], lamo[far], permx[far]
    values[CHIP] = c
    for f, value in enumerate(values):
        edge = jnp.full((TILE, LANES), 1.0 if f in (DIAG, DIAG + 1, PERMX) else 0.0, jnp.float32)
        padded[f, :TILE] = edge
        padded[f, TILE : TILE + ny] = value
        padded[f, TILE + ny :] = edge

    def chip(c, _):
        for parity in range(2):
            d = 2 * c + parity
            start = TILE + 4 * c - HALO + ROWS * parity
            for f in range(FIELDS):
                packed[d, f * ROWS : (f + 1) * ROWS] = padded[f, pl.ds(start, ROWS)]
            packed[d, WELL_ROW : WELL_ROW + 1] = well_rows[pl.ds(d, 1)]
            packed[d, WELL_ROW + 1 :] = jnp.zeros((1, LANES), jnp.float32)
        return 0

    if groups <= 16:
        for c in range(groups // 2):
            chip(c, 0)
    else:
        lax.fori_loop(0, groups // 2, chip, 0)


def sat_parts(here, there, trans):
    p, lw, lo = here
    pn, lwn, lon = there
    t = trans * (p - pn)
    return t * (lw - lwn), t * (lo - lon)


def sat_kernel(press, sat, lamw, lamo, permx, permy, permz, pore, weight, from_chip, from_outside, out):
    ny = sat.shape[1]
    first = core() == 0
    layers = [tuple(r[x] for r in (press, lamw, lamo, permx)) for x in range(2)]
    ends = tuple(from_outside[m] for m in range(4)), tuple(from_chip[m] for m in (0, 2, 3, 4))
    below = tuple(jnp.where(first, a, b) for a, b in zip(*ends))
    above = tuple(jnp.where(first, b, a) for a, b in zip(*ends))
    chain = (below, *layers, above)
    across = []
    for here, there in zip(chain, chain[1:]):
        k, kn = here[3], there[3]
        across.append(sat_parts(here[:3], there[:3], k * kn / (k + kn)))
    for x in range(2):
        p, lw, lo, _ = layers[x]
        water, oil = (a + b for a, b in zip(across[x], across[x + 1]))
        for k, axis in ((permy[x], 0), (permz[x], 1)):
            there = tuple(upper(f, axis) for f in (p, lw, lo))
            a, b = sat_parts((p, lw, lo), there, 0.5 * transmissibility(k, axis))
            water = water + a + lower(a, axis)
            oil = oil + b + lower(b, axis)
        dw, do = slopes(sat[x])
        well = weight[x * ny : (x + 1) * ny] * p
        out[x] = pore[x] * (lw - lo) + dw * (water + well * lw) + do * (oil + well * lo)


def well_kernel(partial, sat, lamw, lamo, cell, well, index, well_rows, out, grad_bhp):
    ny = sat.shape[1]
    groups = well_rows.shape[0]
    wells_each = grad_bhp.shape[1]
    rows = well_rows[...]
    place = well[...] % wells_each
    owners = marks(well[...] // wells_each, groups)
    by_owner = add_thirds(
        dot(jnp.concatenate(split(rows)), marks(place, LANES).astype(jnp.bfloat16), ((1,), (0,)))
    )
    pressure = jnp.sum(by_owner * owners, axis=0, keepdims=True)
    cells = cell[...]
    drop = scatter_cells(index[...] * pressure, marks(cells // LANES, 2 * ny), marks(cells % LANES, LANES))
    for x in range(2):
        dw, do = slopes(sat[x])
        out[x] = partial[x] - (dw * lamw[x] + do * lamo[x]) * drop[x * ny : (x + 1) * ny]
    total = -jnp.sum(rows, axis=0, keepdims=True)
    grad_bhp[...] = total[:, wells_each : 2 * wells_each]


def swap(x):
    return pltpu.roll(x, 4, 0)


def sublane():
    return lax.broadcasted_iota(jnp.int32, (TILE, LANES), 0)


def face_kernel(received, _, own, send, well_rows):
    total = received.shape[0]
    groups = total // CHUNK
    low = sublane() < 4

    def body(parity):
        def tile(s, field):
            start = s * CHUNK + field * ROWS - HALO * parity
            inside = min(max(start, 0), total - TILE)
            rows = received[inside : inside + TILE]
            return rows if inside == start else pltpu.roll(rows, (inside - start) % TILE, 0)

        count = 2 * groups
        below = None
        waiting = []
        for x in range(count):
            s = x // 2
            rhs, diag = tile(s, RHS + x % 2), tile(s, DIAG + x % 2)
            if below is not None:
                rhs, diag = rhs - below[0], diag + below[1]
            below = None
            if x % 2 == 0:
                link = tile(s, INNER)
            elif x % 4 == 1:
                link = tile(s, CHIP)
            elif x < count - 1:
                near, far = (
                    (tile(t, LAMW), tile(t, LAMO), *mobilities(tile(t, SAT)), tile(t, PERMX)) for t in (s, s + 1)
                )
                k, kn = near[4], far[4]
                below = face(near[:4], far[:4], k * kn / (k + kn))
                rhs, diag, link = rhs + below[0], diag + below[1], below[1]
            else:
                link = jnp.zeros_like(rhs)
            fields = (rhs, diag, link, tile(s, CY + x % 2), tile(s, CZ + x % 2))
            for f, value in enumerate(fields):
                own[f, x * TILE : (x + 1) * TILE] = value
            waiting += fields
            while len(waiting) >= 2:
                a, b = waiting[:2]
                waiting = waiting[2:]
                at = ((5 * x + 5 - len(waiting)) // 2 - 1) * TILE
                send[at : at + TILE] = jnp.where(low, pltpu.roll(a, TILE - 2, 0), pltpu.roll(b, 2, 0))

    for parity in range(2):
        pl.when(core() == parity)(functools.partial(body, parity))
    for s in range(groups):
        well_rows[s : s + 1] = received[s * CHUNK + WELL_ROW : s * CHUNK + WELL_ROW + 1]


def solver(diag, link, levels):
    count = len(diag)
    if levels:
        inverse = {j: 1.0 / diag[j] for j in range(1, count, 2)}
        left = {j: link[j - 1] * inverse[j] for j in inverse}
        right = {j: link[j] * inverse[j] for j in inverse if j < count - 1}
        kept_diag, kept_link = [], []
        for i in range(0, count, 2):
            d = diag[i] - link[i] * left[i + 1]
            kept_diag.append(d - link[i - 1] * right[i - 1] if i else d)
            if i < count - 2:
                kept_link.append(link[i] * right[i + 1])
        inner = solver(kept_diag, kept_link, levels - 1)

        def solve(b):
            reduced = []
            for i in range(0, count, 2):
                t = b[i] + left[i + 1] * b[i + 1]
                reduced.append(t + right[i - 1] * b[i - 1] if i else t)
            u = [None] * count
            u[::2] = inner(reduced)
            for j in inverse:
                t = inverse[j] * b[j] + left[j] * u[j - 1]
                u[j] = t + right[j] * u[j + 1] if j < count - 1 else t
            return u

        return solve

    half = count // 2
    weights, inverses = [None] * count, [None] * count
    da, db = diag[0], diag[count - 1]
    for j in range(half - 1):
        m = count - 1 - j
        inverses[j], inverses[m] = 1.0 / da, 1.0 / db
        weights[j], weights[m] = link[j] * inverses[j], link[m - 1] * inverses[m]
        da = diag[j + 1] - link[j] * weights[j]
        db = diag[m - 1] - link[m - 1] * weights[m]
    c = link[half - 1]
    inverse = 1.0 / (da * db - c * c)

    def solve(b):
        b = list(b)
        for j in range(1, half):
            b[j] = b[j] + weights[j - 1] * b[j - 1]
            m = count - 1 - j
            b[m] = b[m] + weights[m + 1] * b[m + 1]
        u = [None] * count
        u[half - 1] = (b[half - 1] * db + c * b[half]) * inverse
        u[half] = (b[half] * da + c * b[half - 1]) * inverse
        for j in range(half - 2, -1, -1):
            u[j] = inverses[j] * b[j] + weights[j] * u[j + 1]
            m = count - 1 - j
            u[m] = inverses[m] * b[m] + weights[m] * u[m - 1]
        return u

    return solve


def sweep_kernel(sweeps, own, other, out):
    count = own.shape[1] // TILE
    row = sublane()
    first = core() == 0
    kept = jnp.logical_and(row >= jnp.where(first, 0, HALO), row < jnp.where(first, ROWS, TILE))
    fields = [[], [], [], [], []]
    for i in range(5 * count // 2):
        packed = other[i * TILE : (i + 1) * TILE]
        turned = swap(packed)
        for n, value in ((2 * i, jnp.where(first, turned, packed)), (2 * i + 1, jnp.where(first, packed, turned))):
            x, f = n // 5, n % 5
            fields[f].append(jnp.where(kept, own[f, x * TILE : (x + 1) * TILE], value))
    rhs, diag, link, cy, cz = fields
    solve = solver(diag, link, REDUCTIONS)
    u = solve(rhs)
    for _ in range(1, sweeps):
        targets = []
        for x in range(count):
            t = rhs[x] + cy[x] * upper(u[x], 0) + lower(cy[x] * u[x], 0)
            targets.append(t + cz[x] * upper(u[x], 1) + lower(cz[x] * u[x], 1))
        u = solve(targets)
    for x in range(count):
        for y in range(2):
            out[y, x : x + 1] = u[x][HALO + y : HALO + y + 1]


def call(kernel, outs, *args, scratch=(), in_hbm=0):
    places = [pltpu.VMEM] * (len(args) - in_hbm) + [pltpu.HBM] * in_hbm
    args = [pltpu.with_memory_space_constraint(v, place) if place == pltpu.HBM else v for v, place in zip(args, places)]
    return pl.pallas_call(
        kernel,
        out_shape=tuple(o if isinstance(o, jax.ShapeDtypeStruct) else jax.ShapeDtypeStruct(o, jnp.float32) for o in outs),
        in_specs=[pl.BlockSpec(memory_space=place) for place in places],
        out_specs=tuple(pl.BlockSpec(memory_space=pltpu.VMEM) for _ in outs),
        scratch_shapes=[pltpu.VMEM(o, jnp.float32) if isinstance(o, tuple) else o for o in scratch],
        compiler_params=pltpu.CompilerParams(vmem_limit_bytes=40 << 20),
    )(*args)


def on_device(
    pressure, saturation, lam_water, lam_oil, perm_x, perm_y, perm_z, pore_volume,
    perf_cell, perf_well, well_index, well_pressure,
):
    groups = lax.axis_size("gx")
    ny = pressure.shape[1]
    wells_each = well_pressure.shape[0]
    fields = (pressure, saturation, lam_water, lam_oil, perm_x, perm_y, perm_z, pore_volume)
    cell, well, index, bhp = (v.reshape(1, -1) for v in (perf_cell, perf_well, well_index, well_pressure))
    given = fields + (cell, well, index, bhp)
    chip_pairs = [(i, i + 1 - 2 * (i % 2)) for i in range(groups)]
    outer_pairs = [(i, i - 1 + 2 * (i % 2)) for i in range(1, groups - 1)]
    box = (2, ny, LANES)

    *loaded, chip_edge = call(
        load_kernel,
        [jax.ShapeDtypeStruct(v.shape, v.dtype) for v in given] + [(5, ny, LANES)],
        *given,
        scratch=[pltpu.SemaphoreType.DMA((len(given) + 5,))],
        in_hbm=len(given),
    )
    press, sat, lamw, lamo, permx, permy, permz, pore, cell, well, index, bhp = loaded
    from_chip = lax.ppermute(chip_edge, "gx", chip_pairs)
    rhs, diag, cy, cz, inner, weight, well_rows = call(
        functools.partial(cell_kernel, groups),
        [box] * 4 + [(ny, LANES), (2 * ny, LANES), (groups, LANES)],
        sat, lamw, lamo, permx, permy, permz, pore, cell, well, index, bhp,
    )
    packed, outer = call(
        functools.partial(pack_kernel, groups),
        [(groups, CHUNK, LANES), (4, ny, LANES)],
        press, sat, lamw, lamo, permx, from_chip, rhs, diag, cy, cz, inner, well_rows,
        scratch=[(FIELDS, ny + 2 * TILE, LANES)],
    )
    received = lax.all_to_all(packed, "gx", split_axis=0, concat_axis=0, tiled=True)
    from_outside = lax.ppermute(outer, "gx", outer_pairs)
    (partial,) = call(
        sat_kernel, [box],
        press, sat, lamw, lamo, permx, permy, permz, pore, weight, from_chip, from_outside,
    )

    count = 2 * groups
    own, send, well_rows = call(
        face_kernel,
        [(5, count * TILE, LANES), (5 * count // 2 * TILE, LANES), (groups, LANES)],
        received.reshape(groups * CHUNK, LANES),
        partial,
    )
    other = lax.ppermute(send, "gx", chip_pairs)
    grad_sat, grad_bhp = call(
        well_kernel, [box, (1, wells_each)], partial, sat, lamw, lamo, cell, well, index, well_rows
    )
    (columns,) = call(functools.partial(sweep_kernel, SWEEPS), [(2, count, LANES)], own, other)
    return grad_sat, grad_bhp.reshape(wells_each), jnp.transpose(columns, (0, 2, 1))


def solution(mesh):
    cells = P(("members", "gx"), None, None)
    line = P(("members", "gx"))
    return jax.shard_map(
        on_device,
        mesh=mesh,
        in_specs=(cells,) * 8 + (line,) * 4,
        out_specs=(cells, line, cells),
        check_vma=False,
    )
```

```python
import functools

import jax
import jax.numpy as jnp
from jax import lax
from jax.experimental import pallas as pl
from jax.experimental.pallas import tpu as pltpu
from jax.sharding import PartitionSpec as P

water_viscosity = 0.5
oil_viscosity = 2.0
compressibility = 0.2
SWEEPS = 4
REDUCTIONS = 2

LANES = 128
TILE = 8
HALO = 3
ROWS = 5
NEAR_RHS, NEAR_DIAG, CHIP, WELL_ROW = 0, 5, 10, 15
REST = 16
FAR_RHS, FAR_DIAG, CY, CZ, INNER, SAT, LAMW, LAMO, PERMX = (REST + ROWS * i for i in (0, 1, 2, 4, 6, 7, 8, 9, 10))
CHUNK = REST + 11 * ROWS + 1


def mobilities(s):
    return s * s * (1.0 / water_viscosity), (1.0 - s) * (1.0 - s) * (1.0 / oil_viscosity)


def slopes(s):
    return s * (2.0 / water_viscosity), (s - 1.0) * (2.0 / oil_viscosity)


def split(x):
    first = x.astype(jnp.bfloat16)
    rest = x - first.astype(jnp.float32)
    second = rest.astype(jnp.bfloat16)
    third = (rest - second.astype(jnp.float32)).astype(jnp.bfloat16)
    return first, second, third


def dot(a, b, over):
    return lax.dot_general(a, b, (over, ((), ())), preferred_element_type=jnp.float32)


def add_thirds(x):
    n = x.shape[0] // 3
    return x[:n] + x[n : 2 * n] + x[2 * n :]


def marks(index, count):
    return (lax.broadcasted_iota(jnp.int32, (count, index.shape[1]), 0) == index).astype(jnp.float32)


def scatter_cells(values, row_marks, lane_marks):
    left = jnp.concatenate([(row_marks * part.astype(jnp.float32)).astype(jnp.bfloat16) for part in split(values)])
    return add_thirds(dot(left, lane_marks.astype(jnp.bfloat16), ((1,), (1,))))


def core():
    return lax.axis_index("gx") % 2


def upper(x, axis):
    return pltpu.roll(x, x.shape[axis] - 1, axis)


def lower(x, axis):
    return pltpu.roll(x, 1, axis)


def transmissibility(k, axis):
    kn = upper(k, axis)
    at = lax.broadcasted_iota(jnp.int32, k.shape, axis)
    return jnp.where(at < k.shape[axis] - 1, 2.0 * k * kn / (k + kn), 0.0)


def face(here, there, trans):
    lw, lo, mw, mo = here
    lwn, lon, mwn, mon = there
    fw = mw + mwn
    fo = mo + mon
    return trans * (fw * (lw - lwn) + fo * (lo - lon)), trans * (fw + fo)


def load_kernel(*refs):
    sources, loaded, edge, sems = refs[:12], refs[12:24], refs[24], refs[25]
    pairs = [(sources[i].at[1 - core()], edge.at[i]) for i in range(5)] + list(zip(sources, loaded))
    copies = [pltpu.make_async_copy(src, dst, sems.at[i]) for i, (src, dst) in enumerate(pairs)]
    for copy in copies:
        copy.start()
    for copy in copies:
        copy.wait()


def pad(ref, value, outside):
    ny = value.shape[0]
    edge = jnp.full((TILE, LANES), outside, jnp.float32)
    ref[:TILE] = edge
    ref[TILE : TILE + ny] = value
    ref[TILE + ny :] = edge


def for_chunks(groups, store):
    def chip(c, _):
        for parity in range(2):
            store(2 * c + parity, TILE + 4 * c - HALO + ROWS * parity)
        return 0

    if groups <= 16:
        for c in range(groups // 2):
            chip(c, 0)
    else:
        lax.fori_loop(0, groups // 2, chip, 0)


def cell_kernel(
    groups, press, sat, lamw, lamo, permx, permy, permz, pore, cell, well, index, bhp,
    near_rhs, near_diag, outer, weight, well_rows, packed, padded, chunks, sem,
):
    ny = sat.shape[1]
    far = core()
    first = far == 0
    cells = cell[...]
    row_marks = marks(cells // LANES, 2 * ny)
    lane_marks = marks(cells % LANES, LANES)
    perf_weight = scatter_cells(index[...], row_marks, lane_marks)
    weight[...] = perf_weight
    flows, layers, rhs, diag, couplings = [], [], [], [], [[], []]
    for x in range(2):
        s, lw, lo = sat[x], lamw[x], lamo[x]
        mw, mo = mobilities(s)
        layers.append((lw, lo, mw, mo))
        flow = mw * lw + mo * lo
        flows.append(flow)
        w = perf_weight[x * ny : (x + 1) * ny]
        rhs.append(flow * w)
        diag.append(compressibility * pore[x] + (mw + mo) * w)
        for axis, k in enumerate((permy[x], permz[x])):
            there = tuple(upper(f, axis) for f in layers[x])
            g, c = face(layers[x], there, 0.5 * transmissibility(k, axis))
            rhs[x] += g - lower(g, axis)
            diag[x] += c + lower(c, axis)
            couplings[axis].append(c)
    k, kn = permx[0], permx[1]
    g, inner = face(layers[0], layers[1], k * kn / (k + kn))
    rhs = rhs[0] + g, rhs[1] - g
    diag = diag[0] + inner, diag[1] + inner
    near_rhs[...] = jnp.where(first, rhs[1], rhs[0])
    near_diag[...] = jnp.where(first, diag[1], diag[0])
    values = [jnp.where(first, rhs[0], rhs[1]), jnp.where(first, diag[0], diag[1]), *couplings[0], *couplings[1], inner]
    values += [sat[far], lamw[far], lamo[far], permx[far]]
    for f, value in enumerate(values):
        pad(padded.at[f], value, 1.0 if REST + f * ROWS in (FAR_DIAG, PERMX) else 0.0)

    def store(d, start):
        for f in range(len(values)):
            chunks[d, f * ROWS : (f + 1) * ROWS] = padded[f, pl.ds(start, ROWS)]
        chunks[d, len(values) * ROWS :] = jnp.zeros((1, LANES), jnp.float32)

    for_chunks(groups, store)
    copy = pltpu.make_async_copy(chunks, packed.at[:, REST:], sem)
    copy.start()

    for i, ref in enumerate((press, lamw, lamo, permx)):
        outer[i] = ref[far]
    flow_parts = jnp.concatenate(split(jnp.concatenate(flows)))
    row_parts = jnp.concatenate([row_marks.astype(jnp.bfloat16)] * 3)
    by_lane = dot(flow_parts, row_parts, ((0,), (0,)))
    inflow = index[...] * jnp.sum(by_lane * lane_marks, axis=0, keepdims=True)
    wells_each = bhp.shape[1]
    owners = marks(well[...] // wells_each, groups)
    places = marks(well[...] % wells_each + wells_each, LANES)
    well_rows[...] = scatter_cells(inflow, owners, places)
    well_rows[:, :wells_each] = jnp.broadcast_to(bhp[...], (groups, wells_each))
    copy.wait()


def pack_kernel(groups, sat, lamw, lamo, permx, from_chip, near_rhs, near_diag, well_rows, _, packed, padded, chunks, sem):
    near = 1 - core()
    k, kn = permx[near], from_chip[4]
    here = (lamw[near], lamo[near], *mobilities(sat[near]))
    there = (from_chip[2], from_chip[3], *mobilities(from_chip[1]))
    g, c = face(here, there, k * kn / (k + kn))
    for i, (value, outside) in enumerate(((near_rhs[...] + g, 0.0), (near_diag[...] + c, 1.0), (c, 0.0))):
        pad(padded.at[i], value, outside)

    def store(d, start):
        for i in range(3):
            chunks[d, i * ROWS : (i + 1) * ROWS] = padded[i, pl.ds(start, ROWS)]
        chunks[d, WELL_ROW : WELL_ROW + 1] = well_rows[pl.ds(d, 1)]

    for_chunks(groups, store)
    copy = pltpu.make_async_copy(chunks, packed.at[:, :REST], sem)
    copy.start()
    copy.wait()


def sat_parts(here, there, trans):
    p, lw, lo = here
    pn, lwn, lon = there
    t = trans * (p - pn)
    return t * (lw - lwn), t * (lo - lon)


def sat_kernel(press, sat, lamw, lamo, permx, permy, permz, pore, weight, from_chip, from_outside, out):
    ny = sat.shape[1]
    first = core() == 0
    layers = [tuple(r[x] for r in (press, lamw, lamo, permx)) for x in range(2)]
    ends = tuple(from_outside[m] for m in range(4)), tuple(from_chip[m] for m in (0, 2, 3, 4))
    below = tuple(jnp.where(first, a, b) for a, b in zip(*ends))
    above = tuple(jnp.where(first, b, a) for a, b in zip(*ends))
    chain = (below, *layers, above)
    across = []
    for here, there in zip(chain, chain[1:]):
        k, kn = here[3], there[3]
        across.append(sat_parts(here[:3], there[:3], k * kn / (k + kn)))
    for x in range(2):
        p, lw, lo, _ = layers[x]
        water, oil = (a + b for a, b in zip(across[x], across[x + 1]))
        for k, axis in ((permy[x], 0), (permz[x], 1)):
            there = tuple(upper(f, axis) for f in (p, lw, lo))
            a, b = sat_parts((p, lw, lo), there, 0.5 * transmissibility(k, axis))
            water = water + a + lower(a, axis)
            oil = oil + b + lower(b, axis)
        dw, do = slopes(sat[x])
        well = weight[x * ny : (x + 1) * ny] * p
        out[x] = pore[x] * (lw - lo) + dw * (water + well * lw) + do * (oil + well * lo)


def well_kernel(partial, sat, lamw, lamo, cell, well, index, well_rows, out, grad_bhp):
    ny = sat.shape[1]
    groups = well_rows.shape[0]
    wells_each = grad_bhp.shape[1]
    rows = well_rows[...]
    place = well[...] % wells_each
    owners = marks(well[...] // wells_each, groups)
    by_owner = add_thirds(
        dot(jnp.concatenate(split(rows)), marks(place, LANES).astype(jnp.bfloat16), ((1,), (0,)))
    )
    pressure = jnp.sum(by_owner * owners, axis=0, keepdims=True)
    cells = cell[...]
    drop = scatter_cells(index[...] * pressure, marks(cells // LANES, 2 * ny), marks(cells % LANES, LANES))
    for x in range(2):
        dw, do = slopes(sat[x])
        out[x] = partial[x] - (dw * lamw[x] + do * lamo[x]) * drop[x * ny : (x + 1) * ny]
    total = -jnp.sum(rows, axis=0, keepdims=True)
    grad_bhp[...] = total[:, wells_each : 2 * wells_each]


def swap(x):
    return pltpu.roll(x, 4, 0)


def sublane():
    return lax.broadcasted_iota(jnp.int32, (TILE, LANES), 0)


def face_kernel(received, _, own, send, well_rows):
    total = received.shape[0]
    groups = total // CHUNK
    low = sublane() < 4

    def body(parity):
        def tile(s, field):
            start = s * CHUNK + field - HALO * parity
            inside = min(max(start, 0), total - TILE)
            rows = received[inside : inside + TILE]
            return rows if inside == start else pltpu.roll(rows, (inside - start) % TILE, 0)

        count = 2 * groups
        below = None
        waiting = []
        for x in range(count):
            s = x // 2
            near = x % 4 in (1, 2)
            rhs, diag = tile(s, NEAR_RHS if near else FAR_RHS), tile(s, NEAR_DIAG if near else FAR_DIAG)
            if below is not None:
                rhs, diag = rhs - below[0], diag + below[1]
            below = None
            if x % 2 == 0:
                link = tile(s, INNER)
            elif x % 4 == 1:
                link = tile(s, CHIP)
            elif x < count - 1:
                here, there = (
                    (tile(t, LAMW), tile(t, LAMO), *mobilities(tile(t, SAT)), tile(t, PERMX)) for t in (s, s + 1)
                )
                k, kn = here[4], there[4]
                below = face(here[:4], there[:4], k * kn / (k + kn))
                rhs, diag, link = rhs + below[0], diag + below[1], below[1]
            else:
                link = jnp.zeros_like(rhs)
            fields = (rhs, diag, link, tile(s, CY + x % 2 * ROWS), tile(s, CZ + x % 2 * ROWS))
            for f, value in enumerate(fields):
                own[f, x * TILE : (x + 1) * TILE] = value
            waiting += fields
            while len(waiting) >= 2:
                a, b = waiting[:2]
                waiting = waiting[2:]
                at = ((5 * x + 5 - len(waiting)) // 2 - 1) * TILE
                send[at : at + TILE] = jnp.where(low, pltpu.roll(a, TILE - 2, 0), pltpu.roll(b, 2, 0))

    for parity in range(2):
        pl.when(core() == parity)(functools.partial(body, parity))
    for s in range(groups):
        well_rows[s : s + 1] = received[s * CHUNK + WELL_ROW : s * CHUNK + WELL_ROW + 1]


def solver(diag, link, levels):
    count = len(diag)
    if levels:
        inverse = {j: 1.0 / diag[j] for j in range(1, count, 2)}
        left = {j: link[j - 1] * inverse[j] for j in inverse}
        right = {j: link[j] * inverse[j] for j in inverse if j < count - 1}
        kept_diag, kept_link = [], []
        for i in range(0, count, 2):
            d = diag[i] - link[i] * left[i + 1]
            kept_diag.append(d - link[i - 1] * right[i - 1] if i else d)
            if i < count - 2:
                kept_link.append(link[i] * right[i + 1])
        inner = solver(kept_diag, kept_link, levels - 1)

        def solve(b):
            reduced = []
            for i in range(0, count, 2):
                t = b[i] + left[i + 1] * b[i + 1]
                reduced.append(t + right[i - 1] * b[i - 1] if i else t)
            u = [None] * count
            u[::2] = inner(reduced)
            for j in inverse:
                t = inverse[j] * b[j] + left[j] * u[j - 1]
                u[j] = t + right[j] * u[j + 1] if j < count - 1 else t
            return u

        return solve

    half = count // 2
    weights, inverses = [None] * count, [None] * count
    da, db = diag[0], diag[count - 1]
    for j in range(half - 1):
        m = count - 1 - j
        inverses[j], inverses[m] = 1.0 / da, 1.0 / db
        weights[j], weights[m] = link[j] * inverses[j], link[m - 1] * inverses[m]
        da = diag[j + 1] - link[j] * weights[j]
        db = diag[m - 1] - link[m - 1] * weights[m]
    c = link[half - 1]
    inverse = 1.0 / (da * db - c * c)

    def solve(b):
        b = list(b)
        for j in range(1, half):
            b[j] = b[j] + weights[j - 1] * b[j - 1]
            m = count - 1 - j
            b[m] = b[m] + weights[m + 1] * b[m + 1]
        u = [None] * count
        u[half - 1] = (b[half - 1] * db + c * b[half]) * inverse
        u[half] = (b[half] * da + c * b[half - 1]) * inverse
        for j in range(half - 2, -1, -1):
            u[j] = inverses[j] * b[j] + weights[j] * u[j + 1]
            m = count - 1 - j
            u[m] = inverses[m] * b[m] + weights[m] * u[m - 1]
        return u

    return solve


def sweep_kernel(sweeps, own, other, out):
    count = own.shape[1] // TILE
    row = sublane()
    first = core() == 0
    kept = jnp.logical_and(row >= jnp.where(first, 0, HALO), row < jnp.where(first, ROWS, TILE))
    fields = [[], [], [], [], []]
    for i in range(5 * count // 2):
        packed = other[i * TILE : (i + 1) * TILE]
        turned = swap(packed)
        for n, value in ((2 * i, jnp.where(first, turned, packed)), (2 * i + 1, jnp.where(first, packed, turned))):
            x, f = n // 5, n % 5
            fields[f].append(jnp.where(kept, own[f, x * TILE : (x + 1) * TILE], value))
    rhs, diag, link, cy, cz = fields
    solve = solver(diag, link, REDUCTIONS)
    u = solve(rhs)
    for _ in range(1, sweeps):
        targets = []
        for x in range(count):
            t = rhs[x] + cy[x] * upper(u[x], 0) + lower(cy[x] * u[x], 0)
            targets.append(t + cz[x] * upper(u[x], 1) + lower(cz[x] * u[x], 1))
        u = solve(targets)
    for x in range(count):
        for y in range(2):
            out[y, x : x + 1] = u[x][HALO + y : HALO + y + 1]


def call(kernel, outs, *args, scratch=(), in_hbm=0, out_hbm=0, aliases=None):
    places = [pltpu.VMEM] * (len(args) - in_hbm) + [pltpu.HBM] * in_hbm
    args = [pltpu.with_memory_space_constraint(v, place) if place == pltpu.HBM else v for v, place in zip(args, places)]
    results = [pltpu.VMEM] * (len(outs) - out_hbm) + [pltpu.HBM] * out_hbm

    def shaped(shape, place):
        return pltpu.HBM(shape, jnp.float32) if place == pltpu.HBM else jax.ShapeDtypeStruct(shape, jnp.float32)

    return pl.pallas_call(
        kernel,
        out_shape=tuple(shaped(o, place) if isinstance(o, tuple) else o for o, place in zip(outs, results)),
        in_specs=[pl.BlockSpec(memory_space=place) for place in places],
        out_specs=tuple(pl.BlockSpec(memory_space=place) for place in results),
        scratch_shapes=[pltpu.VMEM(o, jnp.float32) if isinstance(o, tuple) else o for o in scratch],
        input_output_aliases=aliases or {},
        compiler_params=pltpu.CompilerParams(vmem_limit_bytes=40 << 20),
    )(*args)


def on_device(
    pressure, saturation, lam_water, lam_oil, perm_x, perm_y, perm_z, pore_volume,
    perf_cell, perf_well, well_index, well_pressure,
):
    groups = lax.axis_size("gx")
    ny = pressure.shape[1]
    wells_each = well_pressure.shape[0]
    fields = (pressure, saturation, lam_water, lam_oil, perm_x, perm_y, perm_z, pore_volume)
    cell, well, index, bhp = (v.reshape(1, -1) for v in (perf_cell, perf_well, well_index, well_pressure))
    given = fields + (cell, well, index, bhp)
    chip_pairs = [(i, i + 1 - 2 * (i % 2)) for i in range(groups)]
    outer_pairs = [(i, i - 1 + 2 * (i % 2)) for i in range(1, groups - 1)]
    box = (2, ny, LANES)

    *loaded, chip_edge = call(
        load_kernel,
        [jax.ShapeDtypeStruct(v.shape, v.dtype) for v in given] + [(5, ny, LANES)],
        *given,
        scratch=[pltpu.SemaphoreType.DMA((len(given) + 5,))],
        in_hbm=len(given),
    )
    press, sat, lamw, lamo, permx, permy, permz, pore, cell, well, index, bhp = loaded
    from_chip = lax.ppermute(chip_edge, "gx", chip_pairs)
    plane = (ny, LANES)
    chunk = (groups, CHUNK, LANES)
    near_rhs, near_diag, outer, weight, well_rows, packed = call(
        functools.partial(cell_kernel, groups),
        [plane, plane, (4, ny, LANES), (2 * ny, LANES), (groups, LANES), chunk],
        press, sat, lamw, lamo, permx, permy, permz, pore, cell, well, index, bhp,
        scratch=[(11, ny + 2 * TILE, LANES), (groups, CHUNK - REST, LANES), pltpu.SemaphoreType.DMA],
        out_hbm=1,
    )
    (packed,) = call(
        functools.partial(pack_kernel, groups), [chunk],
        sat, lamw, lamo, permx, from_chip, near_rhs, near_diag, well_rows, packed,
        scratch=[(3, ny + 2 * TILE, LANES), (groups, REST, LANES), pltpu.SemaphoreType.DMA],
        in_hbm=1,
        out_hbm=1,
        aliases={8: 0},
    )
    received = lax.all_to_all(packed, "gx", split_axis=0, concat_axis=0, tiled=True)
    from_outside = lax.ppermute(outer, "gx", outer_pairs)
    (partial,) = call(
        sat_kernel, [box],
        press, sat, lamw, lamo, permx, permy, permz, pore, weight, from_chip, from_outside,
    )

    count = 2 * groups
    own, send, well_rows = call(
        face_kernel,
        [(5, count * TILE, LANES), (5 * count // 2 * TILE, LANES), (groups, LANES)],
        received.reshape(groups * CHUNK, LANES),
        partial,
    )
    other = lax.ppermute(send, "gx", chip_pairs)
    grad_sat, grad_bhp = call(
        well_kernel, [box, (1, wells_each)], partial, sat, lamw, lamo, cell, well, index, well_rows
    )
    (columns,) = call(functools.partial(sweep_kernel, SWEEPS), [(2, count, LANES)], own, other)
    return grad_sat, grad_bhp.reshape(wells_each), jnp.transpose(columns, (0, 2, 1))


def solution(mesh):
    cells = P(("members", "gx"), None, None)
    line = P(("members", "gx"))
    return jax.shard_map(
        on_device,
        mesh=mesh,
        in_specs=(cells,) * 8 + (line,) * 4,
        out_specs=(cells, line, cells),
        check_vma=False,
    )
```

```python
import functools

import jax
import jax.numpy as jnp
from jax import lax
from jax.experimental import pallas as pl
from jax.experimental.pallas import tpu as pltpu
from jax.sharding import PartitionSpec as P

water_viscosity = 0.5
oil_viscosity = 2.0
compressibility = 0.2
SWEEPS = 4
REDUCTIONS = 2

LANES = 128
TILE = 8
HALO = 3
ROWS = 5
NEAR_RHS, NEAR_DIAG, CHIP, WELL_ROW = 0, 5, 10, 15
REST = 16
FAR_RHS, FAR_DIAG, CY, CZ, INNER, SAT, LAMW, LAMO, PERMX = (REST + ROWS * i for i in (0, 1, 2, 4, 6, 7, 8, 9, 10))
CHUNK = REST + 11 * ROWS + 1


def mobilities(s):
    return s * s * (1.0 / water_viscosity), (1.0 - s) * (1.0 - s) * (1.0 / oil_viscosity)


def slopes(s):
    return s * (2.0 / water_viscosity), (s - 1.0) * (2.0 / oil_viscosity)


def split(x):
    first = x.astype(jnp.bfloat16)
    rest = x - first.astype(jnp.float32)
    second = rest.astype(jnp.bfloat16)
    third = (rest - second.astype(jnp.float32)).astype(jnp.bfloat16)
    return first, second, third


def dot(a, b, over):
    return lax.dot_general(a, b, (over, ((), ())), preferred_element_type=jnp.float32)


def add_thirds(x):
    n = x.shape[0] // 3
    return x[:n] + x[n : 2 * n] + x[2 * n :]


def marks(index, count):
    return (lax.broadcasted_iota(jnp.int32, (count, index.shape[1]), 0) == index).astype(jnp.float32)


def scatter_cells(values, row_marks, lane_marks):
    left = jnp.concatenate([(row_marks * part.astype(jnp.float32)).astype(jnp.bfloat16) for part in split(values)])
    return add_thirds(dot(left, lane_marks.astype(jnp.bfloat16), ((1,), (1,))))


def core():
    return lax.axis_index("gx") % 2


def upper(x, axis):
    return pltpu.roll(x, x.shape[axis] - 1, axis)


def lower(x, axis):
    return pltpu.roll(x, 1, axis)


def transmissibility(k, axis):
    kn = upper(k, axis)
    at = lax.broadcasted_iota(jnp.int32, k.shape, axis)
    return jnp.where(at < k.shape[axis] - 1, 2.0 * k * kn / (k + kn), 0.0)


def face(here, there, trans):
    lw, lo, mw, mo = here
    lwn, lon, mwn, mon = there
    fw = mw + mwn
    fo = mo + mon
    return trans * (fw * (lw - lwn) + fo * (lo - lon)), trans * (fw + fo)


def load_kernel(*refs):
    sources, loaded, edge, sems = refs[:12], refs[12:24], refs[24], refs[25]
    pairs = [(sources[i].at[1 - core()], edge.at[i]) for i in range(5)] + list(zip(sources, loaded))
    copies = [pltpu.make_async_copy(src, dst, sems.at[i]) for i, (src, dst) in enumerate(pairs)]
    for copy in copies:
        copy.start()
    for copy in copies:
        copy.wait()


def pad(ref, value, outside):
    ny = value.shape[0]
    edge = jnp.full((TILE, LANES), outside, jnp.float32)
    ref[:TILE] = edge
    ref[TILE : TILE + ny] = value
    ref[TILE + ny :] = edge


def position(device, groups):
    half = groups // 2
    return 2 * (device % half) + device // half


def for_chunks(groups, store):
    def chip(c, _):
        for parity in range(2):
            d = 2 * c + parity
            store(position(d, groups), d, TILE + 4 * c - HALO + ROWS * parity)
        return 0

    if groups <= 16:
        for c in range(groups // 2):
            chip(c, 0)
    else:
        lax.fori_loop(0, groups // 2, chip, 0)


def cell_kernel(
    groups, press, sat, lamw, lamo, permx, permy, permz, pore, cell, well, index, bhp,
    near_rhs, near_diag, outer, weight, well_rows, packed, padded, chunks, sem,
):
    ny = sat.shape[1]
    far = core()
    first = far == 0
    cells = cell[...]
    row_marks = marks(cells // LANES, 2 * ny)
    lane_marks = marks(cells % LANES, LANES)
    perf_weight = scatter_cells(index[...], row_marks, lane_marks)
    weight[...] = perf_weight
    flows, layers, rhs, diag, couplings = [], [], [], [], [[], []]
    for x in range(2):
        s, lw, lo = sat[x], lamw[x], lamo[x]
        mw, mo = mobilities(s)
        layers.append((lw, lo, mw, mo))
        flow = mw * lw + mo * lo
        flows.append(flow)
        w = perf_weight[x * ny : (x + 1) * ny]
        rhs.append(flow * w)
        diag.append(compressibility * pore[x] + (mw + mo) * w)
        for axis, k in enumerate((permy[x], permz[x])):
            there = tuple(upper(f, axis) for f in layers[x])
            g, c = face(layers[x], there, 0.5 * transmissibility(k, axis))
            rhs[x] += g - lower(g, axis)
            diag[x] += c + lower(c, axis)
            couplings[axis].append(c)
    k, kn = permx[0], permx[1]
    g, inner = face(layers[0], layers[1], k * kn / (k + kn))
    rhs = rhs[0] + g, rhs[1] - g
    diag = diag[0] + inner, diag[1] + inner
    near_rhs[...] = jnp.where(first, rhs[1], rhs[0])
    near_diag[...] = jnp.where(first, diag[1], diag[0])
    values = [jnp.where(first, rhs[0], rhs[1]), jnp.where(first, diag[0], diag[1]), *couplings[0], *couplings[1], inner]
    values += [sat[far], lamw[far], lamo[far], permx[far]]
    for f, value in enumerate(values):
        pad(padded.at[f], value, 1.0 if REST + f * ROWS in (FAR_DIAG, PERMX) else 0.0)

    def store(place, _, start):
        for f in range(len(values)):
            chunks[place, f * ROWS : (f + 1) * ROWS] = padded[f, pl.ds(start, ROWS)]
        chunks[place, len(values) * ROWS :] = jnp.zeros((1, LANES), jnp.float32)

    for_chunks(groups, store)
    copy = pltpu.make_async_copy(chunks, packed.at[:, REST:], sem)
    copy.start()

    for i, ref in enumerate((press, lamw, lamo, permx)):
        outer[i] = ref[far]
    flow_parts = jnp.concatenate(split(jnp.concatenate(flows)))
    row_parts = jnp.concatenate([row_marks.astype(jnp.bfloat16)] * 3)
    by_lane = dot(flow_parts, row_parts, ((0,), (0,)))
    inflow = index[...] * jnp.sum(by_lane * lane_marks, axis=0, keepdims=True)
    wells_each = bhp.shape[1]
    owners = marks(well[...] // wells_each, groups)
    places = marks(well[...] % wells_each + wells_each, LANES)
    well_rows[...] = scatter_cells(inflow, owners, places)
    well_rows[:, :wells_each] = jnp.broadcast_to(bhp[...], (groups, wells_each))
    copy.wait()


def pack_kernel(groups, sat, lamw, lamo, permx, from_chip, near_rhs, near_diag, well_rows, _, packed, padded, chunks, sem):
    near = 1 - core()
    k, kn = permx[near], from_chip[4]
    here = (lamw[near], lamo[near], *mobilities(sat[near]))
    there = (from_chip[2], from_chip[3], *mobilities(from_chip[1]))
    g, c = face(here, there, k * kn / (k + kn))
    for i, (value, outside) in enumerate(((near_rhs[...] + g, 0.0), (near_diag[...] + c, 1.0), (c, 0.0))):
        pad(padded.at[i], value, outside)

    def store(place, d, start):
        for i in range(3):
            chunks[place, i * ROWS : (i + 1) * ROWS] = padded[i, pl.ds(start, ROWS)]
        chunks[place, WELL_ROW : WELL_ROW + 1] = well_rows[pl.ds(d, 1)]

    for_chunks(groups, store)
    copy = pltpu.make_async_copy(chunks, packed.at[:, :REST], sem)
    copy.start()
    copy.wait()


def sat_parts(here, there, trans):
    p, lw, lo = here
    pn, lwn, lon = there
    t = trans * (p - pn)
    return t * (lw - lwn), t * (lo - lon)


def sat_kernel(press, sat, lamw, lamo, permx, permy, permz, pore, weight, from_chip, from_outside, out):
    ny = sat.shape[1]
    first = core() == 0
    layers = [tuple(r[x] for r in (press, lamw, lamo, permx)) for x in range(2)]
    ends = tuple(from_outside[m] for m in range(4)), tuple(from_chip[m] for m in (0, 2, 3, 4))
    below = tuple(jnp.where(first, a, b) for a, b in zip(*ends))
    above = tuple(jnp.where(first, b, a) for a, b in zip(*ends))
    chain = (below, *layers, above)
    across = []
    for here, there in zip(chain, chain[1:]):
        k, kn = here[3], there[3]
        across.append(sat_parts(here[:3], there[:3], k * kn / (k + kn)))
    for x in range(2):
        p, lw, lo, _ = layers[x]
        water, oil = (a + b for a, b in zip(across[x], across[x + 1]))
        for k, axis in ((permy[x], 0), (permz[x], 1)):
            there = tuple(upper(f, axis) for f in (p, lw, lo))
            a, b = sat_parts((p, lw, lo), there, 0.5 * transmissibility(k, axis))
            water = water + a + lower(a, axis)
            oil = oil + b + lower(b, axis)
        dw, do = slopes(sat[x])
        well = weight[x * ny : (x + 1) * ny] * p
        out[x] = pore[x] * (lw - lo) + dw * (water + well * lw) + do * (oil + well * lo)


def well_kernel(partial, sat, lamw, lamo, cell, well, index, well_rows, out, grad_bhp):
    ny = sat.shape[1]
    groups = well_rows.shape[0]
    wells_each = grad_bhp.shape[1]
    rows = well_rows[...]
    place = well[...] % wells_each
    owners = marks(well[...] // wells_each, groups)
    by_owner = add_thirds(
        dot(jnp.concatenate(split(rows)), marks(place, LANES).astype(jnp.bfloat16), ((1,), (0,)))
    )
    pressure = jnp.sum(by_owner * owners, axis=0, keepdims=True)
    cells = cell[...]
    drop = scatter_cells(index[...] * pressure, marks(cells // LANES, 2 * ny), marks(cells % LANES, LANES))
    for x in range(2):
        dw, do = slopes(sat[x])
        out[x] = partial[x] - (dw * lamw[x] + do * lamo[x]) * drop[x * ny : (x + 1) * ny]
    total = -jnp.sum(rows, axis=0, keepdims=True)
    grad_bhp[...] = total[:, wells_each : 2 * wells_each]


def swap(x):
    return pltpu.roll(x, 4, 0)


def sublane():
    return lax.broadcasted_iota(jnp.int32, (TILE, LANES), 0)


def face_kernel(received, _, own, send, well_rows):
    total = received.shape[0]
    groups = total // CHUNK
    low = sublane() < 4

    def body(parity):
        def tile(s, field):
            start = position(s, groups) * CHUNK + field - HALO * parity
            inside = min(max(start, 0), total - TILE)
            rows = received[inside : inside + TILE]
            return rows if inside == start else pltpu.roll(rows, (inside - start) % TILE, 0)

        count = 2 * groups
        below = None
        waiting = []
        for x in range(count):
            s = x // 2
            near = x % 4 in (1, 2)
            rhs, diag = tile(s, NEAR_RHS if near else FAR_RHS), tile(s, NEAR_DIAG if near else FAR_DIAG)
            if below is not None:
                rhs, diag = rhs - below[0], diag + below[1]
            below = None
            if x % 2 == 0:
                link = tile(s, INNER)
            elif x % 4 == 1:
                link = tile(s, CHIP)
            elif x < count - 1:
                here, there = (
                    (tile(t, LAMW), tile(t, LAMO), *mobilities(tile(t, SAT)), tile(t, PERMX)) for t in (s, s + 1)
                )
                k, kn = here[4], there[4]
                below = face(here[:4], there[:4], k * kn / (k + kn))
                rhs, diag, link = rhs + below[0], diag + below[1], below[1]
            else:
                link = jnp.zeros_like(rhs)
            fields = (rhs, diag, link, tile(s, CY + x % 2 * ROWS), tile(s, CZ + x % 2 * ROWS))
            for f, value in enumerate(fields):
                own[f, x * TILE : (x + 1) * TILE] = value
            waiting += fields
            while len(waiting) >= 2:
                a, b = waiting[:2]
                waiting = waiting[2:]
                at = ((5 * x + 5 - len(waiting)) // 2 - 1) * TILE
                send[at : at + TILE] = jnp.where(low, pltpu.roll(a, TILE - 2, 0), pltpu.roll(b, 2, 0))

    for parity in range(2):
        pl.when(core() == parity)(functools.partial(body, parity))
    for s in range(groups):
        at = position(s, groups) * CHUNK + WELL_ROW
        well_rows[s : s + 1] = received[at : at + 1]


def solver(diag, link, levels):
    count = len(diag)
    if levels:
        inverse = {j: 1.0 / diag[j] for j in range(1, count, 2)}
        left = {j: link[j - 1] * inverse[j] for j in inverse}
        right = {j: link[j] * inverse[j] for j in inverse if j < count - 1}
        kept_diag, kept_link = [], []
        for i in range(0, count, 2):
            d = diag[i] - link[i] * left[i + 1]
            kept_diag.append(d - link[i - 1] * right[i - 1] if i else d)
            if i < count - 2:
                kept_link.append(link[i] * right[i + 1])
        inner = solver(kept_diag, kept_link, levels - 1)

        def solve(b):
            reduced = []
            for i in range(0, count, 2):
                t = b[i] + left[i + 1] * b[i + 1]
                reduced.append(t + right[i - 1] * b[i - 1] if i else t)
            u = [None] * count
            u[::2] = inner(reduced)
            for j in inverse:
                t = inverse[j] * b[j] + left[j] * u[j - 1]
                u[j] = t + right[j] * u[j + 1] if j < count - 1 else t
            return u

        return solve

    half = count // 2
    weights, inverses = [None] * count, [None] * count
    da, db = diag[0], diag[count - 1]
    for j in range(half - 1):
        m = count - 1 - j
        inverses[j], inverses[m] = 1.0 / da, 1.0 / db
        weights[j], weights[m] = link[j] * inverses[j], link[m - 1] * inverses[m]
        da = diag[j + 1] - link[j] * weights[j]
        db = diag[m - 1] - link[m - 1] * weights[m]
    c = link[half - 1]
    inverse = 1.0 / (da * db - c * c)

    def solve(b):
        b = list(b)
        for j in range(1, half):
            b[j] = b[j] + weights[j - 1] * b[j - 1]
            m = count - 1 - j
            b[m] = b[m] + weights[m + 1] * b[m + 1]
        u = [None] * count
        u[half - 1] = (b[half - 1] * db + c * b[half]) * inverse
        u[half] = (b[half] * da + c * b[half - 1]) * inverse
        for j in range(half - 2, -1, -1):
            u[j] = inverses[j] * b[j] + weights[j] * u[j + 1]
            m = count - 1 - j
            u[m] = inverses[m] * b[m] + weights[m] * u[m - 1]
        return u

    return solve


def sweep_kernel(sweeps, own, other, out):
    count = own.shape[1] // TILE
    row = sublane()
    first = core() == 0
    kept = jnp.logical_and(row >= jnp.where(first, 0, HALO), row < jnp.where(first, ROWS, TILE))
    fields = [[], [], [], [], []]
    for i in range(5 * count // 2):
        packed = other[i * TILE : (i + 1) * TILE]
        turned = swap(packed)
        for n, value in ((2 * i, jnp.where(first, turned, packed)), (2 * i + 1, jnp.where(first, packed, turned))):
            x, f = n // 5, n % 5
            fields[f].append(jnp.where(kept, own[f, x * TILE : (x + 1) * TILE], value))
    rhs, diag, link, cy, cz = fields
    solve = solver(diag, link, REDUCTIONS)
    u = solve(rhs)
    for _ in range(1, sweeps):
        targets = []
        for x in range(count):
            t = rhs[x] + cy[x] * upper(u[x], 0) + lower(cy[x] * u[x], 0)
            targets.append(t + cz[x] * upper(u[x], 1) + lower(cz[x] * u[x], 1))
        u = solve(targets)
    for x in range(count):
        for y in range(2):
            out[y, x : x + 1] = u[x][HALO + y : HALO + y + 1]


def call(kernel, outs, *args, scratch=(), in_hbm=0, out_hbm=0, aliases=None):
    places = [pltpu.VMEM] * (len(args) - in_hbm) + [pltpu.HBM] * in_hbm
    args = [pltpu.with_memory_space_constraint(v, place) if place == pltpu.HBM else v for v, place in zip(args, places)]
    results = [pltpu.VMEM] * (len(outs) - out_hbm) + [pltpu.HBM] * out_hbm

    def shaped(shape, place):
        return pltpu.HBM(shape, jnp.float32) if place == pltpu.HBM else jax.ShapeDtypeStruct(shape, jnp.float32)

    return pl.pallas_call(
        kernel,
        out_shape=tuple(shaped(o, place) if isinstance(o, tuple) else o for o, place in zip(outs, results)),
        in_specs=[pl.BlockSpec(memory_space=place) for place in places],
        out_specs=tuple(pl.BlockSpec(memory_space=place) for place in results),
        scratch_shapes=[pltpu.VMEM(o, jnp.float32) if isinstance(o, tuple) else o for o in scratch],
        input_output_aliases=aliases or {},
        compiler_params=pltpu.CompilerParams(vmem_limit_bytes=40 << 20),
    )(*args)


def on_device(
    pressure, saturation, lam_water, lam_oil, perm_x, perm_y, perm_z, pore_volume,
    perf_cell, perf_well, well_index, well_pressure,
):
    groups = lax.axis_size("gx")
    ny = pressure.shape[1]
    wells_each = well_pressure.shape[0]
    fields = (pressure, saturation, lam_water, lam_oil, perm_x, perm_y, perm_z, pore_volume)
    cell, well, index, bhp = (v.reshape(1, -1) for v in (perf_cell, perf_well, well_index, well_pressure))
    given = fields + (cell, well, index, bhp)
    chip_pairs = [(i, i + 1 - 2 * (i % 2)) for i in range(groups)]
    outer_pairs = [(i, i - 1 + 2 * (i % 2)) for i in range(1, groups - 1)]
    box = (2, ny, LANES)

    *loaded, chip_edge = call(
        load_kernel,
        [jax.ShapeDtypeStruct(v.shape, v.dtype) for v in given] + [(5, ny, LANES)],
        *given,
        scratch=[pltpu.SemaphoreType.DMA((len(given) + 5,))],
        in_hbm=len(given),
    )
    press, sat, lamw, lamo, permx, permy, permz, pore, cell, well, index, bhp = loaded
    from_chip = lax.ppermute(chip_edge, "gx", chip_pairs)
    plane = (ny, LANES)
    chunk = (groups, CHUNK, LANES)
    near_rhs, near_diag, outer, weight, well_rows, packed = call(
        functools.partial(cell_kernel, groups),
        [plane, plane, (4, ny, LANES), (2 * ny, LANES), (groups, LANES), chunk],
        press, sat, lamw, lamo, permx, permy, permz, pore, cell, well, index, bhp,
        scratch=[(11, ny + 2 * TILE, LANES), (groups, CHUNK - REST, LANES), pltpu.SemaphoreType.DMA],
        out_hbm=1,
    )
    (packed,) = call(
        functools.partial(pack_kernel, groups), [chunk],
        sat, lamw, lamo, permx, from_chip, near_rhs, near_diag, well_rows, packed,
        scratch=[(3, ny + 2 * TILE, LANES), (groups, REST, LANES), pltpu.SemaphoreType.DMA],
        in_hbm=1,
        out_hbm=1,
        aliases={8: 0},
    )
    order = sorted(range(groups), key=lambda device: position(device, groups))
    received = lax.all_to_all(packed, "gx", split_axis=0, concat_axis=0, axis_index_groups=[order], tiled=True)
    from_outside = lax.ppermute(outer, "gx", outer_pairs)
    (partial,) = call(
        sat_kernel, [box],
        press, sat, lamw, lamo, permx, permy, permz, pore, weight, from_chip, from_outside,
    )

    count = 2 * groups
    own, send, well_rows = call(
        face_kernel,
        [(5, count * TILE, LANES), (5 * count // 2 * TILE, LANES), (groups, LANES)],
        received.reshape(groups * CHUNK, LANES),
        partial,
    )
    other = lax.ppermute(send, "gx", chip_pairs)
    grad_sat, grad_bhp = call(
        well_kernel, [box, (1, wells_each)], partial, sat, lamw, lamo, cell, well, index, well_rows
    )
    (columns,) = call(functools.partial(sweep_kernel, SWEEPS), [(2, count, LANES)], own, other)
    return grad_sat, grad_bhp.reshape(wells_each), jnp.transpose(columns, (0, 2, 1))


def solution(mesh):
    cells = P(("members", "gx"), None, None)
    line = P(("members", "gx"))
    return jax.shard_map(
        on_device,
        mesh=mesh,
        in_specs=(cells,) * 8 + (line,) * 4,
        out_specs=(cells, line, cells),
        check_vma=False,
    )
```

```python
import functools

import jax
import jax.numpy as jnp
from jax import lax
from jax.experimental import pallas as pl
from jax.experimental.pallas import tpu as pltpu
from jax.sharding import PartitionSpec as P

water_viscosity = 0.5
oil_viscosity = 2.0
compressibility = 0.2
SWEEPS = 4
REDUCTIONS = 2

LANES = 128
TILE = 8
HALO = 3
ROWS = 5
NEAR_RHS, NEAR_DIAG, CHIP, WELL_ROW = 0, 5, 10, 15
REST = 16
FAR_RHS, FAR_DIAG, CY, CZ, INNER, SAT, LAMW, LAMO, PERMX = (REST + ROWS * i for i in (0, 1, 2, 4, 6, 7, 8, 9, 10))
CHUNK = REST + 11 * ROWS + 1


def mobilities(s):
    return s * s * (1.0 / water_viscosity), (1.0 - s) * (1.0 - s) * (1.0 / oil_viscosity)


def slopes(s):
    return s * (2.0 / water_viscosity), (s - 1.0) * (2.0 / oil_viscosity)


def split(x):
    first = x.astype(jnp.bfloat16)
    rest = x - first.astype(jnp.float32)
    second = rest.astype(jnp.bfloat16)
    third = (rest - second.astype(jnp.float32)).astype(jnp.bfloat16)
    return first, second, third


def dot(a, b, over):
    return lax.dot_general(a, b, (over, ((), ())), preferred_element_type=jnp.float32)


def add_thirds(x):
    n = x.shape[0] // 3
    return x[:n] + x[n : 2 * n] + x[2 * n :]


def marks(index, count):
    return (lax.broadcasted_iota(jnp.int32, (count, index.shape[1]), 0) == index).astype(jnp.float32)


def scatter_cells(values, row_marks, lane_marks):
    left = jnp.concatenate([(row_marks * part.astype(jnp.float32)).astype(jnp.bfloat16) for part in split(values)])
    return add_thirds(dot(left, lane_marks.astype(jnp.bfloat16), ((1,), (1,))))


def core():
    return lax.axis_index("gx") % 2


def upper(x, axis):
    return pltpu.roll(x, x.shape[axis] - 1, axis)


def lower(x, axis):
    return pltpu.roll(x, 1, axis)


def transmissibility(k, axis):
    kn = upper(k, axis)
    at = lax.broadcasted_iota(jnp.int32, k.shape, axis)
    return jnp.where(at < k.shape[axis] - 1, 2.0 * k * kn / (k + kn), 0.0)


def face(here, there, trans):
    lw, lo, mw, mo = here
    lwn, lon, mwn, mon = there
    fw = mw + mwn
    fo = mo + mon
    return trans * (fw * (lw - lwn) + fo * (lo - lon)), trans * (fw + fo)


def load_kernel(*refs):
    sources, loaded, edge, sems = refs[:12], refs[12:24], refs[24], refs[25]
    pairs = [(sources[i].at[1 - core()], edge.at[i]) for i in range(5)] + list(zip(sources, loaded))
    copies = [pltpu.make_async_copy(src, dst, sems.at[i]) for i, (src, dst) in enumerate(pairs)]
    for copy in copies:
        copy.start()
    for copy in copies:
        copy.wait()


def pad(ref, value, outside):
    ny = value.shape[0]
    edge = jnp.full((TILE, LANES), outside, jnp.float32)
    ref[:TILE] = edge
    ref[TILE : TILE + ny] = value
    ref[TILE + ny :] = edge


def position(device, groups):
    return groups - 1 - device


def for_chunks(groups, store):
    def chip(c, _):
        for parity in range(2):
            d = 2 * c + parity
            store(position(d, groups), d, TILE + 4 * c - HALO + ROWS * parity)
        return 0

    if groups <= 16:
        for c in range(groups // 2):
            chip(c, 0)
    else:
        lax.fori_loop(0, groups // 2, chip, 0)


def cell_kernel(
    groups, press, sat, lamw, lamo, permx, permy, permz, pore, cell, well, index, bhp,
    near_rhs, near_diag, outer, weight, well_rows, packed, padded, chunks, sem,
):
    ny = sat.shape[1]
    far = core()
    first = far == 0
    cells = cell[...]
    row_marks = marks(cells // LANES, 2 * ny)
    lane_marks = marks(cells % LANES, LANES)
    perf_weight = scatter_cells(index[...], row_marks, lane_marks)
    weight[...] = perf_weight
    flows, layers, rhs, diag, couplings = [], [], [], [], [[], []]
    for x in range(2):
        s, lw, lo = sat[x], lamw[x], lamo[x]
        mw, mo = mobilities(s)
        layers.append((lw, lo, mw, mo))
        flow = mw * lw + mo * lo
        flows.append(flow)
        w = perf_weight[x * ny : (x + 1) * ny]
        rhs.append(flow * w)
        diag.append(compressibility * pore[x] + (mw + mo) * w)
        for axis, k in enumerate((permy[x], permz[x])):
            there = tuple(upper(f, axis) for f in layers[x])
            g, c = face(layers[x], there, 0.5 * transmissibility(k, axis))
            rhs[x] += g - lower(g, axis)
            diag[x] += c + lower(c, axis)
            couplings[axis].append(c)
    k, kn = permx[0], permx[1]
    g, inner = face(layers[0], layers[1], k * kn / (k + kn))
    rhs = rhs[0] + g, rhs[1] - g
    diag = diag[0] + inner, diag[1] + inner
    near_rhs[...] = jnp.where(first, rhs[1], rhs[0])
    near_diag[...] = jnp.where(first, diag[1], diag[0])
    values = [jnp.where(first, rhs[0], rhs[1]), jnp.where(first, diag[0], diag[1]), *couplings[0], *couplings[1], inner]
    values += [sat[far], lamw[far], lamo[far], permx[far]]
    for f, value in enumerate(values):
        pad(padded.at[f], value, 1.0 if REST + f * ROWS in (FAR_DIAG, PERMX) else 0.0)

    def store(place, _, start):
        for f in range(len(values)):
            chunks[place, f * ROWS : (f + 1) * ROWS] = padded[f, pl.ds(start, ROWS)]
        chunks[place, len(values) * ROWS :] = jnp.zeros((1, LANES), jnp.float32)

    for_chunks(groups, store)
    copy = pltpu.make_async_copy(chunks, packed.at[:, REST:], sem)
    copy.start()

    for i, ref in enumerate((press, lamw, lamo, permx)):
        outer[i] = ref[far]
    flow_parts = jnp.concatenate(split(jnp.concatenate(flows)))
    row_parts = jnp.concatenate([row_marks.astype(jnp.bfloat16)] * 3)
    by_lane = dot(flow_parts, row_parts, ((0,), (0,)))
    inflow = index[...] * jnp.sum(by_lane * lane_marks, axis=0, keepdims=True)
    wells_each = bhp.shape[1]
    owners = marks(well[...] // wells_each, groups)
    places = marks(well[...] % wells_each + wells_each, LANES)
    well_rows[...] = scatter_cells(inflow, owners, places)
    well_rows[:, :wells_each] = jnp.broadcast_to(bhp[...], (groups, wells_each))
    copy.wait()


def pack_kernel(groups, sat, lamw, lamo, permx, from_chip, near_rhs, near_diag, well_rows, _, packed, padded, chunks, sem):
    near = 1 - core()
    k, kn = permx[near], from_chip[4]
    here = (lamw[near], lamo[near], *mobilities(sat[near]))
    there = (from_chip[2], from_chip[3], *mobilities(from_chip[1]))
    g, c = face(here, there, k * kn / (k + kn))
    for i, (value, outside) in enumerate(((near_rhs[...] + g, 0.0), (near_diag[...] + c, 1.0), (c, 0.0))):
        pad(padded.at[i], value, outside)

    def store(place, d, start):
        for i in range(3):
            chunks[place, i * ROWS : (i + 1) * ROWS] = padded[i, pl.ds(start, ROWS)]
        chunks[place, WELL_ROW : WELL_ROW + 1] = well_rows[pl.ds(d, 1)]

    for_chunks(groups, store)
    copy = pltpu.make_async_copy(chunks, packed.at[:, :REST], sem)
    copy.start()
    copy.wait()


def sat_parts(here, there, trans):
    p, lw, lo = here
    pn, lwn, lon = there
    t = trans * (p - pn)
    return t * (lw - lwn), t * (lo - lon)


def sat_kernel(press, sat, lamw, lamo, permx, permy, permz, pore, weight, from_chip, from_outside, out):
    ny = sat.shape[1]
    first = core() == 0
    layers = [tuple(r[x] for r in (press, lamw, lamo, permx)) for x in range(2)]
    ends = tuple(from_outside[m] for m in range(4)), tuple(from_chip[m] for m in (0, 2, 3, 4))
    below = tuple(jnp.where(first, a, b) for a, b in zip(*ends))
    above = tuple(jnp.where(first, b, a) for a, b in zip(*ends))
    chain = (below, *layers, above)
    across = []
    for here, there in zip(chain, chain[1:]):
        k, kn = here[3], there[3]
        across.append(sat_parts(here[:3], there[:3], k * kn / (k + kn)))
    for x in range(2):
        p, lw, lo, _ = layers[x]
        water, oil = (a + b for a, b in zip(across[x], across[x + 1]))
        for k, axis in ((permy[x], 0), (permz[x], 1)):
            there = tuple(upper(f, axis) for f in (p, lw, lo))
            a, b = sat_parts((p, lw, lo), there, 0.5 * transmissibility(k, axis))
            water = water + a + lower(a, axis)
            oil = oil + b + lower(b, axis)
        dw, do = slopes(sat[x])
        well = weight[x * ny : (x + 1) * ny] * p
        out[x] = pore[x] * (lw - lo) + dw * (water + well * lw) + do * (oil + well * lo)


def well_kernel(partial, sat, lamw, lamo, cell, well, index, well_rows, out, grad_bhp):
    ny = sat.shape[1]
    groups = well_rows.shape[0]
    wells_each = grad_bhp.shape[1]
    rows = well_rows[...]
    place = well[...] % wells_each
    owners = marks(well[...] // wells_each, groups)
    by_owner = add_thirds(
        dot(jnp.concatenate(split(rows)), marks(place, LANES).astype(jnp.bfloat16), ((1,), (0,)))
    )
    pressure = jnp.sum(by_owner * owners, axis=0, keepdims=True)
    cells = cell[...]
    drop = scatter_cells(index[...] * pressure, marks(cells // LANES, 2 * ny), marks(cells % LANES, LANES))
    for x in range(2):
        dw, do = slopes(sat[x])
        out[x] = partial[x] - (dw * lamw[x] + do * lamo[x]) * drop[x * ny : (x + 1) * ny]
    total = -jnp.sum(rows, axis=0, keepdims=True)
    grad_bhp[...] = total[:, wells_each : 2 * wells_each]


def swap(x):
    return pltpu.roll(x, 4, 0)


def sublane():
    return lax.broadcasted_iota(jnp.int32, (TILE, LANES), 0)


def face_kernel(received, _, own, send, well_rows):
    total = received.shape[0]
    groups = total // CHUNK
    low = sublane() < 4

    def body(parity):
        def tile(s, field):
            start = position(s, groups) * CHUNK + field - HALO * parity
            inside = min(max(start, 0), total - TILE)
            rows = received[inside : inside + TILE]
            return rows if inside == start else pltpu.roll(rows, (inside - start) % TILE, 0)

        count = 2 * groups
        below = None
        waiting = []
        for x in range(count):
            s = x // 2
            near = x % 4 in (1, 2)
            rhs, diag = tile(s, NEAR_RHS if near else FAR_RHS), tile(s, NEAR_DIAG if near else FAR_DIAG)
            if below is not None:
                rhs, diag = rhs - below[0], diag + below[1]
            below = None
            if x % 2 == 0:
                link = tile(s, INNER)
            elif x % 4 == 1:
                link = tile(s, CHIP)
            elif x < count - 1:
                here, there = (
                    (tile(t, LAMW), tile(t, LAMO), *mobilities(tile(t, SAT)), tile(t, PERMX)) for t in (s, s + 1)
                )
                k, kn = here[4], there[4]
                below = face(here[:4], there[:4], k * kn / (k + kn))
                rhs, diag, link = rhs + below[0], diag + below[1], below[1]
            else:
                link = jnp.zeros_like(rhs)
            fields = (rhs, diag, link, tile(s, CY + x % 2 * ROWS), tile(s, CZ + x % 2 * ROWS))
            for f, value in enumerate(fields):
                own[f, x * TILE : (x + 1) * TILE] = value
            waiting += fields
            while len(waiting) >= 2:
                a, b = waiting[:2]
                waiting = waiting[2:]
                at = ((5 * x + 5 - len(waiting)) // 2 - 1) * TILE
                send[at : at + TILE] = jnp.where(low, pltpu.roll(a, TILE - 2, 0), pltpu.roll(b, 2, 0))

    for parity in range(2):
        pl.when(core() == parity)(functools.partial(body, parity))
    for s in range(groups):
        at = position(s, groups) * CHUNK + WELL_ROW
        well_rows[s : s + 1] = received[at : at + 1]


def solver(diag, link, levels):
    count = len(diag)
    if levels:
        inverse = {j: 1.0 / diag[j] for j in range(1, count, 2)}
        left = {j: link[j - 1] * inverse[j] for j in inverse}
        right = {j: link[j] * inverse[j] for j in inverse if j < count - 1}
        kept_diag, kept_link = [], []
        for i in range(0, count, 2):
            d = diag[i] - link[i] * left[i + 1]
            kept_diag.append(d - link[i - 1] * right[i - 1] if i else d)
            if i < count - 2:
                kept_link.append(link[i] * right[i + 1])
        inner = solver(kept_diag, kept_link, levels - 1)

        def solve(b):
            reduced = []
            for i in range(0, count, 2):
                t = b[i] + left[i + 1] * b[i + 1]
                reduced.append(t + right[i - 1] * b[i - 1] if i else t)
            u = [None] * count
            u[::2] = inner(reduced)
            for j in inverse:
                t = inverse[j] * b[j] + left[j] * u[j - 1]
                u[j] = t + right[j] * u[j + 1] if j < count - 1 else t
            return u

        return solve

    half = count // 2
    weights, inverses = [None] * count, [None] * count
    da, db = diag[0], diag[count - 1]
    for j in range(half - 1):
        m = count - 1 - j
        inverses[j], inverses[m] = 1.0 / da, 1.0 / db
        weights[j], weights[m] = link[j] * inverses[j], link[m - 1] * inverses[m]
        da = diag[j + 1] - link[j] * weights[j]
        db = diag[m - 1] - link[m - 1] * weights[m]
    c = link[half - 1]
    inverse = 1.0 / (da * db - c * c)

    def solve(b):
        b = list(b)
        for j in range(1, half):
            b[j] = b[j] + weights[j - 1] * b[j - 1]
            m = count - 1 - j
            b[m] = b[m] + weights[m + 1] * b[m + 1]
        u = [None] * count
        u[half - 1] = (b[half - 1] * db + c * b[half]) * inverse
        u[half] = (b[half] * da + c * b[half - 1]) * inverse
        for j in range(half - 2, -1, -1):
            u[j] = inverses[j] * b[j] + weights[j] * u[j + 1]
            m = count - 1 - j
            u[m] = inverses[m] * b[m] + weights[m] * u[m - 1]
        return u

    return solve


def sweep_kernel(sweeps, own, other, out):
    count = own.shape[1] // TILE
    row = sublane()
    first = core() == 0
    kept = jnp.logical_and(row >= jnp.where(first, 0, HALO), row < jnp.where(first, ROWS, TILE))
    fields = [[], [], [], [], []]
    for i in range(5 * count // 2):
        packed = other[i * TILE : (i + 1) * TILE]
        turned = swap(packed)
        for n, value in ((2 * i, jnp.where(first, turned, packed)), (2 * i + 1, jnp.where(first, packed, turned))):
            x, f = n // 5, n % 5
            fields[f].append(jnp.where(kept, own[f, x * TILE : (x + 1) * TILE], value))
    rhs, diag, link, cy, cz = fields
    solve = solver(diag, link, REDUCTIONS)
    u = solve(rhs)
    for _ in range(1, sweeps):
        targets = []
        for x in range(count):
            t = rhs[x] + cy[x] * upper(u[x], 0) + lower(cy[x] * u[x], 0)
            targets.append(t + cz[x] * upper(u[x], 1) + lower(cz[x] * u[x], 1))
        u = solve(targets)
    for x in range(count):
        for y in range(2):
            out[y, x : x + 1] = u[x][HALO + y : HALO + y + 1]


def call(kernel, outs, *args, scratch=(), in_hbm=0, out_hbm=0, aliases=None):
    places = [pltpu.VMEM] * (len(args) - in_hbm) + [pltpu.HBM] * in_hbm
    args = [pltpu.with_memory_space_constraint(v, place) if place == pltpu.HBM else v for v, place in zip(args, places)]
    results = [pltpu.VMEM] * (len(outs) - out_hbm) + [pltpu.HBM] * out_hbm

    def shaped(shape, place):
        return pltpu.HBM(shape, jnp.float32) if place == pltpu.HBM else jax.ShapeDtypeStruct(shape, jnp.float32)

    return pl.pallas_call(
        kernel,
        out_shape=tuple(shaped(o, place) if isinstance(o, tuple) else o for o, place in zip(outs, results)),
        in_specs=[pl.BlockSpec(memory_space=place) for place in places],
        out_specs=tuple(pl.BlockSpec(memory_space=place) for place in results),
        scratch_shapes=[pltpu.VMEM(o, jnp.float32) if isinstance(o, tuple) else o for o in scratch],
        input_output_aliases=aliases or {},
        compiler_params=pltpu.CompilerParams(vmem_limit_bytes=40 << 20),
    )(*args)


def on_device(
    pressure, saturation, lam_water, lam_oil, perm_x, perm_y, perm_z, pore_volume,
    perf_cell, perf_well, well_index, well_pressure,
):
    groups = lax.axis_size("gx")
    ny = pressure.shape[1]
    wells_each = well_pressure.shape[0]
    fields = (pressure, saturation, lam_water, lam_oil, perm_x, perm_y, perm_z, pore_volume)
    cell, well, index, bhp = (v.reshape(1, -1) for v in (perf_cell, perf_well, well_index, well_pressure))
    given = fields + (cell, well, index, bhp)
    chip_pairs = [(i, i + 1 - 2 * (i % 2)) for i in range(groups)]
    outer_pairs = [(i, i - 1 + 2 * (i % 2)) for i in range(1, groups - 1)]
    box = (2, ny, LANES)

    *loaded, chip_edge = call(
        load_kernel,
        [jax.ShapeDtypeStruct(v.shape, v.dtype) for v in given] + [(5, ny, LANES)],
        *given,
        scratch=[pltpu.SemaphoreType.DMA((len(given) + 5,))],
        in_hbm=len(given),
    )
    press, sat, lamw, lamo, permx, permy, permz, pore, cell, well, index, bhp = loaded
    from_chip = lax.ppermute(chip_edge, "gx", chip_pairs)
    plane = (ny, LANES)
    chunk = (groups, CHUNK, LANES)
    near_rhs, near_diag, outer, weight, well_rows, packed = call(
        functools.partial(cell_kernel, groups),
        [plane, plane, (4, ny, LANES), (2 * ny, LANES), (groups, LANES), chunk],
        press, sat, lamw, lamo, permx, permy, permz, pore, cell, well, index, bhp,
        scratch=[(11, ny + 2 * TILE, LANES), (groups, CHUNK - REST, LANES), pltpu.SemaphoreType.DMA],
        out_hbm=1,
    )
    (packed,) = call(
        functools.partial(pack_kernel, groups), [chunk],
        sat, lamw, lamo, permx, from_chip, near_rhs, near_diag, well_rows, packed,
        scratch=[(3, ny + 2 * TILE, LANES), (groups, REST, LANES), pltpu.SemaphoreType.DMA],
        in_hbm=1,
        out_hbm=1,
        aliases={8: 0},
    )
    order = sorted(range(groups), key=lambda device: position(device, groups))
    received = lax.all_to_all(packed, "gx", split_axis=0, concat_axis=0, axis_index_groups=[order], tiled=True)
    from_outside = lax.ppermute(outer, "gx", outer_pairs)
    (partial,) = call(
        sat_kernel, [box],
        press, sat, lamw, lamo, permx, permy, permz, pore, weight, from_chip, from_outside,
    )

    count = 2 * groups
    own, send, well_rows = call(
        face_kernel,
        [(5, count * TILE, LANES), (5 * count // 2 * TILE, LANES), (groups, LANES)],
        received.reshape(groups * CHUNK, LANES),
        partial,
    )
    other = lax.ppermute(send, "gx", chip_pairs)
    grad_sat, grad_bhp = call(
        well_kernel, [box, (1, wells_each)], partial, sat, lamw, lamo, cell, well, index, well_rows
    )
    (columns,) = call(functools.partial(sweep_kernel, SWEEPS), [(2, count, LANES)], own, other)
    return grad_sat, grad_bhp.reshape(wells_each), jnp.transpose(columns, (0, 2, 1))


def solution(mesh):
    cells = P(("members", "gx"), None, None)
    line = P(("members", "gx"))
    return jax.shard_map(
        on_device,
        mesh=mesh,
        in_specs=(cells,) * 8 + (line,) * 4,
        out_specs=(cells, line, cells),
        check_vma=False,
    )
```

```python
import functools

import jax
import jax.numpy as jnp
from jax import lax
from jax.experimental import pallas as pl
from jax.experimental.pallas import tpu as pltpu
from jax.sharding import PartitionSpec as P

water_viscosity = 0.5
oil_viscosity = 2.0
compressibility = 0.2
SWEEPS = 4
REDUCTIONS = 2

LANES = 128
TILE = 8
HALO = 3
ROWS = 5
NEAR_RHS, NEAR_DIAG, CHIP, WELL_ROW = 0, 5, 10, 15
LATE = 16
FAR_RHS, FAR_DIAG, CY, CZ, INNER, SAT, LAMW, LAMO, PERMX = (ROWS * i for i in (0, 1, 2, 4, 6, 7, 8, 9, 10))
EARLY = 11 * ROWS + 1


def mobilities(s):
    return s * s * (1.0 / water_viscosity), (1.0 - s) * (1.0 - s) * (1.0 / oil_viscosity)


def slopes(s):
    return s * (2.0 / water_viscosity), (s - 1.0) * (2.0 / oil_viscosity)


def split(x):
    first = x.astype(jnp.bfloat16)
    rest = x - first.astype(jnp.float32)
    second = rest.astype(jnp.bfloat16)
    third = (rest - second.astype(jnp.float32)).astype(jnp.bfloat16)
    return first, second, third


def dot(a, b, over):
    return lax.dot_general(a, b, (over, ((), ())), preferred_element_type=jnp.float32)


def add_thirds(x):
    n = x.shape[0] // 3
    return x[:n] + x[n : 2 * n] + x[2 * n :]


def marks(index, count):
    return (lax.broadcasted_iota(jnp.int32, (count, index.shape[1]), 0) == index).astype(jnp.float32)


def scatter_cells(values, row_marks, lane_marks):
    left = jnp.concatenate([(row_marks * part.astype(jnp.float32)).astype(jnp.bfloat16) for part in split(values)])
    return add_thirds(dot(left, lane_marks.astype(jnp.bfloat16), ((1,), (1,))))


def core():
    return lax.axis_index("gx") % 2


def upper(x, axis):
    return pltpu.roll(x, x.shape[axis] - 1, axis)


def lower(x, axis):
    return pltpu.roll(x, 1, axis)


def transmissibility(k, axis):
    kn = upper(k, axis)
    at = lax.broadcasted_iota(jnp.int32, k.shape, axis)
    return jnp.where(at < k.shape[axis] - 1, 2.0 * k * kn / (k + kn), 0.0)


def face(here, there, trans):
    lw, lo, mw, mo = here
    lwn, lon, mwn, mon = there
    fw = mw + mwn
    fo = mo + mon
    return trans * (fw * (lw - lwn) + fo * (lo - lon)), trans * (fw + fo)


def load_kernel(*refs):
    sources, loaded, edge, sems = refs[:12], refs[12:24], refs[24], refs[25]
    pairs = [(sources[i].at[1 - core()], edge.at[i]) for i in range(5)] + list(zip(sources, loaded))
    copies = [pltpu.make_async_copy(src, dst, sems.at[i]) for i, (src, dst) in enumerate(pairs)]
    for copy in copies:
        copy.start()
    for copy in copies:
        copy.wait()


def pad(ref, value, outside):
    ny = value.shape[0]
    edge = jnp.full((TILE, LANES), outside, jnp.float32)
    ref[:TILE] = edge
    ref[TILE : TILE + ny] = value
    ref[TILE + ny :] = edge


def for_chunks(groups, store):
    def chip(c, _):
        for parity in range(2):
            store(2 * c + parity, TILE + 4 * c - HALO + ROWS * parity)
        return 0

    if groups <= 16:
        for c in range(groups // 2):
            chip(c, 0)
    else:
        lax.fori_loop(0, groups // 2, chip, 0)


def cell_kernel(
    groups, press, sat, lamw, lamo, permx, permy, permz, pore, cell, well, index, bhp,
    near_rhs, near_diag, outer, weight, well_rows, packed, padded, chunks, sem,
):
    ny = sat.shape[1]
    far = core()
    first = far == 0
    cells = cell[...]
    row_marks = marks(cells // LANES, 2 * ny)
    lane_marks = marks(cells % LANES, LANES)
    perf_weight = scatter_cells(index[...], row_marks, lane_marks)
    weight[...] = perf_weight
    flows, layers, rhs, diag, couplings = [], [], [], [], [[], []]
    for x in range(2):
        s, lw, lo = sat[x], lamw[x], lamo[x]
        mw, mo = mobilities(s)
        layers.append((lw, lo, mw, mo))
        flow = mw * lw + mo * lo
        flows.append(flow)
        w = perf_weight[x * ny : (x + 1) * ny]
        rhs.append(flow * w)
        diag.append(compressibility * pore[x] + (mw + mo) * w)
        for axis, k in enumerate((permy[x], permz[x])):
            there = tuple(upper(f, axis) for f in layers[x])
            g, c = face(layers[x], there, 0.5 * transmissibility(k, axis))
            rhs[x] += g - lower(g, axis)
            diag[x] += c + lower(c, axis)
            couplings[axis].append(c)
    k, kn = permx[0], permx[1]
    g, inner = face(layers[0], layers[1], k * kn / (k + kn))
    rhs = rhs[0] + g, rhs[1] - g
    diag = diag[0] + inner, diag[1] + inner
    near_rhs[...] = jnp.where(first, rhs[1], rhs[0])
    near_diag[...] = jnp.where(first, diag[1], diag[0])
    values = [jnp.where(first, rhs[0], rhs[1]), jnp.where(first, diag[0], diag[1]), *couplings[0], *couplings[1], inner]
    values += [sat[far], lamw[far], lamo[far], permx[far]]
    for f, value in enumerate(values):
        pad(padded.at[f], value, 1.0 if f * ROWS in (FAR_DIAG, PERMX) else 0.0)

    def store(d, start):
        for f in range(len(values)):
            chunks[d, f * ROWS : (f + 1) * ROWS] = padded[f, pl.ds(start, ROWS)]
        chunks[d, len(values) * ROWS :] = jnp.zeros((1, LANES), jnp.float32)

    for_chunks(groups, store)
    copy = pltpu.make_async_copy(chunks, packed, sem)
    copy.start()

    for i, ref in enumerate((press, lamw, lamo, permx)):
        outer[i] = ref[far]
    flow_parts = jnp.concatenate(split(jnp.concatenate(flows)))
    row_parts = jnp.concatenate([row_marks.astype(jnp.bfloat16)] * 3)
    by_lane = dot(flow_parts, row_parts, ((0,), (0,)))
    inflow = index[...] * jnp.sum(by_lane * lane_marks, axis=0, keepdims=True)
    wells_each = bhp.shape[1]
    owners = marks(well[...] // wells_each, groups)
    places = marks(well[...] % wells_each + wells_each, LANES)
    well_rows[...] = scatter_cells(inflow, owners, places)
    well_rows[:, :wells_each] = jnp.broadcast_to(bhp[...], (groups, wells_each))
    copy.wait()


def pack_kernel(groups, sat, lamw, lamo, permx, from_chip, near_rhs, near_diag, well_rows, packed, padded):
    near = 1 - core()
    k, kn = permx[near], from_chip[4]
    here = (lamw[near], lamo[near], *mobilities(sat[near]))
    there = (from_chip[2], from_chip[3], *mobilities(from_chip[1]))
    g, c = face(here, there, k * kn / (k + kn))
    for i, (value, outside) in enumerate(((near_rhs[...] + g, 0.0), (near_diag[...] + c, 1.0), (c, 0.0))):
        pad(padded.at[i], value, outside)

    def store(d, start):
        for i in range(3):
            packed[d, i * ROWS : (i + 1) * ROWS] = padded[i, pl.ds(start, ROWS)]
        packed[d, WELL_ROW : WELL_ROW + 1] = well_rows[pl.ds(d, 1)]

    for_chunks(groups, store)


def sat_parts(here, there, trans):
    p, lw, lo = here
    pn, lwn, lon = there
    t = trans * (p - pn)
    return t * (lw - lwn), t * (lo - lon)


def sat_kernel(press, sat, lamw, lamo, permx, permy, permz, pore, weight, from_chip, from_outside, out):
    ny = sat.shape[1]
    first = core() == 0
    layers = [tuple(r[x] for r in (press, lamw, lamo, permx)) for x in range(2)]
    ends = tuple(from_outside[m] for m in range(4)), tuple(from_chip[m] for m in (0, 2, 3, 4))
    below = tuple(jnp.where(first, a, b) for a, b in zip(*ends))
    above = tuple(jnp.where(first, b, a) for a, b in zip(*ends))
    chain = (below, *layers, above)
    across = []
    for here, there in zip(chain, chain[1:]):
        k, kn = here[3], there[3]
        across.append(sat_parts(here[:3], there[:3], k * kn / (k + kn)))
    for x in range(2):
        p, lw, lo, _ = layers[x]
        water, oil = (a + b for a, b in zip(across[x], across[x + 1]))
        for k, axis in ((permy[x], 0), (permz[x], 1)):
            there = tuple(upper(f, axis) for f in (p, lw, lo))
            a, b = sat_parts((p, lw, lo), there, 0.5 * transmissibility(k, axis))
            water = water + a + lower(a, axis)
            oil = oil + b + lower(b, axis)
        dw, do = slopes(sat[x])
        well = weight[x * ny : (x + 1) * ny] * p
        out[x] = pore[x] * (lw - lo) + dw * (water + well * lw) + do * (oil + well * lo)


def well_kernel(partial, sat, lamw, lamo, cell, well, index, well_rows, out, grad_bhp):
    ny = sat.shape[1]
    groups = well_rows.shape[0]
    wells_each = grad_bhp.shape[1]
    rows = well_rows[...]
    place = well[...] % wells_each
    owners = marks(well[...] // wells_each, groups)
    by_owner = add_thirds(
        dot(jnp.concatenate(split(rows)), marks(place, LANES).astype(jnp.bfloat16), ((1,), (0,)))
    )
    pressure = jnp.sum(by_owner * owners, axis=0, keepdims=True)
    cells = cell[...]
    drop = scatter_cells(index[...] * pressure, marks(cells // LANES, 2 * ny), marks(cells % LANES, LANES))
    for x in range(2):
        dw, do = slopes(sat[x])
        out[x] = partial[x] - (dw * lamw[x] + do * lamo[x]) * drop[x * ny : (x + 1) * ny]
    total = -jnp.sum(rows, axis=0, keepdims=True)
    grad_bhp[...] = total[:, wells_each : 2 * wells_each]


def swap(x):
    return pltpu.roll(x, 4, 0)


def sublane():
    return lax.broadcasted_iota(jnp.int32, (TILE, LANES), 0)


def face_kernel(early, late, _, own, send, well_rows):
    groups = early.shape[0] // EARLY
    low = sublane() < 4

    def body(parity):
        def tile(s, field, source=early, chunk=EARLY):
            start = s * chunk + field - HALO * parity
            inside = min(max(start, 0), groups * chunk - TILE)
            rows = source[inside : inside + TILE]
            return rows if inside == start else pltpu.roll(rows, (inside - start) % TILE, 0)

        def late_tile(s, field):
            return tile(s, field, late, LATE)

        count = 2 * groups
        below = None
        waiting = []
        for x in range(count):
            s = x // 2
            near = x % 4 in (1, 2)
            rhs = late_tile(s, NEAR_RHS) if near else tile(s, FAR_RHS)
            diag = late_tile(s, NEAR_DIAG) if near else tile(s, FAR_DIAG)
            if below is not None:
                rhs, diag = rhs - below[0], diag + below[1]
            below = None
            if x % 2 == 0:
                link = tile(s, INNER)
            elif x % 4 == 1:
                link = late_tile(s, CHIP)
            elif x < count - 1:
                here, there = (
                    (tile(t, LAMW), tile(t, LAMO), *mobilities(tile(t, SAT)), tile(t, PERMX)) for t in (s, s + 1)
                )
                k, kn = here[4], there[4]
                below = face(here[:4], there[:4], k * kn / (k + kn))
                rhs, diag, link = rhs + below[0], diag + below[1], below[1]
            else:
                link = jnp.zeros_like(rhs)
            fields = (rhs, diag, link, tile(s, CY + x % 2 * ROWS), tile(s, CZ + x % 2 * ROWS))
            for f, value in enumerate(fields):
                own[f, x * TILE : (x + 1) * TILE] = value
            waiting += fields
            while len(waiting) >= 2:
                a, b = waiting[:2]
                waiting = waiting[2:]
                at = ((5 * x + 5 - len(waiting)) // 2 - 1) * TILE
                send[at : at + TILE] = jnp.where(low, pltpu.roll(a, TILE - 2, 0), pltpu.roll(b, 2, 0))

    for parity in range(2):
        pl.when(core() == parity)(functools.partial(body, parity))
    for s in range(groups):
        well_rows[s : s + 1] = late[s * LATE + WELL_ROW : s * LATE + WELL_ROW + 1]


def solver(diag, link, levels):
    count = len(diag)
    if levels:
        inverse = {j: 1.0 / diag[j] for j in range(1, count, 2)}
        left = {j: link[j - 1] * inverse[j] for j in inverse}
        right = {j: link[j] * inverse[j] for j in inverse if j < count - 1}
        kept_diag, kept_link = [], []
        for i in range(0, count, 2):
            d = diag[i] - link[i] * left[i + 1]
            kept_diag.append(d - link[i - 1] * right[i - 1] if i else d)
            if i < count - 2:
                kept_link.append(link[i] * right[i + 1])
        inner = solver(kept_diag, kept_link, levels - 1)

        def solve(b):
            reduced = []
            for i in range(0, count, 2):
                t = b[i] + left[i + 1] * b[i + 1]
                reduced.append(t + right[i - 1] * b[i - 1] if i else t)
            u = [None] * count
            u[::2] = inner(reduced)
            for j in inverse:
                t = inverse[j] * b[j] + left[j] * u[j - 1]
                u[j] = t + right[j] * u[j + 1] if j < count - 1 else t
            return u

        return solve

    half = count // 2
    weights, inverses = [None] * count, [None] * count
    da, db = diag[0], diag[count - 1]
    for j in range(half - 1):
        m = count - 1 - j
        inverses[j], inverses[m] = 1.0 / da, 1.0 / db
        weights[j], weights[m] = link[j] * inverses[j], link[m - 1] * inverses[m]
        da = diag[j + 1] - link[j] * weights[j]
        db = diag[m - 1] - link[m - 1] * weights[m]
    c = link[half - 1]
    inverse = 1.0 / (da * db - c * c)

    def solve(b):
        b = list(b)
        for j in range(1, half):
            b[j] = b[j] + weights[j - 1] * b[j - 1]
            m = count - 1 - j
            b[m] = b[m] + weights[m + 1] * b[m + 1]
        u = [None] * count
        u[half - 1] = (b[half - 1] * db + c * b[half]) * inverse
        u[half] = (b[half] * da + c * b[half - 1]) * inverse
        for j in range(half - 2, -1, -1):
            u[j] = inverses[j] * b[j] + weights[j] * u[j + 1]
            m = count - 1 - j
            u[m] = inverses[m] * b[m] + weights[m] * u[m - 1]
        return u

    return solve


def sweep_kernel(sweeps, own, other, out):
    count = own.shape[1] // TILE
    row = sublane()
    first = core() == 0
    kept = jnp.logical_and(row >= jnp.where(first, 0, HALO), row < jnp.where(first, ROWS, TILE))
    fields = [[], [], [], [], []]
    for i in range(5 * count // 2):
        packed = other[i * TILE : (i + 1) * TILE]
        turned = swap(packed)
        for n, value in ((2 * i, jnp.where(first, turned, packed)), (2 * i + 1, jnp.where(first, packed, turned))):
            x, f = n // 5, n % 5
            fields[f].append(jnp.where(kept, own[f, x * TILE : (x + 1) * TILE], value))
    rhs, diag, link, cy, cz = fields
    solve = solver(diag, link, REDUCTIONS)
    u = solve(rhs)
    for _ in range(1, sweeps):
        targets = []
        for x in range(count):
            t = rhs[x] + cy[x] * upper(u[x], 0) + lower(cy[x] * u[x], 0)
            targets.append(t + cz[x] * upper(u[x], 1) + lower(cz[x] * u[x], 1))
        u = solve(targets)
    for x in range(count):
        for y in range(2):
            out[y, x : x + 1] = u[x][HALO + y : HALO + y + 1]


def call(kernel, outs, *args, scratch=(), in_hbm=0, out_hbm=0):
    places = [pltpu.VMEM] * (len(args) - in_hbm) + [pltpu.HBM] * in_hbm
    args = [pltpu.with_memory_space_constraint(v, place) if place == pltpu.HBM else v for v, place in zip(args, places)]
    results = [pltpu.VMEM] * (len(outs) - out_hbm) + [pltpu.HBM] * out_hbm

    def shaped(shape, place):
        return pltpu.HBM(shape, jnp.float32) if place == pltpu.HBM else jax.ShapeDtypeStruct(shape, jnp.float32)

    return pl.pallas_call(
        kernel,
        out_shape=tuple(shaped(o, place) if isinstance(o, tuple) else o for o, place in zip(outs, results)),
        in_specs=[pl.BlockSpec(memory_space=place) for place in places],
        out_specs=tuple(pl.BlockSpec(memory_space=place) for place in results),
        scratch_shapes=[pltpu.VMEM(o, jnp.float32) if isinstance(o, tuple) else o for o in scratch],
        compiler_params=pltpu.CompilerParams(vmem_limit_bytes=40 << 20),
    )(*args)


def on_device(
    pressure, saturation, lam_water, lam_oil, perm_x, perm_y, perm_z, pore_volume,
    perf_cell, perf_well, well_index, well_pressure,
):
    groups = lax.axis_size("gx")
    ny = pressure.shape[1]
    wells_each = well_pressure.shape[0]
    fields = (pressure, saturation, lam_water, lam_oil, perm_x, perm_y, perm_z, pore_volume)
    cell, well, index, bhp = (v.reshape(1, -1) for v in (perf_cell, perf_well, well_index, well_pressure))
    given = fields + (cell, well, index, bhp)
    chip_pairs = [(i, i + 1 - 2 * (i % 2)) for i in range(groups)]
    outer_pairs = [(i, i - 1 + 2 * (i % 2)) for i in range(1, groups - 1)]
    box = (2, ny, LANES)

    *loaded, chip_edge = call(
        load_kernel,
        [jax.ShapeDtypeStruct(v.shape, v.dtype) for v in given] + [(5, ny, LANES)],
        *given,
        scratch=[pltpu.SemaphoreType.DMA((len(given) + 5,))],
        in_hbm=len(given),
    )
    press, sat, lamw, lamo, permx, permy, permz, pore, cell, well, index, bhp = loaded
    from_chip = lax.ppermute(chip_edge, "gx", chip_pairs)
    plane = (ny, LANES)
    near_rhs, near_diag, outer, weight, well_rows, packed = call(
        functools.partial(cell_kernel, groups),
        [plane, plane, (4, ny, LANES), (2 * ny, LANES), (groups, LANES), (groups, EARLY, LANES)],
        press, sat, lamw, lamo, permx, permy, permz, pore, cell, well, index, bhp,
        scratch=[(11, ny + 2 * TILE, LANES), (groups, EARLY, LANES), pltpu.SemaphoreType.DMA],
        out_hbm=1,
    )
    early = lax.all_to_all(packed, "gx", split_axis=0, concat_axis=0, tiled=True)
    (packed,) = call(
        functools.partial(pack_kernel, groups), [(groups, LATE, LANES)],
        sat, lamw, lamo, permx, from_chip, near_rhs, near_diag, well_rows,
        scratch=[(3, ny + 2 * TILE, LANES)],
    )
    late = lax.all_to_all(packed, "gx", split_axis=0, concat_axis=0, tiled=True)
    from_outside = lax.ppermute(outer, "gx", outer_pairs)
    (partial,) = call(
        sat_kernel, [box],
        press, sat, lamw, lamo, permx, permy, permz, pore, weight, from_chip, from_outside,
    )

    count = 2 * groups
    own, send, well_rows = call(
        face_kernel,
        [(5, count * TILE, LANES), (5 * count // 2 * TILE, LANES), (groups, LANES)],
        early.reshape(groups * EARLY, LANES),
        late.reshape(groups * LATE, LANES),
        partial,
    )
    other = lax.ppermute(send, "gx", chip_pairs)
    grad_sat, grad_bhp = call(
        well_kernel, [box, (1, wells_each)], partial, sat, lamw, lamo, cell, well, index, well_rows
    )
    (columns,) = call(functools.partial(sweep_kernel, SWEEPS), [(2, count, LANES)], own, other)
    return grad_sat, grad_bhp.reshape(wells_each), jnp.transpose(columns, (0, 2, 1))


def solution(mesh):
    cells = P(("members", "gx"), None, None)
    line = P(("members", "gx"))
    return jax.shard_map(
        on_device,
        mesh=mesh,
        in_specs=(cells,) * 8 + (line,) * 4,
        out_specs=(cells, line, cells),
        check_vma=False,
    )
```

```python
import functools

import jax
import jax.numpy as jnp
from jax import lax
from jax.experimental import pallas as pl
from jax.experimental.pallas import tpu as pltpu
from jax.sharding import PartitionSpec as P

water_viscosity = 0.5
oil_viscosity = 2.0
compressibility = 0.2
SWEEPS = 4
REDUCTIONS = 2

LANES = 128
TILE = 8
HALO = 3
ROWS = 5
NEAR_RHS, NEAR_DIAG, CHIP, WELL_ROW = 0, 5, 10, 15
REST = 16
FAR_RHS, FAR_DIAG, CY, CZ, INNER, SAT, LAMW, LAMO, PERMX = (REST + ROWS * i for i in (0, 1, 2, 4, 6, 7, 8, 9, 10))
CHUNK = REST + 11 * ROWS + 1


def mobilities(s):
    return s * s * (1.0 / water_viscosity), (1.0 - s) * (1.0 - s) * (1.0 / oil_viscosity)


def slopes(s):
    return s * (2.0 / water_viscosity), (s - 1.0) * (2.0 / oil_viscosity)


def split(x):
    first = x.astype(jnp.bfloat16)
    rest = x - first.astype(jnp.float32)
    second = rest.astype(jnp.bfloat16)
    third = (rest - second.astype(jnp.float32)).astype(jnp.bfloat16)
    return first, second, third


def dot(a, b, over):
    return lax.dot_general(a, b, (over, ((), ())), preferred_element_type=jnp.float32)


def add_thirds(x):
    n = x.shape[0] // 3
    return x[:n] + x[n : 2 * n] + x[2 * n :]


def marks(index, count):
    return (lax.broadcasted_iota(jnp.int32, (count, index.shape[1]), 0) == index).astype(jnp.float32)


def scatter_cells(values, row_marks, lane_marks):
    left = jnp.concatenate([(row_marks * part.astype(jnp.float32)).astype(jnp.bfloat16) for part in split(values)])
    return add_thirds(dot(left, lane_marks.astype(jnp.bfloat16), ((1,), (1,))))


def core():
    return lax.axis_index("gx") % 2


def upper(x, axis):
    return pltpu.roll(x, x.shape[axis] - 1, axis)


def lower(x, axis):
    return pltpu.roll(x, 1, axis)


def transmissibility(k, axis):
    kn = upper(k, axis)
    at = lax.broadcasted_iota(jnp.int32, k.shape, axis)
    return jnp.where(at < k.shape[axis] - 1, 2.0 * k * kn / (k + kn), 0.0)


def face(here, there, trans):
    lw, lo, mw, mo = here
    lwn, lon, mwn, mon = there
    fw = mw + mwn
    fo = mo + mon
    return trans * (fw * (lw - lwn) + fo * (lo - lon)), trans * (fw + fo)


def load_kernel(*refs):
    sources, loaded, edge, sems = refs[:12], refs[12:24], refs[24], refs[25]
    pairs = [(sources[i].at[1 - core()], edge.at[i]) for i in range(5)] + list(zip(sources, loaded))
    copies = [pltpu.make_async_copy(src, dst, sems.at[i]) for i, (src, dst) in enumerate(pairs)]
    for copy in copies:
        copy.start()
    for copy in copies:
        copy.wait()


def pad(ref, value, outside):
    ny = value.shape[0]
    edge = jnp.full((TILE, LANES), outside, jnp.float32)
    ref[:TILE] = edge
    ref[TILE : TILE + ny] = value
    ref[TILE + ny :] = edge


def position(device, groups):
    return device % 4 * (groups // 4) + device // 4


def for_chunks(groups, store):
    def chip(c, _):
        for parity in range(2):
            d = 2 * c + parity
            store(position(d, groups), d, TILE + 4 * c - HALO + ROWS * parity)
        return 0

    if groups <= 16:
        for c in range(groups // 2):
            chip(c, 0)
    else:
        lax.fori_loop(0, groups // 2, chip, 0)


def cell_kernel(
    groups, press, sat, lamw, lamo, permx, permy, permz, pore, cell, well, index, bhp,
    near_rhs, near_diag, outer, weight, well_rows, packed, padded, chunks, sem,
):
    ny = sat.shape[1]
    far = core()
    first = far == 0
    cells = cell[...]
    row_marks = marks(cells // LANES, 2 * ny)
    lane_marks = marks(cells % LANES, LANES)
    perf_weight = scatter_cells(index[...], row_marks, lane_marks)
    weight[...] = perf_weight
    flows, layers, rhs, diag, couplings = [], [], [], [], [[], []]
    for x in range(2):
        s, lw, lo = sat[x], lamw[x], lamo[x]
        mw, mo = mobilities(s)
        layers.append((lw, lo, mw, mo))
        flow = mw * lw + mo * lo
        flows.append(flow)
        w = perf_weight[x * ny : (x + 1) * ny]
        rhs.append(flow * w)
        diag.append(compressibility * pore[x] + (mw + mo) * w)
        for axis, k in enumerate((permy[x], permz[x])):
            there = tuple(upper(f, axis) for f in layers[x])
            g, c = face(layers[x], there, 0.5 * transmissibility(k, axis))
            rhs[x] += g - lower(g, axis)
            diag[x] += c + lower(c, axis)
            couplings[axis].append(c)
    k, kn = permx[0], permx[1]
    g, inner = face(layers[0], layers[1], k * kn / (k + kn))
    rhs = rhs[0] + g, rhs[1] - g
    diag = diag[0] + inner, diag[1] + inner
    near_rhs[...] = jnp.where(first, rhs[1], rhs[0])
    near_diag[...] = jnp.where(first, diag[1], diag[0])
    values = [jnp.where(first, rhs[0], rhs[1]), jnp.where(first, diag[0], diag[1]), *couplings[0], *couplings[1], inner]
    values += [sat[far], lamw[far], lamo[far], permx[far]]
    for f, value in enumerate(values):
        pad(padded.at[f], value, 1.0 if REST + f * ROWS in (FAR_DIAG, PERMX) else 0.0)

    def store(place, _, start):
        for f in range(len(values)):
            chunks[place, f * ROWS : (f + 1) * ROWS] = padded[f, pl.ds(start, ROWS)]
        chunks[place, len(values) * ROWS :] = jnp.zeros((1, LANES), jnp.float32)

    for_chunks(groups, store)
    copy = pltpu.make_async_copy(chunks, packed.at[:, REST:], sem)
    copy.start()

    for i, ref in enumerate((press, lamw, lamo, permx)):
        outer[i] = ref[far]
    flow_parts = jnp.concatenate(split(jnp.concatenate(flows)))
    row_parts = jnp.concatenate([row_marks.astype(jnp.bfloat16)] * 3)
    by_lane = dot(flow_parts, row_parts, ((0,), (0,)))
    inflow = index[...] * jnp.sum(by_lane * lane_marks, axis=0, keepdims=True)
    wells_each = bhp.shape[1]
    owners = marks(well[...] // wells_each, groups)
    places = marks(well[...] % wells_each + wells_each, LANES)
    well_rows[...] = scatter_cells(inflow, owners, places)
    well_rows[:, :wells_each] = jnp.broadcast_to(bhp[...], (groups, wells_each))
    copy.wait()


def pack_kernel(groups, sat, lamw, lamo, permx, from_chip, near_rhs, near_diag, well_rows, _, packed, padded, chunks, sem):
    near = 1 - core()
    k, kn = permx[near], from_chip[4]
    here = (lamw[near], lamo[near], *mobilities(sat[near]))
    there = (from_chip[2], from_chip[3], *mobilities(from_chip[1]))
    g, c = face(here, there, k * kn / (k + kn))
    for i, (value, outside) in enumerate(((near_rhs[...] + g, 0.0), (near_diag[...] + c, 1.0), (c, 0.0))):
        pad(padded.at[i], value, outside)

    def store(place, d, start):
        for i in range(3):
            chunks[place, i * ROWS : (i + 1) * ROWS] = padded[i, pl.ds(start, ROWS)]
        chunks[place, WELL_ROW : WELL_ROW + 1] = well_rows[pl.ds(d, 1)]

    for_chunks(groups, store)
    copy = pltpu.make_async_copy(chunks, packed.at[:, :REST], sem)
    copy.start()
    copy.wait()


def sat_parts(here, there, trans):
    p, lw, lo = here
    pn, lwn, lon = there
    t = trans * (p - pn)
    return t * (lw - lwn), t * (lo - lon)


def sat_kernel(press, sat, lamw, lamo, permx, permy, permz, pore, weight, from_chip, from_outside, out):
    ny = sat.shape[1]
    first = core() == 0
    layers = [tuple(r[x] for r in (press, lamw, lamo, permx)) for x in range(2)]
    ends = tuple(from_outside[m] for m in range(4)), tuple(from_chip[m] for m in (0, 2, 3, 4))
    below = tuple(jnp.where(first, a, b) for a, b in zip(*ends))
    above = tuple(jnp.where(first, b, a) for a, b in zip(*ends))
    chain = (below, *layers, above)
    across = []
    for here, there in zip(chain, chain[1:]):
        k, kn = here[3], there[3]
        across.append(sat_parts(here[:3], there[:3], k * kn / (k + kn)))
    for x in range(2):
        p, lw, lo, _ = layers[x]
        water, oil = (a + b for a, b in zip(across[x], across[x + 1]))
        for k, axis in ((permy[x], 0), (permz[x], 1)):
            there = tuple(upper(f, axis) for f in (p, lw, lo))
            a, b = sat_parts((p, lw, lo), there, 0.5 * transmissibility(k, axis))
            water = water + a + lower(a, axis)
            oil = oil + b + lower(b, axis)
        dw, do = slopes(sat[x])
        well = weight[x * ny : (x + 1) * ny] * p
        out[x] = pore[x] * (lw - lo) + dw * (water + well * lw) + do * (oil + well * lo)


def well_kernel(partial, sat, lamw, lamo, cell, well, index, well_rows, out, grad_bhp):
    ny = sat.shape[1]
    groups = well_rows.shape[0]
    wells_each = grad_bhp.shape[1]
    rows = well_rows[...]
    place = well[...] % wells_each
    owners = marks(well[...] // wells_each, groups)
    by_owner = add_thirds(
        dot(jnp.concatenate(split(rows)), marks(place, LANES).astype(jnp.bfloat16), ((1,), (0,)))
    )
    pressure = jnp.sum(by_owner * owners, axis=0, keepdims=True)
    cells = cell[...]
    drop = scatter_cells(index[...] * pressure, marks(cells // LANES, 2 * ny), marks(cells % LANES, LANES))
    for x in range(2):
        dw, do = slopes(sat[x])
        out[x] = partial[x] - (dw * lamw[x] + do * lamo[x]) * drop[x * ny : (x + 1) * ny]
    total = -jnp.sum(rows, axis=0, keepdims=True)
    grad_bhp[...] = total[:, wells_each : 2 * wells_each]


def swap(x):
    return pltpu.roll(x, 4, 0)


def sublane():
    return lax.broadcasted_iota(jnp.int32, (TILE, LANES), 0)


def face_kernel(received, _, own, send, well_rows):
    total = received.shape[0]
    groups = total // CHUNK
    low = sublane() < 4

    def body(parity):
        def tile(s, field):
            start = position(s, groups) * CHUNK + field - HALO * parity
            inside = min(max(start, 0), total - TILE)
            rows = received[inside : inside + TILE]
            return rows if inside == start else pltpu.roll(rows, (inside - start) % TILE, 0)

        count = 2 * groups
        below = None
        waiting = []
        for x in range(count):
            s = x // 2
            near = x % 4 in (1, 2)
            rhs, diag = tile(s, NEAR_RHS if near else FAR_RHS), tile(s, NEAR_DIAG if near else FAR_DIAG)
            if below is not None:
                rhs, diag = rhs - below[0], diag + below[1]
            below = None
            if x % 2 == 0:
                link = tile(s, INNER)
            elif x % 4 == 1:
                link = tile(s, CHIP)
            elif x < count - 1:
                here, there = (
                    (tile(t, LAMW), tile(t, LAMO), *mobilities(tile(t, SAT)), tile(t, PERMX)) for t in (s, s + 1)
                )
                k, kn = here[4], there[4]
                below = face(here[:4], there[:4], k * kn / (k + kn))
                rhs, diag, link = rhs + below[0], diag + below[1], below[1]
            else:
                link = jnp.zeros_like(rhs)
            fields = (rhs, diag, link, tile(s, CY + x % 2 * ROWS), tile(s, CZ + x % 2 * ROWS))
            for f, value in enumerate(fields):
                own[f, x * TILE : (x + 1) * TILE] = value
            waiting += fields
            while len(waiting) >= 2:
                a, b = waiting[:2]
                waiting = waiting[2:]
                at = ((5 * x + 5 - len(waiting)) // 2 - 1) * TILE
                send[at : at + TILE] = jnp.where(low, pltpu.roll(a, TILE - 2, 0), pltpu.roll(b, 2, 0))

    for parity in range(2):
        pl.when(core() == parity)(functools.partial(body, parity))
    for s in range(groups):
        at = position(s, groups) * CHUNK + WELL_ROW
        well_rows[s : s + 1] = received[at : at + 1]


def solver(diag, link, levels):
    count = len(diag)
    if levels:
        inverse = {j: 1.0 / diag[j] for j in range(1, count, 2)}
        left = {j: link[j - 1] * inverse[j] for j in inverse}
        right = {j: link[j] * inverse[j] for j in inverse if j < count - 1}
        kept_diag, kept_link = [], []
        for i in range(0, count, 2):
            d = diag[i] - link[i] * left[i + 1]
            kept_diag.append(d - link[i - 1] * right[i - 1] if i else d)
            if i < count - 2:
                kept_link.append(link[i] * right[i + 1])
        inner = solver(kept_diag, kept_link, levels - 1)

        def solve(b):
            reduced = []
            for i in range(0, count, 2):
                t = b[i] + left[i + 1] * b[i + 1]
                reduced.append(t + right[i - 1] * b[i - 1] if i else t)
            u = [None] * count
            u[::2] = inner(reduced)
            for j in inverse:
                t = inverse[j] * b[j] + left[j] * u[j - 1]
                u[j] = t + right[j] * u[j + 1] if j < count - 1 else t
            return u

        return solve

    half = count // 2
    weights, inverses = [None] * count, [None] * count
    da, db = diag[0], diag[count - 1]
    for j in range(half - 1):
        m = count - 1 - j
        inverses[j], inverses[m] = 1.0 / da, 1.0 / db
        weights[j], weights[m] = link[j] * inverses[j], link[m - 1] * inverses[m]
        da = diag[j + 1] - link[j] * weights[j]
        db = diag[m - 1] - link[m - 1] * weights[m]
    c = link[half - 1]
    inverse = 1.0 / (da * db - c * c)

    def solve(b):
        b = list(b)
        for j in range(1, half):
            b[j] = b[j] + weights[j - 1] * b[j - 1]
            m = count - 1 - j
            b[m] = b[m] + weights[m + 1] * b[m + 1]
        u = [None] * count
        u[half - 1] = (b[half - 1] * db + c * b[half]) * inverse
        u[half] = (b[half] * da + c * b[half - 1]) * inverse
        for j in range(half - 2, -1, -1):
            u[j] = inverses[j] * b[j] + weights[j] * u[j + 1]
            m = count - 1 - j
            u[m] = inverses[m] * b[m] + weights[m] * u[m - 1]
        return u

    return solve


def sweep_kernel(sweeps, own, other, out):
    count = own.shape[1] // TILE
    row = sublane()
    first = core() == 0
    kept = jnp.logical_and(row >= jnp.where(first, 0, HALO), row < jnp.where(first, ROWS, TILE))
    fields = [[], [], [], [], []]
    for i in range(5 * count // 2):
        packed = other[i * TILE : (i + 1) * TILE]
        turned = swap(packed)
        for n, value in ((2 * i, jnp.where(first, turned, packed)), (2 * i + 1, jnp.where(first, packed, turned))):
            x, f = n // 5, n % 5
            fields[f].append(jnp.where(kept, own[f, x * TILE : (x + 1) * TILE], value))
    rhs, diag, link, cy, cz = fields
    solve = solver(diag, link, REDUCTIONS)
    u = solve(rhs)
    for _ in range(1, sweeps):
        targets = []
        for x in range(count):
            t = rhs[x] + cy[x] * upper(u[x], 0) + lower(cy[x] * u[x], 0)
            targets.append(t + cz[x] * upper(u[x], 1) + lower(cz[x] * u[x], 1))
        u = solve(targets)
    for x in range(count):
        for y in range(2):
            out[y, x : x + 1] = u[x][HALO + y : HALO + y + 1]


def call(kernel, outs, *args, scratch=(), in_hbm=0, out_hbm=0, aliases=None):
    places = [pltpu.VMEM] * (len(args) - in_hbm) + [pltpu.HBM] * in_hbm
    args = [pltpu.with_memory_space_constraint(v, place) if place == pltpu.HBM else v for v, place in zip(args, places)]
    results = [pltpu.VMEM] * (len(outs) - out_hbm) + [pltpu.HBM] * out_hbm

    def shaped(shape, place):
        return pltpu.HBM(shape, jnp.float32) if place == pltpu.HBM else jax.ShapeDtypeStruct(shape, jnp.float32)

    return pl.pallas_call(
        kernel,
        out_shape=tuple(shaped(o, place) if isinstance(o, tuple) else o for o, place in zip(outs, results)),
        in_specs=[pl.BlockSpec(memory_space=place) for place in places],
        out_specs=tuple(pl.BlockSpec(memory_space=place) for place in results),
        scratch_shapes=[pltpu.VMEM(o, jnp.float32) if isinstance(o, tuple) else o for o in scratch],
        input_output_aliases=aliases or {},
        compiler_params=pltpu.CompilerParams(vmem_limit_bytes=40 << 20),
    )(*args)


def on_device(
    pressure, saturation, lam_water, lam_oil, perm_x, perm_y, perm_z, pore_volume,
    perf_cell, perf_well, well_index, well_pressure,
):
    groups = lax.axis_size("gx")
    ny = pressure.shape[1]
    wells_each = well_pressure.shape[0]
    fields = (pressure, saturation, lam_water, lam_oil, perm_x, perm_y, perm_z, pore_volume)
    cell, well, index, bhp = (v.reshape(1, -1) for v in (perf_cell, perf_well, well_index, well_pressure))
    given = fields + (cell, well, index, bhp)
    chip_pairs = [(i, i + 1 - 2 * (i % 2)) for i in range(groups)]
    outer_pairs = [(i, i - 1 + 2 * (i % 2)) for i in range(1, groups - 1)]
    box = (2, ny, LANES)

    *loaded, chip_edge = call(
        load_kernel,
        [jax.ShapeDtypeStruct(v.shape, v.dtype) for v in given] + [(5, ny, LANES)],
        *given,
        scratch=[pltpu.SemaphoreType.DMA((len(given) + 5,))],
        in_hbm=len(given),
    )
    press, sat, lamw, lamo, permx, permy, permz, pore, cell, well, index, bhp = loaded
    from_chip = lax.ppermute(chip_edge, "gx", chip_pairs)
    plane = (ny, LANES)
    chunk = (groups, CHUNK, LANES)
    near_rhs, near_diag, outer, weight, well_rows, packed = call(
        functools.partial(cell_kernel, groups),
        [plane, plane, (4, ny, LANES), (2 * ny, LANES), (groups, LANES), chunk],
        press, sat, lamw, lamo, permx, permy, permz, pore, cell, well, index, bhp,
        scratch=[(11, ny + 2 * TILE, LANES), (groups, CHUNK - REST, LANES), pltpu.SemaphoreType.DMA],
        out_hbm=1,
    )
    (packed,) = call(
        functools.partial(pack_kernel, groups), [chunk],
        sat, lamw, lamo, permx, from_chip, near_rhs, near_diag, well_rows, packed,
        scratch=[(3, ny + 2 * TILE, LANES), (groups, REST, LANES), pltpu.SemaphoreType.DMA],
        in_hbm=1,
        out_hbm=1,
        aliases={8: 0},
    )
    order = sorted(range(groups), key=lambda device: position(device, groups))
    received = lax.all_to_all(packed, "gx", split_axis=0, concat_axis=0, axis_index_groups=[order], tiled=True)
    from_outside = lax.ppermute(outer, "gx", outer_pairs)
    (partial,) = call(
        sat_kernel, [box],
        press, sat, lamw, lamo, permx, permy, permz, pore, weight, from_chip, from_outside,
    )

    count = 2 * groups
    own, send, well_rows = call(
        face_kernel,
        [(5, count * TILE, LANES), (5 * count // 2 * TILE, LANES), (groups, LANES)],
        received.reshape(groups * CHUNK, LANES),
        partial,
    )
    other = lax.ppermute(send, "gx", chip_pairs)
    grad_sat, grad_bhp = call(
        well_kernel, [box, (1, wells_each)], partial, sat, lamw, lamo, cell, well, index, well_rows
    )
    (columns,) = call(functools.partial(sweep_kernel, SWEEPS), [(2, count, LANES)], own, other)
    return grad_sat, grad_bhp.reshape(wells_each), jnp.transpose(columns, (0, 2, 1))


def solution(mesh):
    cells = P(("members", "gx"), None, None)
    line = P(("members", "gx"))
    return jax.shard_map(
        on_device,
        mesh=mesh,
        in_specs=(cells,) * 8 + (line,) * 4,
        out_specs=(cells, line, cells),
        check_vma=False,
    )
```

```python
import functools

import jax
import jax.numpy as jnp
from jax import lax
from jax.experimental import pallas as pl
from jax.experimental.pallas import tpu as pltpu
from jax.sharding import PartitionSpec as P

water_viscosity = 0.5
oil_viscosity = 2.0
compressibility = 0.2
SWEEPS = 4
REDUCTIONS = 2

LANES = 128
TILE = 8
HALO = 3
ROWS = 5
NEAR_RHS, NEAR_DIAG, CHIP, WELL_ROW = 0, 5, 10, 15
REST = 16
FAR_RHS, FAR_DIAG, CY, CZ, INNER, SAT, LAMW, LAMO, PERMX = (REST + ROWS * i for i in (0, 1, 2, 4, 6, 7, 8, 9, 10))
CHUNK = REST + 11 * ROWS + 1


def mobilities(s):
    return s * s * (1.0 / water_viscosity), (1.0 - s) * (1.0 - s) * (1.0 / oil_viscosity)


def slopes(s):
    return s * (2.0 / water_viscosity), (s - 1.0) * (2.0 / oil_viscosity)


def split(x):
    first = x.astype(jnp.bfloat16)
    rest = x - first.astype(jnp.float32)
    second = rest.astype(jnp.bfloat16)
    third = (rest - second.astype(jnp.float32)).astype(jnp.bfloat16)
    return first, second, third


def dot(a, b, over):
    return lax.dot_general(a, b, (over, ((), ())), preferred_element_type=jnp.float32)


def add_thirds(x):
    n = x.shape[0] // 3
    return x[:n] + x[n : 2 * n] + x[2 * n :]


def marks(index, count):
    return (lax.broadcasted_iota(jnp.int32, (count, index.shape[1]), 0) == index).astype(jnp.float32)


def scatter_cells(values, row_marks, lane_marks):
    left = jnp.concatenate([(row_marks * part.astype(jnp.float32)).astype(jnp.bfloat16) for part in split(values)])
    return add_thirds(dot(left, lane_marks.astype(jnp.bfloat16), ((1,), (1,))))


def core():
    return lax.axis_index("gx") % 2


def upper(x, axis):
    return pltpu.roll(x, x.shape[axis] - 1, axis)


def lower(x, axis):
    return pltpu.roll(x, 1, axis)


def transmissibility(k, axis):
    kn = upper(k, axis)
    at = lax.broadcasted_iota(jnp.int32, k.shape, axis)
    return jnp.where(at < k.shape[axis] - 1, 2.0 * k * kn / (k + kn), 0.0)


def face(here, there, trans):
    lw, lo, mw, mo = here
    lwn, lon, mwn, mon = there
    fw = mw + mwn
    fo = mo + mon
    return trans * (fw * (lw - lwn) + fo * (lo - lon)), trans * (fw + fo)


def load_kernel(*refs):
    sources, loaded, edge, sems = refs[:12], refs[12:24], refs[24], refs[25]
    pairs = [(sources[i].at[1 - core()], edge.at[i]) for i in range(5)] + list(zip(sources, loaded))
    copies = [pltpu.make_async_copy(src, dst, sems.at[i]) for i, (src, dst) in enumerate(pairs)]
    for copy in copies:
        copy.start()
    for copy in copies:
        copy.wait()


def pad(ref, value, outside):
    ny = value.shape[0]
    edge = jnp.full((TILE, LANES), outside, jnp.float32)
    ref[:TILE] = edge
    ref[TILE : TILE + ny] = value
    ref[TILE + ny :] = edge


def for_chunks(groups, store):
    def chip(c, _):
        for parity in range(2):
            store(2 * c + parity, TILE + 4 * c - HALO + ROWS * parity)
        return 0

    if groups <= 16:
        for c in range(groups // 2):
            chip(c, 0)
    else:
        lax.fori_loop(0, groups // 2, chip, 0)


def cell_kernel(
    groups, press, sat, lamw, lamo, permx, permy, permz, pore, cell, well, index, bhp,
    near_rhs, near_diag, outer, weight, well_rows, packed, padded, chunks, sem,
):
    ny = sat.shape[1]
    far = core()
    first = far == 0
    cells = cell[...]
    row_marks = marks(cells // LANES, 2 * ny)
    lane_marks = marks(cells % LANES, LANES)
    perf_weight = scatter_cells(index[...], row_marks, lane_marks)
    weight[...] = perf_weight
    flows, layers, rhs, diag, couplings = [], [], [], [], [[], []]
    for x in range(2):
        s, lw, lo = sat[x], lamw[x], lamo[x]
        mw, mo = mobilities(s)
        layers.append((lw, lo, mw, mo))
        flow = mw * lw + mo * lo
        flows.append(flow)
        w = perf_weight[x * ny : (x + 1) * ny]
        rhs.append(flow * w)
        diag.append(compressibility * pore[x] + (mw + mo) * w)
        for axis, k in enumerate((permy[x], permz[x])):
            there = tuple(upper(f, axis) for f in layers[x])
            g, c = face(layers[x], there, 0.5 * transmissibility(k, axis))
            rhs[x] += g - lower(g, axis)
            diag[x] += c + lower(c, axis)
            couplings[axis].append(c)
    k, kn = permx[0], permx[1]
    g, inner = face(layers[0], layers[1], k * kn / (k + kn))
    rhs = rhs[0] + g, rhs[1] - g
    diag = diag[0] + inner, diag[1] + inner
    near_rhs[...] = jnp.where(first, rhs[1], rhs[0])
    near_diag[...] = jnp.where(first, diag[1], diag[0])
    values = [jnp.where(first, rhs[0], rhs[1]), jnp.where(first, diag[0], diag[1]), *couplings[0], *couplings[1], inner]
    values += [sat[far], lamw[far], lamo[far], permx[far]]
    for f, value in enumerate(values):
        pad(padded.at[f], value, 1.0 if REST + f * ROWS in (FAR_DIAG, PERMX) else 0.0)

    def store(d, start):
        for f in range(len(values)):
            chunks[d, f * ROWS : (f + 1) * ROWS] = padded[f, pl.ds(start, ROWS)]
        chunks[d, len(values) * ROWS :] = jnp.zeros((1, LANES), jnp.float32)

    for_chunks(groups, store)
    copy = pltpu.make_async_copy(chunks, packed.at[:, REST:], sem)
    copy.start()

    for i, ref in enumerate((press, lamw, lamo, permx)):
        outer[i] = ref[far]
    flow_parts = jnp.concatenate(split(jnp.concatenate(flows)))
    row_parts = jnp.concatenate([row_marks.astype(jnp.bfloat16)] * 3)
    by_lane = dot(flow_parts, row_parts, ((0,), (0,)))
    inflow = index[...] * jnp.sum(by_lane * lane_marks, axis=0, keepdims=True)
    wells_each = bhp.shape[1]
    owners = marks(well[...] // wells_each, groups)
    places = marks(well[...] % wells_each + wells_each, LANES)
    well_rows[...] = scatter_cells(inflow, owners, places)
    well_rows[:, :wells_each] = jnp.broadcast_to(bhp[...], (groups, wells_each))
    copy.wait()


def pack_kernel(groups, sat, lamw, lamo, permx, from_chip, near_rhs, near_diag, well_rows, _, packed, padded, chunks, sem):
    near = 1 - core()
    k, kn = permx[near], from_chip[4]
    here = (lamw[near], lamo[near], *mobilities(sat[near]))
    there = (from_chip[2], from_chip[3], *mobilities(from_chip[1]))
    g, c = face(here, there, k * kn / (k + kn))
    for i, (value, outside) in enumerate(((near_rhs[...] + g, 0.0), (near_diag[...] + c, 1.0), (c, 0.0))):
        pad(padded.at[i], value, outside)

    def store(d, start):
        for i in range(3):
            chunks[d, i * ROWS : (i + 1) * ROWS] = padded[i, pl.ds(start, ROWS)]
        chunks[d, WELL_ROW : WELL_ROW + 1] = well_rows[pl.ds(d, 1)]

    for_chunks(groups, store)
    copy = pltpu.make_async_copy(chunks, packed.at[:, :REST], sem)
    copy.start()
    copy.wait()


def sat_parts(here, there, trans):
    p, lw, lo = here
    pn, lwn, lon = there
    t = trans * (p - pn)
    return t * (lw - lwn), t * (lo - lon)


def sat_kernel(press, sat, lamw, lamo, permx, permy, permz, pore, weight, from_chip, from_outside, out):
    ny = sat.shape[1]
    first = core() == 0
    layers = [tuple(r[x] for r in (press, lamw, lamo, permx)) for x in range(2)]
    ends = tuple(from_outside[m] for m in range(4)), tuple(from_chip[m] for m in (0, 2, 3, 4))
    below = tuple(jnp.where(first, a, b) for a, b in zip(*ends))
    above = tuple(jnp.where(first, b, a) for a, b in zip(*ends))
    chain = (below, *layers, above)
    across = []
    for here, there in zip(chain, chain[1:]):
        k, kn = here[3], there[3]
        across.append(sat_parts(here[:3], there[:3], k * kn / (k + kn)))
    for x in range(2):
        p, lw, lo, _ = layers[x]
        water, oil = (a + b for a, b in zip(across[x], across[x + 1]))
        for k, axis in ((permy[x], 0), (permz[x], 1)):
            there = tuple(upper(f, axis) for f in (p, lw, lo))
            a, b = sat_parts((p, lw, lo), there, 0.5 * transmissibility(k, axis))
            water = water + a + lower(a, axis)
            oil = oil + b + lower(b, axis)
        dw, do = slopes(sat[x])
        well = weight[x * ny : (x + 1) * ny] * p
        out[x] = pore[x] * (lw - lo) + dw * (water + well * lw) + do * (oil + well * lo)


def well_kernel(partial, sat, lamw, lamo, cell, well, index, well_rows, out, grad_bhp):
    ny = sat.shape[1]
    groups = well_rows.shape[0]
    wells_each = grad_bhp.shape[1]
    rows = well_rows[...]
    place = well[...] % wells_each
    owners = marks(well[...] // wells_each, groups)
    by_owner = add_thirds(
        dot(jnp.concatenate(split(rows)), marks(place, LANES).astype(jnp.bfloat16), ((1,), (0,)))
    )
    pressure = jnp.sum(by_owner * owners, axis=0, keepdims=True)
    cells = cell[...]
    drop = scatter_cells(index[...] * pressure, marks(cells // LANES, 2 * ny), marks(cells % LANES, LANES))
    for x in range(2):
        dw, do = slopes(sat[x])
        out[x] = partial[x] - (dw * lamw[x] + do * lamo[x]) * drop[x * ny : (x + 1) * ny]
    total = -jnp.sum(rows, axis=0, keepdims=True)
    grad_bhp[...] = total[:, wells_each : 2 * wells_each]


def turned(x, by):
    return pltpu.roll(x, by % TILE, 0) if by % TILE else x


def sublane():
    return lax.broadcasted_iota(jnp.int32, (TILE, LANES), 0)


def face_kernel(received, _, own, send, well_rows):
    total = received.shape[0]
    groups = total // CHUNK
    row = sublane()

    def body(parity):
        def tile(s, field):
            start = s * CHUNK + field - HALO * parity
            inside = min(max(start, 0), total - TILE)
            rows = received[inside : inside + TILE]
            return rows if inside == start else pltpu.roll(rows, (inside - start) % TILE, 0)

        count = 2 * groups
        below = None
        for x in range(count):
            s = x // 2
            near = x % 4 in (1, 2)
            rhs, diag = tile(s, NEAR_RHS if near else FAR_RHS), tile(s, NEAR_DIAG if near else FAR_DIAG)
            if below is not None:
                rhs, diag = rhs - below[0], diag + below[1]
            below = None
            if x % 2 == 0:
                link = tile(s, INNER)
            elif x % 4 == 1:
                link = tile(s, CHIP)
            elif x < count - 1:
                here, there = (
                    (tile(t, LAMW), tile(t, LAMO), *mobilities(tile(t, SAT)), tile(t, PERMX)) for t in (s, s + 1)
                )
                k, kn = here[4], there[4]
                below = face(here[:4], there[:4], k * kn / (k + kn))
                rhs, diag, link = rhs + below[0], diag + below[1], below[1]
            else:
                link = jnp.zeros_like(rhs)
            fields = (rhs, diag, link, tile(s, CY + x % 2 * ROWS), tile(s, CZ + x % 2 * ROWS))
            for f, value in enumerate(fields):
                own[f, x * TILE : (x + 1) * TILE] = value
            rhs, diag, link, cy, cz = fields
            start = HALO - 1 + parity
            send[2 * x * TILE : (2 * x + 1) * TILE] = jnp.where(
                row < 3, turned(rhs, -start), jnp.where(row < 6, turned(diag, 3 - start), turned(cz, 3))
            )
            send[(2 * x + 1) * TILE : (2 * x + 2) * TILE] = jnp.where(row < 3, turned(link, -start), turned(cy, 3 - start))

    for parity in range(2):
        pl.when(core() == parity)(functools.partial(body, parity))
    for s in range(groups):
        well_rows[s : s + 1] = received[s * CHUNK + WELL_ROW : s * CHUNK + WELL_ROW + 1]


def solver(diag, link, levels):
    count = len(diag)
    if levels:
        inverse = {j: 1.0 / diag[j] for j in range(1, count, 2)}
        left = {j: link[j - 1] * inverse[j] for j in inverse}
        right = {j: link[j] * inverse[j] for j in inverse if j < count - 1}
        kept_diag, kept_link = [], []
        for i in range(0, count, 2):
            d = diag[i] - link[i] * left[i + 1]
            kept_diag.append(d - link[i - 1] * right[i - 1] if i else d)
            if i < count - 2:
                kept_link.append(link[i] * right[i + 1])
        inner = solver(kept_diag, kept_link, levels - 1)

        def solve(b):
            reduced = []
            for i in range(0, count, 2):
                t = b[i] + left[i + 1] * b[i + 1]
                reduced.append(t + right[i - 1] * b[i - 1] if i else t)
            u = [None] * count
            u[::2] = inner(reduced)
            for j in inverse:
                t = inverse[j] * b[j] + left[j] * u[j - 1]
                u[j] = t + right[j] * u[j + 1] if j < count - 1 else t
            return u

        return solve

    half = count // 2
    weights, inverses = [None] * count, [None] * count
    da, db = diag[0], diag[count - 1]
    for j in range(half - 1):
        m = count - 1 - j
        inverses[j], inverses[m] = 1.0 / da, 1.0 / db
        weights[j], weights[m] = link[j] * inverses[j], link[m - 1] * inverses[m]
        da = diag[j + 1] - link[j] * weights[j]
        db = diag[m - 1] - link[m - 1] * weights[m]
    c = link[half - 1]
    inverse = 1.0 / (da * db - c * c)

    def solve(b):
        b = list(b)
        for j in range(1, half):
            b[j] = b[j] + weights[j - 1] * b[j - 1]
            m = count - 1 - j
            b[m] = b[m] + weights[m + 1] * b[m + 1]
        u = [None] * count
        u[half - 1] = (b[half - 1] * db + c * b[half]) * inverse
        u[half] = (b[half] * da + c * b[half - 1]) * inverse
        for j in range(half - 2, -1, -1):
            u[j] = inverses[j] * b[j] + weights[j] * u[j + 1]
            m = count - 1 - j
            u[m] = inverses[m] * b[m] + weights[m] * u[m - 1]
        return u

    return solve


def sweep_kernel(sweeps, own, other, out):
    count = own.shape[1] // TILE
    row = sublane()
    first = core() == 0
    kept = jnp.logical_and(row >= jnp.where(first, 0, HALO), row < jnp.where(first, ROWS, TILE))
    fields = [[], [], [], [], []]
    for x in range(count):
        one, two = (other[i * TILE : (i + 1) * TILE] for i in (2 * x, 2 * x + 1))
        for f, (packed, by, otherwise) in enumerate(((one, 5, 0), (one, 2, 5), (two, 5, 0), (two, 2, 5), (one, 7, 3))):
            value = jnp.where(first, turned(packed, by), turned(packed, otherwise))
            fields[f].append(jnp.where(kept, own[f, x * TILE : (x + 1) * TILE], value))
    rhs, diag, link, cy, cz = fields
    solve = solver(diag, link, REDUCTIONS)
    u = solve(rhs)
    for _ in range(1, sweeps):
        targets = []
        for x in range(count):
            t = rhs[x] + cy[x] * upper(u[x], 0) + lower(cy[x] * u[x], 0)
            targets.append(t + cz[x] * upper(u[x], 1) + lower(cz[x] * u[x], 1))
        u = solve(targets)
    for x in range(count):
        for y in range(2):
            out[y, x : x + 1] = u[x][HALO + y : HALO + y + 1]


def call(kernel, outs, *args, scratch=(), in_hbm=0, out_hbm=0, aliases=None):
    places = [pltpu.VMEM] * (len(args) - in_hbm) + [pltpu.HBM] * in_hbm
    args = [pltpu.with_memory_space_constraint(v, place) if place == pltpu.HBM else v for v, place in zip(args, places)]
    results = [pltpu.VMEM] * (len(outs) - out_hbm) + [pltpu.HBM] * out_hbm

    def shaped(shape, place):
        return pltpu.HBM(shape, jnp.float32) if place == pltpu.HBM else jax.ShapeDtypeStruct(shape, jnp.float32)

    return pl.pallas_call(
        kernel,
        out_shape=tuple(shaped(o, place) if isinstance(o, tuple) else o for o, place in zip(outs, results)),
        in_specs=[pl.BlockSpec(memory_space=place) for place in places],
        out_specs=tuple(pl.BlockSpec(memory_space=place) for place in results),
        scratch_shapes=[pltpu.VMEM(o, jnp.float32) if isinstance(o, tuple) else o for o in scratch],
        input_output_aliases=aliases or {},
        compiler_params=pltpu.CompilerParams(vmem_limit_bytes=40 << 20),
    )(*args)


def on_device(
    pressure, saturation, lam_water, lam_oil, perm_x, perm_y, perm_z, pore_volume,
    perf_cell, perf_well, well_index, well_pressure,
):
    groups = lax.axis_size("gx")
    ny = pressure.shape[1]
    wells_each = well_pressure.shape[0]
    fields = (pressure, saturation, lam_water, lam_oil, perm_x, perm_y, perm_z, pore_volume)
    cell, well, index, bhp = (v.reshape(1, -1) for v in (perf_cell, perf_well, well_index, well_pressure))
    given = fields + (cell, well, index, bhp)
    chip_pairs = [(i, i + 1 - 2 * (i % 2)) for i in range(groups)]
    outer_pairs = [(i, i - 1 + 2 * (i % 2)) for i in range(1, groups - 1)]
    box = (2, ny, LANES)

    *loaded, chip_edge = call(
        load_kernel,
        [jax.ShapeDtypeStruct(v.shape, v.dtype) for v in given] + [(5, ny, LANES)],
        *given,
        scratch=[pltpu.SemaphoreType.DMA((len(given) + 5,))],
        in_hbm=len(given),
    )
    press, sat, lamw, lamo, permx, permy, permz, pore, cell, well, index, bhp = loaded
    from_chip = lax.ppermute(chip_edge, "gx", chip_pairs)
    plane = (ny, LANES)
    chunk = (groups, CHUNK, LANES)
    near_rhs, near_diag, outer, weight, well_rows, packed = call(
        functools.partial(cell_kernel, groups),
        [plane, plane, (4, ny, LANES), (2 * ny, LANES), (groups, LANES), chunk],
        press, sat, lamw, lamo, permx, permy, permz, pore, cell, well, index, bhp,
        scratch=[(11, ny + 2 * TILE, LANES), (groups, CHUNK - REST, LANES), pltpu.SemaphoreType.DMA],
        out_hbm=1,
    )
    (packed,) = call(
        functools.partial(pack_kernel, groups), [chunk],
        sat, lamw, lamo, permx, from_chip, near_rhs, near_diag, well_rows, packed,
        scratch=[(3, ny + 2 * TILE, LANES), (groups, REST, LANES), pltpu.SemaphoreType.DMA],
        in_hbm=1,
        out_hbm=1,
        aliases={8: 0},
    )
    received = lax.all_to_all(packed, "gx", split_axis=0, concat_axis=0, tiled=True)
    from_outside = lax.ppermute(outer, "gx", outer_pairs)
    (partial,) = call(
        sat_kernel, [box],
        press, sat, lamw, lamo, permx, permy, permz, pore, weight, from_chip, from_outside,
    )

    count = 2 * groups
    own, send, well_rows = call(
        face_kernel,
        [(5, count * TILE, LANES), (2 * count * TILE, LANES), (groups, LANES)],
        received.reshape(groups * CHUNK, LANES),
        partial,
    )
    other = lax.ppermute(send, "gx", chip_pairs)
    grad_sat, grad_bhp = call(
        well_kernel, [box, (1, wells_each)], partial, sat, lamw, lamo, cell, well, index, well_rows
    )
    (columns,) = call(functools.partial(sweep_kernel, SWEEPS), [(2, count, LANES)], own, other)
    return grad_sat, grad_bhp.reshape(wells_each), jnp.transpose(columns, (0, 2, 1))


def solution(mesh):
    cells = P(("members", "gx"), None, None)
    line = P(("members", "gx"))
    return jax.shard_map(
        on_device,
        mesh=mesh,
        in_specs=(cells,) * 8 + (line,) * 4,
        out_specs=(cells, line, cells),
        check_vma=False,
    )
```

```python
import functools

import jax
import jax.numpy as jnp
from jax import lax
from jax.experimental import pallas as pl
from jax.experimental.pallas import tpu as pltpu
from jax.sharding import PartitionSpec as P

water_viscosity = 0.5
oil_viscosity = 2.0
compressibility = 0.2
SWEEPS = 4
REDUCTIONS = 3

LANES = 128
TILE = 8
HALO = 3
ROWS = 5
NEAR_RHS, NEAR_DIAG, CHIP, WELL_ROW = 0, 5, 10, 15
REST = 16
FAR_RHS, FAR_DIAG, CY, CZ, INNER, SAT, LAMW, LAMO, PERMX = (REST + ROWS * i for i in (0, 1, 2, 4, 6, 7, 8, 9, 10))
CHUNK = REST + 11 * ROWS + 1


def mobilities(s):
    return s * s * (1.0 / water_viscosity), (1.0 - s) * (1.0 - s) * (1.0 / oil_viscosity)


def slopes(s):
    return s * (2.0 / water_viscosity), (s - 1.0) * (2.0 / oil_viscosity)


def split(x):
    first = x.astype(jnp.bfloat16)
    rest = x - first.astype(jnp.float32)
    second = rest.astype(jnp.bfloat16)
    third = (rest - second.astype(jnp.float32)).astype(jnp.bfloat16)
    return first, second, third


def dot(a, b, over):
    return lax.dot_general(a, b, (over, ((), ())), preferred_element_type=jnp.float32)


def add_thirds(x):
    n = x.shape[0] // 3
    return x[:n] + x[n : 2 * n] + x[2 * n :]


def marks(index, count):
    return (lax.broadcasted_iota(jnp.int32, (count, index.shape[1]), 0) == index).astype(jnp.float32)


def scatter_cells(values, row_marks, lane_marks):
    left = jnp.concatenate([(row_marks * part.astype(jnp.float32)).astype(jnp.bfloat16) for part in split(values)])
    return add_thirds(dot(left, lane_marks.astype(jnp.bfloat16), ((1,), (1,))))


def core():
    return lax.axis_index("gx") % 2


def upper(x, axis):
    return pltpu.roll(x, x.shape[axis] - 1, axis)


def lower(x, axis):
    return pltpu.roll(x, 1, axis)


def transmissibility(k, axis):
    kn = upper(k, axis)
    at = lax.broadcasted_iota(jnp.int32, k.shape, axis)
    return jnp.where(at < k.shape[axis] - 1, 2.0 * k * kn / (k + kn), 0.0)


def face(here, there, trans):
    lw, lo, mw, mo = here
    lwn, lon, mwn, mon = there
    fw = mw + mwn
    fo = mo + mon
    return trans * (fw * (lw - lwn) + fo * (lo - lon)), trans * (fw + fo)


def load_kernel(*refs):
    sources, loaded, edge, sems = refs[:12], refs[12:24], refs[24], refs[25]
    pairs = [(sources[i].at[1 - core()], edge.at[i]) for i in range(5)] + list(zip(sources, loaded))
    copies = [pltpu.make_async_copy(src, dst, sems.at[i]) for i, (src, dst) in enumerate(pairs)]
    for copy in copies:
        copy.start()
    for copy in copies:
        copy.wait()


def pad(ref, value, outside):
    ny = value.shape[0]
    edge = jnp.full((TILE, LANES), outside, jnp.float32)
    ref[:TILE] = edge
    ref[TILE : TILE + ny] = value
    ref[TILE + ny :] = edge


def for_chunks(groups, store):
    def chip(c, _):
        for parity in range(2):
            store(2 * c + parity, TILE + 4 * c - HALO + ROWS * parity)
        return 0

    if groups <= 16:
        for c in range(groups // 2):
            chip(c, 0)
    else:
        lax.fori_loop(0, groups // 2, chip, 0)


def cell_kernel(
    groups, press, sat, lamw, lamo, permx, permy, permz, pore, cell, well, index, bhp,
    near_rhs, near_diag, outer, weight, well_rows, packed, padded, chunks, sem,
):
    ny = sat.shape[1]
    far = core()
    first = far == 0
    cells = cell[...]
    row_marks = marks(cells // LANES, 2 * ny)
    lane_marks = marks(cells % LANES, LANES)
    perf_weight = scatter_cells(index[...], row_marks, lane_marks)
    weight[...] = perf_weight
    flows, layers, rhs, diag, couplings = [], [], [], [], [[], []]
    for x in range(2):
        s, lw, lo = sat[x], lamw[x], lamo[x]
        mw, mo = mobilities(s)
        layers.append((lw, lo, mw, mo))
        flow = mw * lw + mo * lo
        flows.append(flow)
        w = perf_weight[x * ny : (x + 1) * ny]
        rhs.append(flow * w)
        diag.append(compressibility * pore[x] + (mw + mo) * w)
        for axis, k in enumerate((permy[x], permz[x])):
            there = tuple(upper(f, axis) for f in layers[x])
            g, c = face(layers[x], there, 0.5 * transmissibility(k, axis))
            rhs[x] += g - lower(g, axis)
            diag[x] += c + lower(c, axis)
            couplings[axis].append(c)
    k, kn = permx[0], permx[1]
    g, inner = face(layers[0], layers[1], k * kn / (k + kn))
    rhs = rhs[0] + g, rhs[1] - g
    diag = diag[0] + inner, diag[1] + inner
    near_rhs[...] = jnp.where(first, rhs[1], rhs[0])
    near_diag[...] = jnp.where(first, diag[1], diag[0])
    values = [jnp.where(first, rhs[0], rhs[1]), jnp.where(first, diag[0], diag[1]), *couplings[0], *couplings[1], inner]
    values += [sat[far], lamw[far], lamo[far], permx[far]]
    for f, value in enumerate(values):
        pad(padded.at[f], value, 1.0 if REST + f * ROWS in (FAR_DIAG, PERMX) else 0.0)

    def store(d, start):
        for f in range(len(values)):
            chunks[d, f * ROWS : (f + 1) * ROWS] = padded[f, pl.ds(start, ROWS)]
        chunks[d, len(values) * ROWS :] = jnp.zeros((1, LANES), jnp.float32)

    for_chunks(groups, store)
    copy = pltpu.make_async_copy(chunks, packed.at[:, REST:], sem)
    copy.start()

    for i, ref in enumerate((press, lamw, lamo, permx)):
        outer[i] = ref[far]
    flow_parts = jnp.concatenate(split(jnp.concatenate(flows)))
    row_parts = jnp.concatenate([row_marks.astype(jnp.bfloat16)] * 3)
    by_lane = dot(flow_parts, row_parts, ((0,), (0,)))
    inflow = index[...] * jnp.sum(by_lane * lane_marks, axis=0, keepdims=True)
    wells_each = bhp.shape[1]
    owners = marks(well[...] // wells_each, groups)
    places = marks(well[...] % wells_each + wells_each, LANES)
    well_rows[...] = scatter_cells(inflow, owners, places)
    well_rows[:, :wells_each] = jnp.broadcast_to(bhp[...], (groups, wells_each))
    copy.wait()


def pack_kernel(groups, sat, lamw, lamo, permx, from_chip, near_rhs, near_diag, well_rows, _, packed, padded, chunks, sem):
    near = 1 - core()
    k, kn = permx[near], from_chip[4]
    here = (lamw[near], lamo[near], *mobilities(sat[near]))
    there = (from_chip[2], from_chip[3], *mobilities(from_chip[1]))
    g, c = face(here, there, k * kn / (k + kn))
    for i, (value, outside) in enumerate(((near_rhs[...] + g, 0.0), (near_diag[...] + c, 1.0), (c, 0.0))):
        pad(padded.at[i], value, outside)

    def store(d, start):
        for i in range(3):
            chunks[d, i * ROWS : (i + 1) * ROWS] = padded[i, pl.ds(start, ROWS)]
        chunks[d, WELL_ROW : WELL_ROW + 1] = well_rows[pl.ds(d, 1)]

    for_chunks(groups, store)
    copy = pltpu.make_async_copy(chunks, packed.at[:, :REST], sem)
    copy.start()
    copy.wait()


def sat_parts(here, there, trans):
    p, lw, lo = here
    pn, lwn, lon = there
    t = trans * (p - pn)
    return t * (lw - lwn), t * (lo - lon)


def sat_kernel(press, sat, lamw, lamo, permx, permy, permz, pore, weight, from_chip, from_outside, out):
    ny = sat.shape[1]
    first = core() == 0
    layers = [tuple(r[x] for r in (press, lamw, lamo, permx)) for x in range(2)]
    ends = tuple(from_outside[m] for m in range(4)), tuple(from_chip[m] for m in (0, 2, 3, 4))
    below = tuple(jnp.where(first, a, b) for a, b in zip(*ends))
    above = tuple(jnp.where(first, b, a) for a, b in zip(*ends))
    chain = (below, *layers, above)
    across = []
    for here, there in zip(chain, chain[1:]):
        k, kn = here[3], there[3]
        across.append(sat_parts(here[:3], there[:3], k * kn / (k + kn)))
    for x in range(2):
        p, lw, lo, _ = layers[x]
        water, oil = (a + b for a, b in zip(across[x], across[x + 1]))
        for k, axis in ((permy[x], 0), (permz[x], 1)):
            there = tuple(upper(f, axis) for f in (p, lw, lo))
            a, b = sat_parts((p, lw, lo), there, 0.5 * transmissibility(k, axis))
            water = water + a + lower(a, axis)
            oil = oil + b + lower(b, axis)
        dw, do = slopes(sat[x])
        well = weight[x * ny : (x + 1) * ny] * p
        out[x] = pore[x] * (lw - lo) + dw * (water + well * lw) + do * (oil + well * lo)


def well_kernel(partial, sat, lamw, lamo, cell, well, index, well_rows, out, grad_bhp):
    ny = sat.shape[1]
    groups = well_rows.shape[0]
    wells_each = grad_bhp.shape[1]
    rows = well_rows[...]
    place = well[...] % wells_each
    owners = marks(well[...] // wells_each, groups)
    by_owner = add_thirds(
        dot(jnp.concatenate(split(rows)), marks(place, LANES).astype(jnp.bfloat16), ((1,), (0,)))
    )
    pressure = jnp.sum(by_owner * owners, axis=0, keepdims=True)
    cells = cell[...]
    drop = scatter_cells(index[...] * pressure, marks(cells // LANES, 2 * ny), marks(cells % LANES, LANES))
    for x in range(2):
        dw, do = slopes(sat[x])
        out[x] = partial[x] - (dw * lamw[x] + do * lamo[x]) * drop[x * ny : (x + 1) * ny]
    total = -jnp.sum(rows, axis=0, keepdims=True)
    grad_bhp[...] = total[:, wells_each : 2 * wells_each]


def turned(x, by):
    return pltpu.roll(x, by % TILE, 0) if by % TILE else x


def sublane():
    return lax.broadcasted_iota(jnp.int32, (TILE, LANES), 0)


def face_kernel(received, _, own, send, well_rows):
    total = received.shape[0]
    groups = total // CHUNK
    row = sublane()

    def body(parity):
        def tile(s, field):
            start = s * CHUNK + field - HALO * parity
            inside = min(max(start, 0), total - TILE)
            rows = received[inside : inside + TILE]
            return rows if inside == start else pltpu.roll(rows, (inside - start) % TILE, 0)

        count = 2 * groups
        below = None
        for x in range(count):
            s = x // 2
            near = x % 4 in (1, 2)
            rhs, diag = tile(s, NEAR_RHS if near else FAR_RHS), tile(s, NEAR_DIAG if near else FAR_DIAG)
            if below is not None:
                rhs, diag = rhs - below[0], diag + below[1]
            below = None
            if x % 2 == 0:
                link = tile(s, INNER)
            elif x % 4 == 1:
                link = tile(s, CHIP)
            elif x < count - 1:
                here, there = (
                    (tile(t, LAMW), tile(t, LAMO), *mobilities(tile(t, SAT)), tile(t, PERMX)) for t in (s, s + 1)
                )
                k, kn = here[4], there[4]
                below = face(here[:4], there[:4], k * kn / (k + kn))
                rhs, diag, link = rhs + below[0], diag + below[1], below[1]
            else:
                link = jnp.zeros_like(rhs)
            fields = (rhs, diag, link, tile(s, CY + x % 2 * ROWS), tile(s, CZ + x % 2 * ROWS))
            for f, value in enumerate(fields):
                own[f, x * TILE : (x + 1) * TILE] = value
            rhs, diag, link, cy, cz = fields
            start = HALO - 1 + parity
            send[2 * x * TILE : (2 * x + 1) * TILE] = jnp.where(
                row < 3, turned(rhs, -start), jnp.where(row < 6, turned(diag, 3 - start), turned(cz, 3))
            )
            send[(2 * x + 1) * TILE : (2 * x + 2) * TILE] = jnp.where(row < 3, turned(link, -start), turned(cy, 3 - start))

    for parity in range(2):
        pl.when(core() == parity)(functools.partial(body, parity))
    for s in range(groups):
        well_rows[s : s + 1] = received[s * CHUNK + WELL_ROW : s * CHUNK + WELL_ROW + 1]


def solver(diag, link, levels):
    count = len(diag)
    if levels:
        inverse = {j: 1.0 / diag[j] for j in range(1, count, 2)}
        left = {j: link[j - 1] * inverse[j] for j in inverse}
        right = {j: link[j] * inverse[j] for j in inverse if j < count - 1}
        kept_diag, kept_link = [], []
        for i in range(0, count, 2):
            d = diag[i] - link[i] * left[i + 1]
            kept_diag.append(d - link[i - 1] * right[i - 1] if i else d)
            if i < count - 2:
                kept_link.append(link[i] * right[i + 1])
        inner = solver(kept_diag, kept_link, levels - 1)

        def solve(b):
            reduced = []
            for i in range(0, count, 2):
                t = b[i] + left[i + 1] * b[i + 1]
                reduced.append(t + right[i - 1] * b[i - 1] if i else t)
            u = [None] * count
            u[::2] = inner(reduced)
            for j in inverse:
                t = inverse[j] * b[j] + left[j] * u[j - 1]
                u[j] = t + right[j] * u[j + 1] if j < count - 1 else t
            return u

        return solve

    half = count // 2
    weights, inverses = [None] * count, [None] * count
    da, db = diag[0], diag[count - 1]
    for j in range(half - 1):
        m = count - 1 - j
        inverses[j], inverses[m] = 1.0 / da, 1.0 / db
        weights[j], weights[m] = link[j] * inverses[j], link[m - 1] * inverses[m]
        da = diag[j + 1] - link[j] * weights[j]
        db = diag[m - 1] - link[m - 1] * weights[m]
    c = link[half - 1]
    inverse = 1.0 / (da * db - c * c)

    def solve(b):
        b = list(b)
        for j in range(1, half):
            b[j] = b[j] + weights[j - 1] * b[j - 1]
            m = count - 1 - j
            b[m] = b[m] + weights[m + 1] * b[m + 1]
        u = [None] * count
        u[half - 1] = (b[half - 1] * db + c * b[half]) * inverse
        u[half] = (b[half] * da + c * b[half - 1]) * inverse
        for j in range(half - 2, -1, -1):
            u[j] = inverses[j] * b[j] + weights[j] * u[j + 1]
            m = count - 1 - j
            u[m] = inverses[m] * b[m] + weights[m] * u[m - 1]
        return u

    return solve


def sweep_kernel(sweeps, own, other, out):
    count = own.shape[1] // TILE
    row = sublane()
    first = core() == 0
    kept = jnp.logical_and(row >= jnp.where(first, 0, HALO), row < jnp.where(first, ROWS, TILE))
    fields = [[], [], [], [], []]
    for x in range(count):
        one, two = (other[i * TILE : (i + 1) * TILE] for i in (2 * x, 2 * x + 1))
        for f, (packed, by, otherwise) in enumerate(((one, 5, 0), (one, 2, 5), (two, 5, 0), (two, 2, 5), (one, 7, 3))):
            value = jnp.where(first, turned(packed, by), turned(packed, otherwise))
            fields[f].append(jnp.where(kept, own[f, x * TILE : (x + 1) * TILE], value))
    rhs, diag, link, cy, cz = fields
    solve = solver(diag, link, REDUCTIONS)
    u = solve(rhs)
    for _ in range(1, sweeps):
        targets = []
        for x in range(count):
            t = rhs[x] + cy[x] * upper(u[x], 0) + lower(cy[x] * u[x], 0)
            targets.append(t + cz[x] * upper(u[x], 1) + lower(cz[x] * u[x], 1))
        u = solve(targets)
    for x in range(count):
        for y in range(2):
            out[y, x : x + 1] = u[x][HALO + y : HALO + y + 1]


def call(kernel, outs, *args, scratch=(), in_hbm=0, out_hbm=0, aliases=None):
    places = [pltpu.VMEM] * (len(args) - in_hbm) + [pltpu.HBM] * in_hbm
    args = [pltpu.with_memory_space_constraint(v, place) if place == pltpu.HBM else v for v, place in zip(args, places)]
    results = [pltpu.VMEM] * (len(outs) - out_hbm) + [pltpu.HBM] * out_hbm

    def shaped(shape, place):
        return pltpu.HBM(shape, jnp.float32) if place == pltpu.HBM else jax.ShapeDtypeStruct(shape, jnp.float32)

    return pl.pallas_call(
        kernel,
        out_shape=tuple(shaped(o, place) if isinstance(o, tuple) else o for o, place in zip(outs, results)),
        in_specs=[pl.BlockSpec(memory_space=place) for place in places],
        out_specs=tuple(pl.BlockSpec(memory_space=place) for place in results),
        scratch_shapes=[pltpu.VMEM(o, jnp.float32) if isinstance(o, tuple) else o for o in scratch],
        input_output_aliases=aliases or {},
        compiler_params=pltpu.CompilerParams(vmem_limit_bytes=40 << 20),
    )(*args)


def on_device(
    pressure, saturation, lam_water, lam_oil, perm_x, perm_y, perm_z, pore_volume,
    perf_cell, perf_well, well_index, well_pressure,
):
    groups = lax.axis_size("gx")
    ny = pressure.shape[1]
    wells_each = well_pressure.shape[0]
    fields = (pressure, saturation, lam_water, lam_oil, perm_x, perm_y, perm_z, pore_volume)
    cell, well, index, bhp = (v.reshape(1, -1) for v in (perf_cell, perf_well, well_index, well_pressure))
    given = fields + (cell, well, index, bhp)
    chip_pairs = [(i, i + 1 - 2 * (i % 2)) for i in range(groups)]
    outer_pairs = [(i, i - 1 + 2 * (i % 2)) for i in range(1, groups - 1)]
    box = (2, ny, LANES)

    *loaded, chip_edge = call(
        load_kernel,
        [jax.ShapeDtypeStruct(v.shape, v.dtype) for v in given] + [(5, ny, LANES)],
        *given,
        scratch=[pltpu.SemaphoreType.DMA((len(given) + 5,))],
        in_hbm=len(given),
    )
    press, sat, lamw, lamo, permx, permy, permz, pore, cell, well, index, bhp = loaded
    from_chip = lax.ppermute(chip_edge, "gx", chip_pairs)
    plane = (ny, LANES)
    chunk = (groups, CHUNK, LANES)
    near_rhs, near_diag, outer, weight, well_rows, packed = call(
        functools.partial(cell_kernel, groups),
        [plane, plane, (4, ny, LANES), (2 * ny, LANES), (groups, LANES), chunk],
        press, sat, lamw, lamo, permx, permy, permz, pore, cell, well, index, bhp,
        scratch=[(11, ny + 2 * TILE, LANES), (groups, CHUNK - REST, LANES), pltpu.SemaphoreType.DMA],
        out_hbm=1,
    )
    (packed,) = call(
        functools.partial(pack_kernel, groups), [chunk],
        sat, lamw, lamo, permx, from_chip, near_rhs, near_diag, well_rows, packed,
        scratch=[(3, ny + 2 * TILE, LANES), (groups, REST, LANES), pltpu.SemaphoreType.DMA],
        in_hbm=1,
        out_hbm=1,
        aliases={8: 0},
    )
    received = lax.all_to_all(packed, "gx", split_axis=0, concat_axis=0, tiled=True)
    from_outside = lax.ppermute(outer, "gx", outer_pairs)
    (partial,) = call(
        sat_kernel, [box],
        press, sat, lamw, lamo, permx, permy, permz, pore, weight, from_chip, from_outside,
    )

    count = 2 * groups
    own, send, well_rows = call(
        face_kernel,
        [(5, count * TILE, LANES), (2 * count * TILE, LANES), (groups, LANES)],
        received.reshape(groups * CHUNK, LANES),
        partial,
    )
    other = lax.ppermute(send, "gx", chip_pairs)
    grad_sat, grad_bhp = call(
        well_kernel, [box, (1, wells_each)], partial, sat, lamw, lamo, cell, well, index, well_rows
    )
    (columns,) = call(functools.partial(sweep_kernel, SWEEPS), [(2, count, LANES)], own, other)
    return grad_sat, grad_bhp.reshape(wells_each), jnp.transpose(columns, (0, 2, 1))


def solution(mesh):
    cells = P(("members", "gx"), None, None)
    line = P(("members", "gx"))
    return jax.shard_map(
        on_device,
        mesh=mesh,
        in_specs=(cells,) * 8 + (line,) * 4,
        out_specs=(cells, line, cells),
        check_vma=False,
    )
```
